32 devices in a mesh: tm: 4 (over y, x), sx: 2 (over core), sy: 4 (over z).
Axes of the slice: x: 2, y: 2, z: 4, core: 2. Of those that a mesh axis runs over, the one named last changes fastest.
Arguments:
- driving_input: float32 [128, 8, 16, 512], P('tm', None, 'sx', 'sy'), may hold values from -4 to 4
- regime: int32 [8, 16, 512], P(None, 'sx', 'sy'), may hold values from 0 to 7
- reaction_rates: float32 [8], replicated, may hold values from 0.005 to 1
Outputs:
- solution: float32 [128, 8, 16, 512], P('tm', None, 'sx', 'sy')
The draws below stay inside these ranges and needn't reach their ends.
All inputs are finite; a program needn't handle non-finite values.
Results may differ from the reference program's by a relative error of at most 0.00007.
Values sent between devices are 32-bit elements; how exact they have to be, the bound alone decides.
A program may use at most 64 MiB of HBM per device.

```python
import jax
import jax.numpy as jnp
from jax import lax

L = 128
NZ = 8
AGGREGATE_XCELLS = 8
AGGREGATE_YCELLS = 32
RATES = 8
SWEEPS = 4
NX = 16
NY = 512
NCX = 2
NCY = 16
NC = 32


def draw_driving_input(key, part):
    full_shape = (L, NZ, NX, NY)
    return jax.random.truncated_normal(key, -4.0, 4.0, full_shape, jnp.float32)


def draw_reaction_rates(key, part):
    lower_end = 0.005
    upper_end = 1.0
    exponent = jax.random.uniform(key, (RATES,), jnp.float32, jnp.log(lower_end), jnp.log(upper_end))
    return jnp.clip(jnp.exp(exponent), 0.005, 1.0)


def plant(values, rng, smallest, high):
    shape = values.shape
    place = [jax.random.randint(jax.random.fold_in(rng, axis), (), 0, shape[axis]) for axis in range(len(shape))]
    values = values.at[tuple(place)].set(smallest)
    longest = shape.index(max(shape))
    place[longest] = (place[longest] + 1) % shape[longest]
    return values.at[tuple(place)].set(high)


def setup_inputs(seed: int = 0) -> dict:
    key_list = jax.random.split(jax.random.key(seed), 4)
    return {
        "driving_input": draw_driving_input(jax.random.fold_in(key_list[3], 71), 0),
        "regime": plant(jax.random.randint(key_list[1], (NZ, NX, NY), 0, RATES), jax.random.fold_in(key_list[1], 1), 0, RATES - 1).astype(jnp.int32),
        "reaction_rates": draw_reaction_rates(jax.random.fold_in(key_list[3], 71), 0),
    }


TWO_PI = 2.0 * 3.141592653589793

def angle_table(row_index, col_index, cycle_duration):
    product = row_index[:, None] * col_index[None, :] % cycle_duration
    angles = product.astype(jnp.float32) * (TWO_PI / cycle_duration)
    return (jnp.cos(angles), jnp.sin(angles))

def matmul(left_side, right_side):
    return jnp.dot(left_side.astype(jnp.float32), right_side.astype(jnp.float32), precision=lax.Precision.HIGHEST, preferred_element_type=jnp.float32)

def complex_mul(left_real, left_imag, pair):
    return jnp.stack([left_real * pair[0] - left_imag * pair[1], left_real * pair[1] + left_imag * pair[0]])

def neighbors(present_guess):
    padded = jnp.pad(present_guess, ((0, 0), (0, 0), (1, 1), (1, 1)))
    running = padded[:, :, 2:, 1:-1] + padded[:, :, :-2, 1:-1]
    running = running + padded[:, :, 1:-1, 2:] + padded[:, :, 1:-1, :-2]
    running = running + jnp.roll(present_guess, 1, axis=1) + jnp.roll(present_guess, -1, axis=1)
    return running

def aggregate(values):
    leading = values.shape[:-3]
    blocks = values.reshape(leading + (NZ, NCX, AGGREGATE_XCELLS, NCY, AGGREGATE_YCELLS))
    return jnp.sum(blocks, axis=(-5, -3, -1)).reshape(leading + (NCX * NCY,))

def reference(driving_input, regime, reaction_rates):
    unrolled_array = driving_input.reshape(L, -1)
    all_index = jnp.arange(L, dtype=jnp.int32)
    cosine, sine = angle_table(all_index, all_index, L)
    spec_real = matmul(cosine, unrolled_array).reshape(driving_input.shape)
    spec_imag = (-matmul(sine, unrolled_array)).reshape(driving_input.shape)
    reaction = jnp.zeros(regime.shape, jnp.float32)
    for regime_no in range(RATES):
        reaction = reaction + jnp.where(regime == regime_no, reaction_rates[regime_no], jnp.zeros((), jnp.float32))
    rate_sums = aggregate(reaction)
    position = jnp.arange(NC, dtype=jnp.int32)
    coarse_x = position // NCY
    coarse_y = position % NCY
    x_gap = jnp.abs(coarse_x[:, None] - coarse_x[None, :])
    y_gap = jnp.abs(coarse_y[:, None] - coarse_y[None, :])
    coupling = -(AGGREGATE_YCELLS * NZ) * ((x_gap == 1) & (y_gap == 0)).astype(jnp.float32)
    coupling = coupling - AGGREGATE_XCELLS * NZ * ((x_gap == 0) & (y_gap == 1)).astype(jnp.float32)
    identity = (position[:, None] == position[None, :]).astype(jnp.float32)
    face_count = 2 * (AGGREGATE_YCELLS * NZ + AGGREGATE_XCELLS * NZ)
    volume = AGGREGATE_XCELLS * AGGREGATE_YCELLS * NZ
    diagonal = rate_sums + face_count

    def solve(entry_set):
        frequency, source_real, source_imag = entry_set
        phase_angle = frequency.astype(jnp.float32) * (TWO_PI / L)
        shift_real = 1.0 - jnp.cos(phase_angle)
        shift_imag = jnp.sin(phase_angle)
        diag_real = reaction + 6.0 + shift_real
        diag_imag = jnp.zeros_like(diag_real) + shift_imag
        modulus = diag_real * diag_real + diag_imag * diag_imag
        inverse_real = diag_real / modulus
        inverse_imag = -diag_imag / modulus
        source_term = jnp.stack([source_real, source_imag])
        present_guess = complex_mul(inverse_real, inverse_imag, source_term)
        for sweep_no in range(SWEEPS - 1):
            present_guess = complex_mul(inverse_real, inverse_imag, source_term + neighbors(present_guess))
        applied = complex_mul(diag_real, diag_imag, present_guess) - neighbors(present_guess)
        residual = source_term - applied
        coarse_right = jnp.transpose(aggregate(residual), (1, 0))
        system = coupling + identity * (diagonal + volume * shift_real)[None, :]
        factor = jnp.linalg.cholesky(system)
        forward_sub = lax.linalg.triangular_solve(factor, coarse_right, left_side=True, lower=True)
        coarse = lax.linalg.triangular_solve(factor, forward_sub, left_side=True, lower=True, transpose_a=True)
        local_part = jnp.transpose(coarse, (1, 0)).reshape(2, 1, NCX, 1, NCY, 1)
        spread_values = jnp.broadcast_to(local_part, (2, NZ, NCX, AGGREGATE_XCELLS, NCY, AGGREGATE_YCELLS)).reshape(2, NZ, NCX * AGGREGATE_XCELLS, NCY * AGGREGATE_YCELLS)
        return present_guess + spread_values
    corrected = lax.map(solve, (all_index, spec_real, spec_imag))
    real_part = corrected[:, 0].reshape(L, -1)
    imag_part = corrected[:, 1].reshape(L, -1)
    result = (matmul(cosine, real_part) - matmul(sine, imag_part)) / L
    return result.reshape(driving_input.shape)
```

```python
import functools

import jax
import jax.numpy as jnp
import numpy as np
from jax import lax
from jax.experimental import pallas as pl
from jax.experimental.pallas import tpu as pltpu
from jax.sharding import PartitionSpec as P

AGGREGATE_XCELLS = 8
AGGREGATE_YCELLS = 32
SWEEPS = 4


TWO_PI = 2.0 * 3.141592653589793


def extended(block, sides, width):
    for axis, dim in sides:
        count = lax.axis_size(axis)
        forward = [(i, i + 1) for i in range(count - 1)]
        backward = [(target, source) for source, target in forward]
        low = lax.ppermute(
            lax.slice_in_dim(block, block.shape[dim] - width, None, axis=dim), axis, forward
        )
        high = lax.ppermute(lax.slice_in_dim(block, 0, width, axis=dim), axis, backward)
        block = jnp.concatenate([low, block, high], axis=dim)
    return block


def angle_table(row_index, col_index, cycle_duration):
    product = row_index[:, None] * col_index[None, :] % cycle_duration
    angles = product.astype(jnp.float32) * (TWO_PI / cycle_duration)
    return (jnp.cos(angles), jnp.sin(angles))


def matmul(left_side, right_side):
    return jnp.dot(
        left_side, right_side, precision=lax.Precision.HIGHEST, preferred_element_type=jnp.float32
    )


def complex_mul(left_real, left_imag, pair):
    return jnp.stack(
        [left_real * pair[0] - left_imag * pair[1], left_real * pair[1] + left_imag * pair[0]]
    )


def neighbors(present_guess):
    padded = extended(present_guess, (("sx", 3), ("sy", 4)), 1)
    running = padded[:, :, :, 2:, 1:-1] + padded[:, :, :, :-2, 1:-1]
    running = running + padded[:, :, :, 1:-1, 2:] + padded[:, :, :, 1:-1, :-2]
    running = running + jnp.roll(present_guess, 1, axis=2) + jnp.roll(present_guess, -1, axis=2)
    return running


def local_general(driving_input, regime, reaction_rates):
    moment_count, third_axis_count, first_axis_count, second_axis_count = driving_input.shape
    temporal_spacing = lax.axis_size("tm")
    sy_size = lax.axis_size("sy")
    cycle_duration = moment_count * temporal_spacing
    unknowns_in_tile = third_axis_count * first_axis_count * second_axis_count
    processor_lines = driving_input.reshape(moment_count, unknowns_in_tile)
    owned_slice_number = lax.axis_index("tm") * moment_count + jnp.arange(
        moment_count, dtype=jnp.int32
    )
    all_index = jnp.arange(cycle_duration, dtype=jnp.int32)
    cos_rows, sin_rows = angle_table(owned_slice_number, all_index, cycle_duration)

    def forward(running, segment, offset):
        return jnp.stack([matmul(cos_rows, segment), -matmul(sin_rows, segment)])

    eigen_spectra = forward(
        jnp.zeros((2, moment_count, unknowns_in_tile), jnp.float32),
        lax.all_gather(processor_lines, "tm", axis=0, tiled=True),
        jnp.int32(0),
    )
    source_term = eigen_spectra.reshape(
        2, moment_count, third_axis_count, first_axis_count, second_axis_count
    )
    phase_angle = owned_slice_number.astype(jnp.float32) * (TWO_PI / cycle_duration)
    shift_real = (1.0 - jnp.cos(phase_angle))[:, None, None, None]
    shift_imag = jnp.sin(phase_angle)[:, None, None, None]
    reaction = jnp.zeros(regime.shape, jnp.float32)
    for regime_no in range(reaction_rates.shape[0]):
        reaction = reaction + jnp.where(
            regime == regime_no, reaction_rates[regime_no], jnp.zeros((), jnp.float32)
        )
    diag_real = reaction[None] + 6.0 + shift_real
    diag_imag = jnp.zeros_like(diag_real) + shift_imag
    modulus = diag_real * diag_real + diag_imag * diag_imag
    inverse_real = diag_real / modulus
    inverse_imag = -diag_imag / modulus
    present_guess = complex_mul(inverse_real, inverse_imag, source_term)
    for sweep_no in range(SWEEPS - 1):
        present_guess = complex_mul(
            inverse_real, inverse_imag, source_term + neighbors(present_guess)
        )
    applied = complex_mul(diag_real, diag_imag, present_guess) - neighbors(present_guess)
    residual = source_term - applied
    first_axis_teams = first_axis_count // AGGREGATE_XCELLS
    second_axis_teams = second_axis_count // AGGREGATE_YCELLS
    per_device = first_axis_teams * second_axis_teams

    def aggregate(values):
        leading = values.shape[:-3]
        blocks = values.reshape(
            leading
            + (
                third_axis_count,
                first_axis_teams,
                AGGREGATE_XCELLS,
                second_axis_teams,
                AGGREGATE_YCELLS,
            )
        )
        return jnp.sum(blocks, axis=(-5, -3, -1)).reshape(leading + (per_device,))

    coarse_right = jnp.transpose(aggregate(residual), (1, 0, 2))
    rate_sums = aggregate(reaction)
    shift_column = 1.0 - jnp.cos(phase_angle)
    face_count = 2 * (AGGREGATE_YCELLS * third_axis_count + AGGREGATE_XCELLS * third_axis_count)
    volume = AGGREGATE_XCELLS * AGGREGATE_YCELLS * third_axis_count
    spatial = lax.axis_size("sx") * sy_size
    slot_count = -(-moment_count // spatial)
    padding_rows = slot_count * spatial - moment_count
    padded_right = jnp.pad(coarse_right, ((0, padding_rows), (0, 0), (0, 0)))
    sum_copies = jnp.broadcast_to(rate_sums[None, None, :], (spatial, 1, per_device))
    shared_right, shared_sums = (
        lax.all_to_all(padded_right, ("sx", "sy"), split_axis=0, concat_axis=2, tiled=True),
        lax.all_to_all(sum_copies, ("sx", "sy"), split_axis=0, concat_axis=2, tiled=True),
    )
    spatial_rank = lax.axis_index("sx") * sy_size + lax.axis_index("sy")
    padded_shift = jnp.pad(shift_column, (0, padding_rows))
    slot_shift = lax.dynamic_slice_in_dim(padded_shift, spatial_rank * slot_count, slot_count, 0)
    sum_values = shared_sums[0, 0]
    coarse_total = sum_values.shape[0]
    position = jnp.arange(coarse_total, dtype=jnp.int32)
    device = position // per_device
    within = position % per_device
    coarse_x = device // sy_size * first_axis_teams + within // second_axis_teams
    coarse_y = device % sy_size * second_axis_teams + within % second_axis_teams
    x_gap = jnp.abs(coarse_x[:, None] - coarse_x[None, :])
    y_gap = jnp.abs(coarse_y[:, None] - coarse_y[None, :])
    coupling = -(AGGREGATE_YCELLS * third_axis_count) * ((x_gap == 1) & (y_gap == 0)).astype(
        jnp.float32
    )
    coupling = coupling - AGGREGATE_XCELLS * third_axis_count * (
        (x_gap == 0) & (y_gap == 1)
    ).astype(jnp.float32)
    identity = (position[:, None] == position[None, :]).astype(jnp.float32)
    diagonal = sum_values + face_count
    system = (
        coupling[None]
        + identity[None] * (diagonal[None, :] + volume * slot_shift[:, None])[:, None, :]
    )
    factor = jnp.linalg.cholesky(system)
    right_side = jnp.transpose(shared_right, (0, 2, 1))
    forward_sub = lax.linalg.triangular_solve(factor, right_side, left_side=True, lower=True)
    coarse = lax.linalg.triangular_solve(
        factor, forward_sub, left_side=True, lower=True, transpose_a=True
    )
    solved = jnp.transpose(coarse, (0, 2, 1))
    returned = lax.all_to_all(solved, ("sx", "sy"), split_axis=2, concat_axis=0, tiled=True)
    own_coarse = returned[:moment_count]
    local_part = jnp.transpose(own_coarse, (1, 0, 2)).reshape(
        2, moment_count, 1, first_axis_teams, 1, second_axis_teams, 1
    )
    spread_values = jnp.broadcast_to(
        local_part,
        (
            2,
            moment_count,
            third_axis_count,
            first_axis_teams,
            AGGREGATE_XCELLS,
            second_axis_teams,
            AGGREGATE_YCELLS,
        ),
    )
    present_guess = present_guess + spread_values.reshape(
        2, moment_count, third_axis_count, first_axis_count, second_axis_count
    )
    unrolled_array = present_guess.reshape(2, moment_count, unknowns_in_tile)

    def backward(running, segment, offset):
        return matmul(cos_rows, segment[0]) - matmul(sin_rows, segment[1])

    result = (
        backward(
            jnp.zeros((moment_count, unknowns_in_tile), jnp.float32),
            lax.all_gather(unrolled_array, "tm", axis=1, tiled=True),
            jnp.int32(0),
        )
        / cycle_duration
    )
    return result.reshape(driving_input.shape)


def time_tables(count):
    half = count // 2
    lane = np.arange(count)
    frequency = np.where(lane <= half, lane, lane - half)
    imaginary = lane > half
    moment = np.arange(count)
    angle = 2.0 * np.pi * (moment[:, None] * frequency[None, :] % count) / count
    forward = np.where(imaginary[None, :], -np.sin(angle), np.cos(angle))
    weight = np.where((lane == 0) | (lane == half), 1.0, 2.0) / count
    theta = 2.0 * np.pi * frequency / count
    signed = np.where(lane % half == 0, 0.0, np.sin(theta)) * np.where(lane < half, 1.0, -1.0)
    shift = np.zeros((8, count))
    shift[0] = 1.0 - np.cos(theta)
    shift[1] = signed
    return (
        forward.astype(np.float32),
        (forward * weight[None, :]).astype(np.float32),
        shift.astype(np.float32),
    )


def fused_kernel(
    sizes,
    rates_ref,
    field_ref,
    regime_ref,
    forward_ref,
    backward_ref,
    shift_ref,
    out_ref,
    send_buf,
    recv_buf,
    send_back,
    recv_back,
    cell_rates,
    rate_tiles,
    coarse_tiles,
    weights,
    source,
    inv_real,
    inv_cross,
    iterate_0,
    iterate_1,
    iterate_2,
    final,
    there_send,
    there_recv,
    back_send,
    back_recv,
    rate_send,
    rate_recv,
    coarse_send,
    coarse_recv,
    halo_send,
    halo_recv,
):
    teams, nsx, nsy, moments, nz, nx, lanes, width = sizes
    total = teams * moments
    half = total // 2
    groups = nz // teams
    chunk = moments * groups * nx
    row_cells = width * nz
    spatial = nsx * nsy
    devices = teams * spatial
    highest = lax.Precision.HIGHEST
    tm = lax.axis_index("tm")
    ix = lax.axis_index("sx")
    iy = lax.axis_index("sy")
    here = ix * nsy + iy
    me = tm * spatial + here

    def place(rank):
        return {
            "tm": rank // spatial,
            "sx": (rank % spatial) // nsy,
            "sy": rank % nsy,
        }

    barrier = pltpu.get_barrier_semaphore()

    def greet(offset, carry):
        pl.semaphore_signal(
            barrier,
            inc=1,
            device_id=place((me + offset) % devices),
            device_id_type=pl.DeviceIdType.MESH,
        )
        return carry

    lax.fori_loop(1, devices, greet, 0)

    rates = jnp.zeros(regime_ref.shape, jnp.float32)
    regime = regime_ref[...]
    for number in range(rates_ref.shape[0]):
        rates = rates + jnp.where(regime == number, rates_ref[number], 0.0)
    cell_rates[...] = rates.reshape(nz * nx, lanes)
    rate_tiles[here] = jnp.sum(rates, axis=0)

    lane_block = lax.broadcasted_iota(jnp.int32, (1, nx, lanes), 2) // width

    def swap(parts):
        result = []
        for target in range(teams):
            merged = parts[target]
            for other in range(teams):
                if other != target:
                    turn = (width * (other - target)) % lanes
                    merged = jnp.where(
                        lane_block == other, pltpu.roll(parts[other], turn, 2), merged
                    )
            result.append(merged)
        return result

    step = 2

    def pack(index, carry):
        first = index * step
        for group in range(groups):
            parts = swap(
                [field_ref[pl.ds(first, step), group * teams + j] for j in range(teams)]
            )
            for target in range(teams):
                for inner in range(step):
                    row = target * chunk + ((first + inner) * groups + group) * nx
                    send_buf[pl.ds(pl.multiple_of(row, nx), nx), :] = parts[target][inner]
        return carry

    lax.fori_loop(0, moments // step, pack, 0)
    pl.semaphore_wait(barrier, devices - 1)

    def chunk_of(ref, index):
        return ref.at[pl.ds(pl.multiple_of(index * chunk, chunk), chunk), :]

    def there(offset):
        peer = (tm + offset) % teams
        return pltpu.make_async_remote_copy(
            src_ref=chunk_of(send_buf, peer),
            dst_ref=chunk_of(recv_buf, tm),
            send_sem=there_send.at[offset],
            recv_sem=there_recv.at[offset],
            device_id={"tm": peer, "sx": ix, "sy": iy},
            device_id_type=pl.DeviceIdType.MESH,
        )

    def rate_copy(offset):
        peer = (here + offset) % spatial
        return pltpu.make_async_remote_copy(
            src_ref=rate_tiles.at[here],
            dst_ref=rate_tiles.at[here],
            send_sem=rate_send.at[offset],
            recv_sem=rate_recv.at[offset],
            device_id={"tm": tm, "sx": peer // nsy, "sy": peer % nsy},
            device_id_type=pl.DeviceIdType.MESH,
        )

    for offset in range(1, spatial):
        rate_copy(offset).start()
    for offset in range(1, teams):
        there(offset).start()
    recv_buf[pl.ds(pl.multiple_of(tm * chunk, chunk), chunk), :] = send_buf[
        pl.ds(pl.multiple_of(tm * chunk, chunk), chunk), :
    ]

    shift_real = shift_ref[0:1, :]
    shift_cross = shift_ref[1:2, :]

    def divisors(x, carry):
        rows = cell_rates[pl.ds(x, nz, stride=nx), :]
        rows = pltpu.roll(rows, ((teams - tm) * width) % lanes, 1)
        for y in range(width):
            diag = jnp.broadcast_to(rows[:, y : y + 1], (nz, total)) + 6.0 + shift_real
            inverse = 1.0 / (diag * diag + shift_cross * shift_cross)
            at = pl.ds(pl.multiple_of(x * row_cells + y * nz, nz), nz)
            inv_real[at, :] = diag * inverse
            inv_cross[at, :] = shift_cross * inverse
        return carry

    lax.fori_loop(0, nx, divisors, 0)

    ncy = nsy * teams
    for offset in range(1, spatial):
        rate_copy(offset).wait()
    strip_block = lax.broadcasted_iota(jnp.int32, (nx, lanes), 1) // width
    faces = 2 * (width * nz + nx * nz)
    couple_x = -float(width * nz)
    couple_y = -float(nx * nz)
    unknowns = ncy * nsx
    band = [[None] * (nsx + 1) for _ in range(unknowns)]
    right = []
    own = (iy * teams + tm) * nsx + ix
    for gy in range(ncy):
        for gx in range(nsx):
            number = gy * nsx + gx
            tile = rate_tiles[gx * nsy + gy // teams]
            amount = jnp.sum(jnp.where(strip_block == gy % teams, tile, 0.0), axis=0, keepdims=True)
            amount = jnp.sum(amount, axis=1, keepdims=True)
            band[number][0] = amount + faces + float(nx * width * nz) * shift_real
            if gx + 1 < nsx:
                band[number][1] = jnp.full((1, total), couple_x, jnp.float32)
            if gy + 1 < ncy:
                extra = jnp.full((1, total), couple_y, jnp.float32)
                before = band[number][nsx]
                band[number][nsx] = extra if before is None else before + extra
            right.append(jnp.where(own == number, jnp.ones((1, total), jnp.float32), 0.0))
    inverses = []
    for i in range(unknowns):
        inverse = 1.0 / band[i][0]
        inverses.append(inverse)
        for a in range(1, nsx + 1):
            if band[i][a] is None or i + a >= unknowns:
                continue
            ratio = band[i][a] * inverse
            right[i + a] = right[i + a] - ratio * right[i]
            for b in range(a, nsx + 1):
                if band[i][b] is None or i + b >= unknowns:
                    continue
                term = ratio * band[i][b]
                before = band[i + a][b - a]
                band[i + a][b - a] = -term if before is None else before - term
    row_solution = [None] * unknowns
    for i in reversed(range(unknowns)):
        value = right[i]
        for a in range(1, nsx + 1):
            if i + a < unknowns and band[i][a] is not None:
                value = value - band[i][a] * row_solution[i + a]
        row_solution[i] = value * inverses[i]
    zero_row = jnp.zeros((1, total), jnp.float32)

    def weight(gx, gy):
        inside = 0 <= gx < nsx and 0 <= gy < ncy
        return row_solution[gy * nsx + gx] if inside else zero_row

    for gy in range(ncy):
        for gx in range(nsx):
            slot = (gy % teams) * spatial + gx * nsy + gy // teams
            weights[slot] = jnp.concatenate(
                [
                    weight(gx, gy),
                    weight(gx - 1, gy),
                    weight(gx + 1, gy),
                    weight(gx, gy - 1),
                    weight(gx, gy + 1),
                    zero_row,
                    zero_row,
                    zero_row,
                ],
                axis=0,
            )

    strip = iy * teams + tm
    has = (ix > 0, ix < nsx - 1, strip > 0, strip < ncy - 1)

    def strip_place(rank):
        return {"tm": rank % teams, "sx": ix, "sy": rank // teams}

    neighbour = (
        {"tm": tm, "sx": (ix + nsx - 1) % nsx, "sy": iy},
        {"tm": tm, "sx": (ix + 1) % nsx, "sy": iy},
        strip_place((strip + ncy - 1) % ncy),
        strip_place((strip + 1) % ncy),
    )
    xs, ys = pl.ds(1, nx), pl.ds(1, width)
    iterates = (iterate_0, iterate_1, iterate_2)

    def layers(ref):
        edges = (ref.at[1, ys], ref.at[nx, ys], ref.at[xs, 1], ref.at[xs, width])
        halos = (ref.at[0, ys], ref.at[nx + 1, ys], ref.at[xs, 0], ref.at[xs, width + 1])
        return edges, halos

    for ref in iterates:
        _, halos = layers(ref)
        for side in range(4):

            @pl.when(jnp.logical_not(has[side]))
            def _(halo=halos[side]):
                halo[...] = jnp.zeros(halo.shape, jnp.float32)

    def halo_copies(number):
        edges, halos = layers(iterates[number])
        return [
            pltpu.make_async_remote_copy(
                src_ref=edges[side],
                dst_ref=halos[side ^ 1],
                send_sem=halo_send.at[number * 4 + side],
                recv_sem=halo_recv.at[number * 4 + (side ^ 1)],
                device_id=neighbour[side],
                device_id_type=pl.DeviceIdType.MESH,
            )
            for side in range(4)
        ]

    def exchange(number):
        copies = halo_copies(number)
        for side in range(4):

            @pl.when(has[side])
            def _(copy=copies[side]):
                copy.start()

        for side in range(4):

            @pl.when(has[side])
            def _(side=side):
                copies[side].wait_send()
                copies[side ^ 1].wait_recv()

    def divide(x, values):
        at = pl.ds(pl.multiple_of(x * row_cells, row_cells), row_cells)
        turned = pltpu.roll(values, half, 1)
        return inv_real[at, :] * values + inv_cross[at, :] * turned

    for offset in range(1, teams):
        there(offset).wait()

    def transform(x, carry):
        for group in range(groups):
            block = recv_buf[pl.ds(group * nx + x, total, stride=groups * nx), :]
            block = lax.dot_general(
                block,
                forward_ref[...],
                (((0,), (0,)), ((), ())),
                precision=highest,
                preferred_element_type=jnp.float32,
            )
            for j in range(teams):
                z = group * teams + j
                source[pl.ds(x * row_cells + z, width, stride=nz), :] = block[
                    j * width : (j + 1) * width
                ]
        at = pl.ds(pl.multiple_of(x * row_cells, row_cells), row_cells)
        iterate_0[x + 1, ys] = divide(x, source[at, :]).reshape(width, nz, total)
        return carry

    lax.fori_loop(0, nx, transform, 0)

    def sweep(old, x):
        middle = old[x + 1, ys]
        running = old[x, ys] + old[x + 2, ys]
        running = running + old[x + 1, pl.ds(0, width)] + old[x + 1, pl.ds(2, width)]
        running = running + pltpu.roll(middle, 1, 1) + pltpu.roll(middle, nz - 1, 1)
        at = pl.ds(pl.multiple_of(x * row_cells, row_cells), row_cells)
        return divide(x, source[at, :] + running.reshape(row_cells, total))

    for number in range(2):
        exchange(number)

        def advance(x, carry, old=iterates[number], new=iterates[number + 1]):
            new[x + 1, ys] = sweep(old, x).reshape(width, nz, total)
            return carry

        lax.fori_loop(0, nx, advance, 0)
    exchange(2)

    def finish(x, carry):
        sums, weighted, sources, low_y, high_y = carry
        values = sweep(iterate_2, x)
        at = pl.ds(pl.multiple_of(x * row_cells, row_cells), row_cells)
        final[at, :] = values
        cells = values.reshape(width, nz, total)
        rows = cell_rates[pl.ds(x, nz, stride=nx), :]
        rows = pltpu.roll(rows, ((teams - tm) * width) % lanes, 1)
        for y in range(width):
            weighted = weighted + cells[y] * rows[:, y : y + 1]
        sources = sources + jnp.sum(source[at, :].reshape(width, nz, total), axis=0)
        layer = jnp.sum(cells, axis=0)
        return sums + layer, weighted, sources, low_y + cells[0], high_y + cells[width - 1]

    blank = jnp.zeros((nz, total), jnp.float32)
    sums, weighted, sources, low_y, high_y = lax.fori_loop(
        0, nx, finish, (blank, blank, blank, blank, blank)
    )
    layer_rows = width * nz
    low_x = jnp.sum(final[0:layer_rows, :].reshape(width, nz, total), axis=0)
    high_x = jnp.sum(
        final[(nx - 1) * layer_rows : nx * layer_rows, :].reshape(width, nz, total), axis=0
    )
    balance = sources - weighted - shift_real * sums + shift_cross * pltpu.roll(sums, half, 1)
    balance = balance - low_x - high_x - low_y - high_y
    coarse_tiles[me] = jnp.concatenate(
        [
            jnp.sum(part, axis=0, keepdims=True)
            for part in (balance, low_x, high_x, low_y, high_y)
        ]
        + [zero_row] * 3,
        axis=0,
    )

    def coarse_copy(offset):
        return pltpu.make_async_remote_copy(
            src_ref=coarse_tiles.at[me],
            dst_ref=coarse_tiles.at[me],
            send_sem=coarse_send.at[offset],
            recv_sem=coarse_recv.at[offset],
            device_id=place((me + offset) % devices),
            device_id_type=pl.DeviceIdType.MESH,
        )

    def coarse_start(offset, carry):
        coarse_copy(offset).start()
        return carry

    def coarse_wait(offset, carry):
        coarse_copy(offset).wait()
        return carry

    lax.fori_loop(1, devices, coarse_start, 0)
    lax.fori_loop(1, devices, coarse_wait, 0)
    correction = jnp.sum(coarse_tiles[...] * weights[...], axis=0)
    correction = jnp.sum(correction, axis=0, keepdims=True)

    def restore(x, carry):
        for group in range(groups):
            block = jnp.concatenate(
                [
                    final[pl.ds(x * row_cells + group * teams + j, width, stride=nz), :]
                    for j in range(teams)
                ],
                axis=0,
            )
            block = lax.dot_general(
                backward_ref[...],
                block + correction,
                (((1,), (1,)), ((), ())),
                precision=highest,
                preferred_element_type=jnp.float32,
            )
            send_back[pl.ds(group * nx + x, total, stride=groups * nx), :] = block
        return carry

    lax.fori_loop(0, nx, restore, 0)

    def back(offset):
        peer = (tm + offset) % teams
        return pltpu.make_async_remote_copy(
            src_ref=chunk_of(send_back, peer),
            dst_ref=chunk_of(recv_back, tm),
            send_sem=back_send.at[offset],
            recv_sem=back_recv.at[offset],
            device_id={"tm": peer, "sx": ix, "sy": iy},
            device_id_type=pl.DeviceIdType.MESH,
        )

    for offset in range(1, teams):
        back(offset).start()
    recv_back[pl.ds(pl.multiple_of(tm * chunk, chunk), chunk), :] = send_back[
        pl.ds(pl.multiple_of(tm * chunk, chunk), chunk), :
    ]
    for offset in range(1, teams):
        back(offset).wait()

    def unpack(index, carry):
        first = index * step
        for group in range(groups):
            parts = []
            for origin in range(teams):
                rows = []
                for inner in range(step):
                    row = origin * chunk + ((first + inner) * groups + group) * nx
                    rows.append(recv_back[pl.ds(pl.multiple_of(row, nx), nx), :])
                parts.append(jnp.stack(rows))
            parts = swap(parts)
            for j in range(teams):
                out_ref[pl.ds(first, step), group * teams + j] = parts[j]
        return carry

    lax.fori_loop(0, moments // step, unpack, 0)


def local_fused(teams, nsx, nsy, driving_input, regime, reaction_rates):
    moments, nz, nx, lanes = driving_input.shape
    width = lanes // teams
    total = teams * moments
    forward, backward, shift = time_tables(total)
    sizes = (teams, nsx, nsy, moments, nz, nx, lanes, width)
    cells = nx * width * nz
    devices = teams * nsx * nsy
    rows = total * (nz // teams) * nx
    f32 = jnp.float32
    padded = pltpu.VMEM((nx + 2, width + 2, nz, total), f32)
    vmem = pl.BlockSpec(memory_space=pltpu.VMEM)
    dma = pltpu.SemaphoreType.DMA
    return pl.pallas_call(
        functools.partial(fused_kernel, sizes),
        out_shape=jax.ShapeDtypeStruct(driving_input.shape, f32),
        in_specs=[pl.BlockSpec(memory_space=pltpu.SMEM)] + [vmem] * 5,
        out_specs=vmem,
        scratch_shapes=[
            pltpu.VMEM((rows, lanes), f32),
            pltpu.VMEM((rows, lanes), f32),
            pltpu.VMEM((rows, lanes), f32),
            pltpu.VMEM((rows, lanes), f32),
            pltpu.VMEM((nz * nx, lanes), f32),
            pltpu.VMEM((nsx * nsy, nx, lanes), f32),
            pltpu.VMEM((devices, 8, total), f32),
            pltpu.VMEM((devices, 8, total), f32),
            pltpu.VMEM((cells, total), f32),
            pltpu.VMEM((cells, total), f32),
            pltpu.VMEM((cells, total), f32),
            padded,
            padded,
            padded,
            pltpu.VMEM((cells, total), f32),
            dma((teams,)),
            dma((teams,)),
            dma((teams,)),
            dma((teams,)),
            dma((nsx * nsy,)),
            dma((nsx * nsy,)),
            dma((devices,)),
            dma((devices,)),
            dma((12,)),
            dma((12,)),
        ],
        compiler_params=pltpu.CompilerParams(
            collective_id=0, has_side_effects=True, vmem_limit_bytes=48 * 1024 * 1024
        ),
    )(
        reaction_rates,
        driving_input,
        regime,
        jnp.asarray(forward),
        jnp.asarray(backward),
        jnp.asarray(shift),
    )


def local(driving_input, regime, reaction_rates):
    moments, nz, nx, lanes = driving_input.shape
    teams, nsx, nsy = (lax.axis_size(axis) for axis in ("tm", "sx", "sy"))
    one_aggregate = nx == AGGREGATE_XCELLS and lanes == teams * AGGREGATE_YCELLS
    tiled = nx == 8 and nz == 8 and nz % teams == 0 and lanes == 128
    if one_aggregate and tiled and teams * moments == 128 and SWEEPS == 4:
        return local_fused(teams, nsx, nsy, driving_input, regime, reaction_rates)
    return local_general(driving_input, regime, reaction_rates)


def solution(mesh):
    placed = (P("tm", None, "sx", "sy"), P(None, "sx", "sy"), P())
    return jax.shard_map(
        local, mesh=mesh, in_specs=placed, out_specs=P("tm", None, "sx", "sy"), check_vma=False
    )
```

```python
import functools

import jax
import jax.numpy as jnp
import numpy as np
from jax import lax
from jax.experimental import pallas as pl
from jax.experimental.pallas import tpu as pltpu
from jax.sharding import PartitionSpec as P

AGGREGATE_XCELLS = 8
AGGREGATE_YCELLS = 32
SWEEPS = 4


TWO_PI = 2.0 * 3.141592653589793


def extended(block, sides, width):
    for axis, dim in sides:
        count = lax.axis_size(axis)
        forward = [(i, i + 1) for i in range(count - 1)]
        backward = [(target, source) for source, target in forward]
        low = lax.ppermute(
            lax.slice_in_dim(block, block.shape[dim] - width, None, axis=dim), axis, forward
        )
        high = lax.ppermute(lax.slice_in_dim(block, 0, width, axis=dim), axis, backward)
        block = jnp.concatenate([low, block, high], axis=dim)
    return block


def angle_table(row_index, col_index, cycle_duration):
    product = row_index[:, None] * col_index[None, :] % cycle_duration
    angles = product.astype(jnp.float32) * (TWO_PI / cycle_duration)
    return (jnp.cos(angles), jnp.sin(angles))


def matmul(left_side, right_side):
    return jnp.dot(
        left_side, right_side, precision=lax.Precision.HIGHEST, preferred_element_type=jnp.float32
    )


def complex_mul(left_real, left_imag, pair):
    return jnp.stack(
        [left_real * pair[0] - left_imag * pair[1], left_real * pair[1] + left_imag * pair[0]]
    )


def neighbors(present_guess):
    padded = extended(present_guess, (("sx", 3), ("sy", 4)), 1)
    running = padded[:, :, :, 2:, 1:-1] + padded[:, :, :, :-2, 1:-1]
    running = running + padded[:, :, :, 1:-1, 2:] + padded[:, :, :, 1:-1, :-2]
    running = running + jnp.roll(present_guess, 1, axis=2) + jnp.roll(present_guess, -1, axis=2)
    return running


def local_general(driving_input, regime, reaction_rates):
    moment_count, third_axis_count, first_axis_count, second_axis_count = driving_input.shape
    temporal_spacing = lax.axis_size("tm")
    sy_size = lax.axis_size("sy")
    cycle_duration = moment_count * temporal_spacing
    unknowns_in_tile = third_axis_count * first_axis_count * second_axis_count
    processor_lines = driving_input.reshape(moment_count, unknowns_in_tile)
    owned_slice_number = lax.axis_index("tm") * moment_count + jnp.arange(
        moment_count, dtype=jnp.int32
    )
    all_index = jnp.arange(cycle_duration, dtype=jnp.int32)
    cos_rows, sin_rows = angle_table(owned_slice_number, all_index, cycle_duration)

    def forward(running, segment, offset):
        return jnp.stack([matmul(cos_rows, segment), -matmul(sin_rows, segment)])

    eigen_spectra = forward(
        jnp.zeros((2, moment_count, unknowns_in_tile), jnp.float32),
        lax.all_gather(processor_lines, "tm", axis=0, tiled=True),
        jnp.int32(0),
    )
    source_term = eigen_spectra.reshape(
        2, moment_count, third_axis_count, first_axis_count, second_axis_count
    )
    phase_angle = owned_slice_number.astype(jnp.float32) * (TWO_PI / cycle_duration)
    shift_real = (1.0 - jnp.cos(phase_angle))[:, None, None, None]
    shift_imag = jnp.sin(phase_angle)[:, None, None, None]
    reaction = jnp.zeros(regime.shape, jnp.float32)
    for regime_no in range(reaction_rates.shape[0]):
        reaction = reaction + jnp.where(
            regime == regime_no, reaction_rates[regime_no], jnp.zeros((), jnp.float32)
        )
    diag_real = reaction[None] + 6.0 + shift_real
    diag_imag = jnp.zeros_like(diag_real) + shift_imag
    modulus = diag_real * diag_real + diag_imag * diag_imag
    inverse_real = diag_real / modulus
    inverse_imag = -diag_imag / modulus
    present_guess = complex_mul(inverse_real, inverse_imag, source_term)
    for sweep_no in range(SWEEPS - 1):
        present_guess = complex_mul(
            inverse_real, inverse_imag, source_term + neighbors(present_guess)
        )
    applied = complex_mul(diag_real, diag_imag, present_guess) - neighbors(present_guess)
    residual = source_term - applied
    first_axis_teams = first_axis_count // AGGREGATE_XCELLS
    second_axis_teams = second_axis_count // AGGREGATE_YCELLS
    per_device = first_axis_teams * second_axis_teams

    def aggregate(values):
        leading = values.shape[:-3]
        blocks = values.reshape(
            leading
            + (
                third_axis_count,
                first_axis_teams,
                AGGREGATE_XCELLS,
                second_axis_teams,
                AGGREGATE_YCELLS,
            )
        )
        return jnp.sum(blocks, axis=(-5, -3, -1)).reshape(leading + (per_device,))

    coarse_right = jnp.transpose(aggregate(residual), (1, 0, 2))
    rate_sums = aggregate(reaction)
    shift_column = 1.0 - jnp.cos(phase_angle)
    face_count = 2 * (AGGREGATE_YCELLS * third_axis_count + AGGREGATE_XCELLS * third_axis_count)
    volume = AGGREGATE_XCELLS * AGGREGATE_YCELLS * third_axis_count
    spatial = lax.axis_size("sx") * sy_size
    slot_count = -(-moment_count // spatial)
    padding_rows = slot_count * spatial - moment_count
    padded_right = jnp.pad(coarse_right, ((0, padding_rows), (0, 0), (0, 0)))
    sum_copies = jnp.broadcast_to(rate_sums[None, None, :], (spatial, 1, per_device))
    shared_right, shared_sums = (
        lax.all_to_all(padded_right, ("sx", "sy"), split_axis=0, concat_axis=2, tiled=True),
        lax.all_to_all(sum_copies, ("sx", "sy"), split_axis=0, concat_axis=2, tiled=True),
    )
    spatial_rank = lax.axis_index("sx") * sy_size + lax.axis_index("sy")
    padded_shift = jnp.pad(shift_column, (0, padding_rows))
    slot_shift = lax.dynamic_slice_in_dim(padded_shift, spatial_rank * slot_count, slot_count, 0)
    sum_values = shared_sums[0, 0]
    coarse_total = sum_values.shape[0]
    position = jnp.arange(coarse_total, dtype=jnp.int32)
    device = position // per_device
    within = position % per_device
    coarse_x = device // sy_size * first_axis_teams + within // second_axis_teams
    coarse_y = device % sy_size * second_axis_teams + within % second_axis_teams
    x_gap = jnp.abs(coarse_x[:, None] - coarse_x[None, :])
    y_gap = jnp.abs(coarse_y[:, None] - coarse_y[None, :])
    coupling = -(AGGREGATE_YCELLS * third_axis_count) * ((x_gap == 1) & (y_gap == 0)).astype(
        jnp.float32
    )
    coupling = coupling - AGGREGATE_XCELLS * third_axis_count * (
        (x_gap == 0) & (y_gap == 1)
    ).astype(jnp.float32)
    identity = (position[:, None] == position[None, :]).astype(jnp.float32)
    diagonal = sum_values + face_count
    system = (
        coupling[None]
        + identity[None] * (diagonal[None, :] + volume * slot_shift[:, None])[:, None, :]
    )
    factor = jnp.linalg.cholesky(system)
    right_side = jnp.transpose(shared_right, (0, 2, 1))
    forward_sub = lax.linalg.triangular_solve(factor, right_side, left_side=True, lower=True)
    coarse = lax.linalg.triangular_solve(
        factor, forward_sub, left_side=True, lower=True, transpose_a=True
    )
    solved = jnp.transpose(coarse, (0, 2, 1))
    returned = lax.all_to_all(solved, ("sx", "sy"), split_axis=2, concat_axis=0, tiled=True)
    own_coarse = returned[:moment_count]
    local_part = jnp.transpose(own_coarse, (1, 0, 2)).reshape(
        2, moment_count, 1, first_axis_teams, 1, second_axis_teams, 1
    )
    spread_values = jnp.broadcast_to(
        local_part,
        (
            2,
            moment_count,
            third_axis_count,
            first_axis_teams,
            AGGREGATE_XCELLS,
            second_axis_teams,
            AGGREGATE_YCELLS,
        ),
    )
    present_guess = present_guess + spread_values.reshape(
        2, moment_count, third_axis_count, first_axis_count, second_axis_count
    )
    unrolled_array = present_guess.reshape(2, moment_count, unknowns_in_tile)

    def backward(running, segment, offset):
        return matmul(cos_rows, segment[0]) - matmul(sin_rows, segment[1])

    result = (
        backward(
            jnp.zeros((moment_count, unknowns_in_tile), jnp.float32),
            lax.all_gather(unrolled_array, "tm", axis=1, tiled=True),
            jnp.int32(0),
        )
        / cycle_duration
    )
    return result.reshape(driving_input.shape)


def time_tables(count):
    half = count // 2
    lane = np.arange(count)
    frequency = np.where(lane <= half, lane, lane - half)
    imaginary = lane > half
    moment = np.arange(count)
    angle = 2.0 * np.pi * (moment[:, None] * frequency[None, :] % count) / count
    forward = np.where(imaginary[None, :], -np.sin(angle), np.cos(angle))
    weight = np.where((lane == 0) | (lane == half), 1.0, 2.0) / count
    theta = 2.0 * np.pi * frequency / count
    signed = np.where(lane % half == 0, 0.0, np.sin(theta)) * np.where(lane < half, 1.0, -1.0)
    shift = np.zeros((8, count))
    shift[0] = 1.0 - np.cos(theta)
    shift[1] = signed
    return np.concatenate([forward, forward * weight[None, :], shift]).astype(np.float32)


def fused_kernel(
    sizes,
    rates_ref,
    field_hbm,
    regime_hbm,
    table_hbm,
    out_hbm,
    field_ref,
    regime_ref,
    table_ref,
    out_ref,
    send_buf,
    recv_buf,
    send_back,
    recv_back,
    cell_rates,
    rate_tiles,
    coarse_tiles,
    solved_tiles,
    shifts,
    source,
    inv_real,
    inv_cross,
    iterate_0,
    iterate_1,
    iterate_2,
    final,
    load_sem,
    store_sem,
    there_send,
    there_recv,
    back_send,
    back_recv,
    rate_send,
    rate_recv,
    coarse_send,
    coarse_recv,
    halo_send,
    halo_recv,
):
    teams, nsx, nsy, moments, nz, nx, lanes, width = sizes
    total = teams * moments
    half = total // 2
    groups = nz // teams
    piece = moments * nx
    row_cells = width * nz
    spatial = nsx * nsy
    devices = teams * spatial
    highest = lax.Precision.HIGHEST
    tm = lax.axis_index("tm")
    ix = lax.axis_index("sx")
    iy = lax.axis_index("sy")
    here = ix * nsy + iy
    me = tm * spatial + here

    def group_part(ref, group):
        return ref.at[:, pl.ds(group * teams, teams)]

    loads = [
        pltpu.make_async_copy(
            group_part(field_hbm, group), group_part(field_ref, group), load_sem.at[group]
        )
        for group in range(groups)
    ]
    loads.append(pltpu.make_async_copy(regime_hbm, regime_ref, load_sem.at[groups]))
    loads.append(pltpu.make_async_copy(table_hbm, table_ref, load_sem.at[groups + 1]))
    for load in loads:
        load.start()

    def place(rank):
        return {
            "tm": rank // spatial,
            "sx": (rank % spatial) // nsy,
            "sy": rank % nsy,
        }

    barrier = pltpu.get_barrier_semaphore()

    def greet(offset, carry):
        pl.semaphore_signal(
            barrier,
            inc=1,
            device_id=place((me + offset) % devices),
            device_id_type=pl.DeviceIdType.MESH,
        )
        return carry

    lax.fori_loop(1, devices, greet, 0)

    lane_block = lax.broadcasted_iota(jnp.int32, (1, nx, lanes), 2) // width

    def swap(parts):
        if teams & (teams - 1) == 0:
            bit = teams // 2
            while bit:
                upper = lane_block & bit != 0
                result = list(parts)
                for low in range(teams):
                    if low & bit:
                        continue
                    first, second = parts[low], parts[low | bit]
                    result[low] = jnp.where(upper, pltpu.roll(second, width * bit, 2), first)
                    result[low | bit] = jnp.where(
                        upper, second, pltpu.roll(first, lanes - width * bit, 2)
                    )
                parts = result
                bit //= 2
            return parts
        result = []
        for target in range(teams):
            merged = parts[target]
            for other in range(teams):
                if other != target:
                    turn = (width * (other - target)) % lanes
                    merged = jnp.where(
                        lane_block == other, pltpu.roll(parts[other], turn, 2), merged
                    )
            result.append(merged)
        return result

    step = 4

    def row_at(group, origin, moment):
        return pl.ds(
            pl.multiple_of((group * teams + origin) * piece + moment * nx, nx), step * nx
        )

    def pack(group):
        def body(index, carry):
            first = index * step
            parts = swap(
                [field_ref[pl.ds(first, step), group * teams + j] for j in range(teams)]
            )
            for target in range(teams):
                send_buf[row_at(group, target, first), :] = parts[target].reshape(
                    step * nx, lanes
                )
            return carry

        lax.fori_loop(0, moments // step, body, 0)

    def piece_of(ref, group, index):
        return ref.at[pl.ds(pl.multiple_of((group * teams + index) * piece, piece), piece), :]

    def over_teams(source_buf, target_buf, send_sem, recv_sem, group, offset):
        peer = (tm + offset) % teams
        return pltpu.make_async_remote_copy(
            src_ref=piece_of(source_buf, group, peer),
            dst_ref=piece_of(target_buf, group, tm),
            send_sem=send_sem.at[group * teams + offset],
            recv_sem=recv_sem.at[group * teams + offset],
            device_id={"tm": peer, "sx": ix, "sy": iy},
            device_id_type=pl.DeviceIdType.MESH,
        )

    def there(group, offset):
        return over_teams(send_buf, recv_buf, there_send, there_recv, group, offset)

    def back(group, offset):
        return over_teams(send_back, recv_back, back_send, back_recv, group, offset)

    def keep(source_buf, target_buf, group):
        at = pl.ds(pl.multiple_of((group * teams + tm) * piece, piece), piece)
        target_buf[at, :] = source_buf[at, :]

    for group in range(groups):
        loads[group].wait()
        pack(group)
        if group == 0:
            pl.semaphore_wait(barrier, devices - 1)
        for offset in range(1, teams):
            there(group, offset).start()

    loads[groups].wait()
    rates = jnp.zeros(regime_ref.shape, jnp.float32)
    regime = regime_ref[...]
    for number in range(rates_ref.shape[0]):
        rates = rates + jnp.where(regime == number, rates_ref[number], 0.0)
    cell_rates[...] = rates.reshape(nz * nx, lanes)
    rate_tiles[here] = jnp.sum(rates, axis=0)

    def rate_copy(offset):
        peer = (here + offset) % spatial
        return pltpu.make_async_remote_copy(
            src_ref=rate_tiles.at[here],
            dst_ref=rate_tiles.at[here],
            send_sem=rate_send.at[offset],
            recv_sem=rate_recv.at[offset],
            device_id={"tm": tm, "sx": peer // nsy, "sy": peer % nsy},
            device_id_type=pl.DeviceIdType.MESH,
        )

    for offset in range(1, spatial):
        rate_copy(offset).start()
    for group in range(groups):
        keep(send_buf, recv_buf, group)
    loads[groups + 1].wait()

    shift_real = table_ref[2 * total : 2 * total + 1, :]
    shift_cross = table_ref[2 * total + 1 : 2 * total + 2, :]

    def divisors(x, carry):
        rows = cell_rates[pl.ds(x, nz, stride=nx), :]
        rows = pltpu.roll(rows, ((teams - tm) * width) % lanes, 1)
        for y in range(width):
            diag = jnp.broadcast_to(rows[:, y : y + 1], (nz, total)) + 6.0 + shift_real
            inverse = 1.0 / (diag * diag + shift_cross * shift_cross)
            at = pl.ds(pl.multiple_of(x * row_cells + y * nz, nz), nz)
            inv_real[at, :] = diag * inverse
            inv_cross[at, :] = shift_cross * inverse
        return carry

    lax.fori_loop(0, nx, divisors, 0)

    ncy = nsy * teams
    for offset in range(1, spatial):
        rate_copy(offset).wait()
    strip_block = lax.broadcasted_iota(jnp.int32, (nx, lanes), 1) // width
    faces = 2 * (width * nz + nx * nz)
    couple_x = -float(width * nz)
    couple_y = -float(nx * nz)
    unknowns = ncy * nsx
    band = [[None] * (nsx + 1) for _ in range(unknowns)]
    for gy in range(ncy):
        for gx in range(nsx):
            number = gy * nsx + gx
            tile = rate_tiles[gx * nsy + gy // teams]
            amount = jnp.sum(jnp.where(strip_block == gy % teams, tile, 0.0), axis=0, keepdims=True)
            amount = jnp.sum(amount, axis=1, keepdims=True)
            band[number][0] = amount + faces + float(nx * width * nz) * shift_real
            if gx + 1 < nsx:
                band[number][1] = jnp.full((1, total), couple_x, jnp.float32)
            if gy + 1 < ncy:
                extra = jnp.full((1, total), couple_y, jnp.float32)
                before = band[number][nsx]
                band[number][nsx] = extra if before is None else before + extra
    inverses = []
    ratios = []
    for i in range(unknowns):
        inverse = 1.0 / band[i][0]
        inverses.append(inverse)
        ratios.append([None] * (nsx + 1))
        for a in range(1, nsx + 1):
            if band[i][a] is None or i + a >= unknowns:
                continue
            ratio = band[i][a] * inverse
            ratios[i][a] = ratio
            for b in range(a, nsx + 1):
                if band[i][b] is None or i + b >= unknowns:
                    continue
                term = ratio * band[i][b]
                before = band[i + a][b - a]
                band[i + a][b - a] = -term if before is None else before - term

    strip = iy * teams + tm
    has = (ix > 0, ix < nsx - 1, strip > 0, strip < ncy - 1)

    def strip_place(rank):
        return {"tm": rank % teams, "sx": ix, "sy": rank // teams}

    neighbour = (
        {"tm": tm, "sx": (ix + nsx - 1) % nsx, "sy": iy},
        {"tm": tm, "sx": (ix + 1) % nsx, "sy": iy},
        strip_place((strip + ncy - 1) % ncy),
        strip_place((strip + 1) % ncy),
    )
    xs, ys = pl.ds(1, nx), pl.ds(1, width)
    iterates = (iterate_0, iterate_1, iterate_2)

    def layers(ref):
        edges = (ref.at[1, ys], ref.at[nx, ys], ref.at[xs, 1], ref.at[xs, width])
        halos = (ref.at[0, ys], ref.at[nx + 1, ys], ref.at[xs, 0], ref.at[xs, width + 1])
        return edges, halos

    for ref in iterates:
        _, halos = layers(ref)
        for side in range(4):

            @pl.when(jnp.logical_not(has[side]))
            def _(halo=halos[side]):
                halo[...] = jnp.zeros(halo.shape, jnp.float32)

    def halo_copies(number, sides):
        edges, halos = layers(iterates[number])
        return [
            pltpu.make_async_remote_copy(
                src_ref=edges[side],
                dst_ref=halos[side ^ 1],
                send_sem=halo_send.at[number * 4 + side],
                recv_sem=halo_recv.at[number * 4 + (side ^ 1)],
                device_id=neighbour[side],
                device_id_type=pl.DeviceIdType.MESH,
            )
            for side in sides
        ]

    def exchange_start(number, sides):
        for side, copy in zip(sides, halo_copies(number, sides)):

            @pl.when(has[side])
            def _(copy=copy):
                copy.start()

    def exchange_wait(number):
        copies = halo_copies(number, range(4))
        for side in range(4):

            @pl.when(has[side])
            def _(side=side):
                copies[side].wait_send()
                copies[side ^ 1].wait_recv()

    def cells_at(x, first, count):
        return pl.ds(pl.multiple_of(x * row_cells + first * nz, nz), count * nz)

    def divide(at, values):
        turned = pltpu.roll(values, half, 1)
        return inv_real[at, :] * values + inv_cross[at, :] * turned

    def sweep(old, x, first, count):
        middle = old[x + 1, pl.ds(first + 1, count)]
        running = old[x, pl.ds(first + 1, count)] + old[x + 2, pl.ds(first + 1, count)]
        running = running + old[x + 1, pl.ds(first, count)]
        running = running + old[x + 1, pl.ds(first + 2, count)]
        running = running + pltpu.roll(middle, 1, 1) + pltpu.roll(middle, nz - 1, 1)
        at = cells_at(x, first, count)
        return divide(at, source[at, :] + running.reshape(count * nz, total))

    def update(number, x, first, count):
        at = cells_at(x, first, count)
        if number == 0:
            values = divide(at, source[at, :])
        else:
            values = sweep(iterates[number - 1], x, first, count)
        iterates[number][x + 1, pl.ds(first + 1, count)] = values.reshape(count, nz, total)

    def advance(number):
        if number:
            exchange_wait(number - 1)
        update(number, 0, 0, width)
        update(number, nx - 1, 0, width)
        exchange_start(number, (0, 1))

        def edge(x, carry):
            update(number, x, 0, 1)
            update(number, x, width - 1, 1)
            return carry

        def inner(x, carry):
            update(number, x, 1, width - 2)
            return carry

        lax.fori_loop(1, nx - 1, edge, 0, unroll=True)
        exchange_start(number, (2, 3))
        lax.fori_loop(1, nx - 1, inner, 0)

    for group in range(groups):
        for offset in range(1, teams):
            there(group, offset).wait()

        def transform(x, carry, group=group):
            block = recv_buf[pl.ds(group * teams * piece + x, total, stride=nx), :]
            block = lax.dot_general(
                block,
                table_ref[0:total, :],
                (((0,), (0,)), ((), ())),
                precision=highest,
                preferred_element_type=jnp.float32,
            )
            for j in range(teams):
                z = group * teams + j
                source[pl.ds(x * row_cells + z, width, stride=nz), :] = block[
                    j * width : (j + 1) * width
                ]
            return carry

        lax.fori_loop(0, nx, transform, 0, unroll=4)

    for number in range(3):
        advance(number)
    exchange_wait(2)

    def finish(x, carry):
        sums, low_y, high_y = carry
        values = sweep(iterate_2, x, 0, width)
        final[cells_at(x, 0, width), :] = values
        change = values.reshape(width, nz, total) - iterate_2[x + 1, ys]
        layer = jnp.sum(change, axis=0)
        shifts[x] = layer
        return sums + layer, low_y + change[0], high_y + change[width - 1]

    blank = jnp.zeros((nz, total), jnp.float32)
    sums, low_y, high_y = lax.fori_loop(0, nx, finish, (blank, blank, blank))
    low_x, high_x = shifts[0], shifts[nx - 1]
    balance = 6.0 * sums - low_x - high_x - low_y - high_y
    zero_row = jnp.zeros((1, total), jnp.float32)
    coarse_tiles[me] = jnp.concatenate(
        [
            jnp.sum(part, axis=0, keepdims=True)
            for part in (balance, low_x, high_x, low_y, high_y)
        ]
        + [zero_row] * 3,
        axis=0,
    )

    def coarse_copy(offset):
        return pltpu.make_async_remote_copy(
            src_ref=coarse_tiles.at[me],
            dst_ref=coarse_tiles.at[me],
            send_sem=coarse_send.at[offset],
            recv_sem=coarse_recv.at[offset],
            device_id=place((me + offset) % devices),
            device_id_type=pl.DeviceIdType.MESH,
        )

    def coarse_start(offset, carry):
        coarse_copy(offset).start()
        return carry

    def coarse_wait(offset, carry):
        coarse_copy(offset).wait()
        return carry

    for group in range(groups):

        def restore(x, carry, group=group):
            block = jnp.concatenate(
                [
                    final[pl.ds(x * row_cells + group * teams + j, width, stride=nz), :]
                    for j in range(teams)
                ],
                axis=0,
            )
            block = lax.dot_general(
                table_ref[total : 2 * total, :],
                block,
                (((1,), (1,)), ((), ())),
                precision=highest,
                preferred_element_type=jnp.float32,
            )
            send_back[pl.ds(group * teams * piece + x, total, stride=nx), :] = block
            return carry

        lax.fori_loop(0, nx, restore, 0, unroll=4)
        for offset in range(1, teams):
            back(group, offset).start()
        if group == 0:
            lax.fori_loop(1, devices, coarse_start, 0)

    for group in range(groups):
        keep(send_back, recv_back, group)
    lax.fori_loop(1, devices, coarse_wait, 0)

    def coarse_row(gx, gy, row):
        if not (0 <= gx < nsx and 0 <= gy < ncy):
            return zero_row
        slot = (gy % teams) * spatial + gx * nsy + gy // teams
        return coarse_tiles[slot, row : row + 1, :]

    right = []
    for gy in range(ncy):
        for gx in range(nsx):
            right.append(
                coarse_row(gx, gy, 0)
                + coarse_row(gx + 1, gy, 1)
                + coarse_row(gx - 1, gy, 2)
                + coarse_row(gx, gy + 1, 3)
                + coarse_row(gx, gy - 1, 4)
            )
    for i in range(unknowns):
        for a in range(1, nsx + 1):
            if ratios[i][a] is not None:
                right[i + a] = right[i + a] - ratios[i][a] * right[i]
    for i in reversed(range(unknowns)):
        value = right[i] * inverses[i]
        for a in range(1, nsx + 1):
            if ratios[i][a] is not None:
                value = value - ratios[i][a] * right[i + a]
        right[i] = value
    for gx in range(nsx):
        for block in range(nsy):
            for d in range(teams):
                number = (block * teams + d) * nsx + gx
                solved_tiles[gx * nsy + block, d : d + 1, :] = right[number]
    own_rows = solved_tiles[here]
    spread = jnp.concatenate(
        [jnp.broadcast_to(own_rows[d : d + 1], (width, total)) for d in range(teams)], axis=0
    )
    own_moments = pl.ds(pl.multiple_of(total + tm * moments, moments), moments)
    shifts[0:moments // nx] = lax.dot_general(
        table_ref[own_moments, :],
        spread,
        (((1,), (1,)), ((), ())),
        precision=highest,
        preferred_element_type=jnp.float32,
    ).reshape(moments // nx, nx, lanes)

    stores = []
    for group in range(groups):
        for offset in range(1, teams):
            back(group, offset).wait()

        def unpack(index, carry, group=group):
            first = index * nx
            added = shifts[index]
            for inner in range(0, nx, step):
                parts = swap(
                    [
                        recv_back[row_at(group, origin, first + inner), :].reshape(
                            step, nx, lanes
                        )
                        for origin in range(teams)
                    ]
                )
                amount = jnp.stack(
                    [
                        jnp.broadcast_to(added[k : k + 1], (nx, lanes))
                        for k in range(inner, inner + step)
                    ]
                )
                for j in range(teams):
                    out_ref[pl.ds(first + inner, step), group * teams + j] = parts[j] + amount
            return carry

        lax.fori_loop(0, moments // nx, unpack, 0)
        store = pltpu.make_async_copy(
            group_part(out_ref, group), group_part(out_hbm, group), store_sem.at[group]
        )
        store.start()
        stores.append(store)
    for store in stores:
        store.wait()


def local_fused(teams, nsx, nsy, driving_input, regime, reaction_rates):
    moments, nz, nx, lanes = driving_input.shape
    width = lanes // teams
    total = teams * moments
    table = time_tables(total)
    sizes = (teams, nsx, nsy, moments, nz, nx, lanes, width)
    cells = nx * width * nz
    devices = teams * nsx * nsy
    groups = nz // teams
    rows = total * groups * nx
    f32 = jnp.float32
    padded = pltpu.VMEM((nx + 2, width + 2, nz, total), f32)
    in_place = pl.BlockSpec(memory_space=pl.ANY)
    dma = pltpu.SemaphoreType.DMA
    return pl.pallas_call(
        functools.partial(fused_kernel, sizes),
        out_shape=jax.ShapeDtypeStruct(driving_input.shape, f32),
        in_specs=[pl.BlockSpec(memory_space=pltpu.SMEM)] + [in_place] * 3,
        out_specs=in_place,
        scratch_shapes=[
            pltpu.VMEM(driving_input.shape, f32),
            pltpu.VMEM(regime.shape, jnp.int32),
            pltpu.VMEM(table.shape, f32),
            pltpu.VMEM(driving_input.shape, f32),
            pltpu.VMEM((rows, lanes), f32),
            pltpu.VMEM((rows, lanes), f32),
            pltpu.VMEM((rows, lanes), f32),
            pltpu.VMEM((rows, lanes), f32),
            pltpu.VMEM((nz * nx, lanes), f32),
            pltpu.VMEM((nsx * nsy, nx, lanes), f32),
            pltpu.VMEM((devices, 8, total), f32),
            pltpu.VMEM((nsx * nsy, max(teams, 8), total), f32),
            pltpu.VMEM((max(nx, moments // nx), 8, total), f32),
            pltpu.VMEM((cells, total), f32),
            pltpu.VMEM((cells, total), f32),
            pltpu.VMEM((cells, total), f32),
            padded,
            padded,
            padded,
            pltpu.VMEM((cells, total), f32),
            dma((groups + 2,)),
            dma((groups,)),
            dma((groups * teams,)),
            dma((groups * teams,)),
            dma((groups * teams,)),
            dma((groups * teams,)),
            dma((nsx * nsy,)),
            dma((nsx * nsy,)),
            dma((devices,)),
            dma((devices,)),
            dma((12,)),
            dma((12,)),
        ],
        compiler_params=pltpu.CompilerParams(
            collective_id=0, has_side_effects=True, vmem_limit_bytes=60 * 1024 * 1024
        ),
    )(reaction_rates, driving_input, regime, jnp.asarray(table))


def local(driving_input, regime, reaction_rates):
    moments, nz, nx, lanes = driving_input.shape
    teams, nsx, nsy = (lax.axis_size(axis) for axis in ("tm", "sx", "sy"))
    one_aggregate = nx == AGGREGATE_XCELLS and lanes == teams * AGGREGATE_YCELLS
    tiled = nx == 8 and nz == 8 and nz % teams == 0 and lanes == 128
    if one_aggregate and tiled and teams * moments == 128 and moments % 8 == 0 and SWEEPS == 4:
        return local_fused(teams, nsx, nsy, driving_input, regime, reaction_rates)
    return local_general(driving_input, regime, reaction_rates)


def solution(mesh):
    placed = (P("tm", None, "sx", "sy"), P(None, "sx", "sy"), P())
    return jax.shard_map(
        local, mesh=mesh, in_specs=placed, out_specs=P("tm", None, "sx", "sy"), check_vma=False
    )
```

```python
import functools

import jax
import jax.numpy as jnp
import numpy as np
from jax import lax
from jax.experimental import pallas as pl
from jax.experimental.pallas import tpu as pltpu
from jax.sharding import PartitionSpec as P

AGGREGATE_XCELLS = 8
AGGREGATE_YCELLS = 32
SWEEPS = 4


TWO_PI = 2.0 * 3.141592653589793


def extended(block, sides, width):
    for axis, dim in sides:
        count = lax.axis_size(axis)
        forward = [(i, i + 1) for i in range(count - 1)]
        backward = [(target, source) for source, target in forward]
        low = lax.ppermute(
            lax.slice_in_dim(block, block.shape[dim] - width, None, axis=dim), axis, forward
        )
        high = lax.ppermute(lax.slice_in_dim(block, 0, width, axis=dim), axis, backward)
        block = jnp.concatenate([low, block, high], axis=dim)
    return block


def angle_table(row_index, col_index, cycle_duration):
    product = row_index[:, None] * col_index[None, :] % cycle_duration
    angles = product.astype(jnp.float32) * (TWO_PI / cycle_duration)
    return (jnp.cos(angles), jnp.sin(angles))


def matmul(left_side, right_side):
    return jnp.dot(
        left_side, right_side, precision=lax.Precision.HIGHEST, preferred_element_type=jnp.float32
    )


def complex_mul(left_real, left_imag, pair):
    return jnp.stack(
        [left_real * pair[0] - left_imag * pair[1], left_real * pair[1] + left_imag * pair[0]]
    )


def neighbors(present_guess):
    padded = extended(present_guess, (("sx", 3), ("sy", 4)), 1)
    running = padded[:, :, :, 2:, 1:-1] + padded[:, :, :, :-2, 1:-1]
    running = running + padded[:, :, :, 1:-1, 2:] + padded[:, :, :, 1:-1, :-2]
    running = running + jnp.roll(present_guess, 1, axis=2) + jnp.roll(present_guess, -1, axis=2)
    return running


def local_general(driving_input, regime, reaction_rates):
    moment_count, third_axis_count, first_axis_count, second_axis_count = driving_input.shape
    temporal_spacing = lax.axis_size("tm")
    sy_size = lax.axis_size("sy")
    cycle_duration = moment_count * temporal_spacing
    unknowns_in_tile = third_axis_count * first_axis_count * second_axis_count
    processor_lines = driving_input.reshape(moment_count, unknowns_in_tile)
    owned_slice_number = lax.axis_index("tm") * moment_count + jnp.arange(
        moment_count, dtype=jnp.int32
    )
    all_index = jnp.arange(cycle_duration, dtype=jnp.int32)
    cos_rows, sin_rows = angle_table(owned_slice_number, all_index, cycle_duration)

    def forward(running, segment, offset):
        return jnp.stack([matmul(cos_rows, segment), -matmul(sin_rows, segment)])

    eigen_spectra = forward(
        jnp.zeros((2, moment_count, unknowns_in_tile), jnp.float32),
        lax.all_gather(processor_lines, "tm", axis=0, tiled=True),
        jnp.int32(0),
    )
    source_term = eigen_spectra.reshape(
        2, moment_count, third_axis_count, first_axis_count, second_axis_count
    )
    phase_angle = owned_slice_number.astype(jnp.float32) * (TWO_PI / cycle_duration)
    shift_real = (1.0 - jnp.cos(phase_angle))[:, None, None, None]
    shift_imag = jnp.sin(phase_angle)[:, None, None, None]
    reaction = jnp.zeros(regime.shape, jnp.float32)
    for regime_no in range(reaction_rates.shape[0]):
        reaction = reaction + jnp.where(
            regime == regime_no, reaction_rates[regime_no], jnp.zeros((), jnp.float32)
        )
    diag_real = reaction[None] + 6.0 + shift_real
    diag_imag = jnp.zeros_like(diag_real) + shift_imag
    modulus = diag_real * diag_real + diag_imag * diag_imag
    inverse_real = diag_real / modulus
    inverse_imag = -diag_imag / modulus
    present_guess = complex_mul(inverse_real, inverse_imag, source_term)
    for sweep_no in range(SWEEPS - 1):
        present_guess = complex_mul(
            inverse_real, inverse_imag, source_term + neighbors(present_guess)
        )
    applied = complex_mul(diag_real, diag_imag, present_guess) - neighbors(present_guess)
    residual = source_term - applied
    first_axis_teams = first_axis_count // AGGREGATE_XCELLS
    second_axis_teams = second_axis_count // AGGREGATE_YCELLS
    per_device = first_axis_teams * second_axis_teams

    def aggregate(values):
        leading = values.shape[:-3]
        blocks = values.reshape(
            leading
            + (
                third_axis_count,
                first_axis_teams,
                AGGREGATE_XCELLS,
                second_axis_teams,
                AGGREGATE_YCELLS,
            )
        )
        return jnp.sum(blocks, axis=(-5, -3, -1)).reshape(leading + (per_device,))

    coarse_right = jnp.transpose(aggregate(residual), (1, 0, 2))
    rate_sums = aggregate(reaction)
    shift_column = 1.0 - jnp.cos(phase_angle)
    face_count = 2 * (AGGREGATE_YCELLS * third_axis_count + AGGREGATE_XCELLS * third_axis_count)
    volume = AGGREGATE_XCELLS * AGGREGATE_YCELLS * third_axis_count
    spatial = lax.axis_size("sx") * sy_size
    slot_count = -(-moment_count // spatial)
    padding_rows = slot_count * spatial - moment_count
    padded_right = jnp.pad(coarse_right, ((0, padding_rows), (0, 0), (0, 0)))
    sum_copies = jnp.broadcast_to(rate_sums[None, None, :], (spatial, 1, per_device))
    shared_right, shared_sums = (
        lax.all_to_all(padded_right, ("sx", "sy"), split_axis=0, concat_axis=2, tiled=True),
        lax.all_to_all(sum_copies, ("sx", "sy"), split_axis=0, concat_axis=2, tiled=True),
    )
    spatial_rank = lax.axis_index("sx") * sy_size + lax.axis_index("sy")
    padded_shift = jnp.pad(shift_column, (0, padding_rows))
    slot_shift = lax.dynamic_slice_in_dim(padded_shift, spatial_rank * slot_count, slot_count, 0)
    sum_values = shared_sums[0, 0]
    coarse_total = sum_values.shape[0]
    position = jnp.arange(coarse_total, dtype=jnp.int32)
    device = position // per_device
    within = position % per_device
    coarse_x = device // sy_size * first_axis_teams + within // second_axis_teams
    coarse_y = device % sy_size * second_axis_teams + within % second_axis_teams
    x_gap = jnp.abs(coarse_x[:, None] - coarse_x[None, :])
    y_gap = jnp.abs(coarse_y[:, None] - coarse_y[None, :])
    coupling = -(AGGREGATE_YCELLS * third_axis_count) * ((x_gap == 1) & (y_gap == 0)).astype(
        jnp.float32
    )
    coupling = coupling - AGGREGATE_XCELLS * third_axis_count * (
        (x_gap == 0) & (y_gap == 1)
    ).astype(jnp.float32)
    identity = (position[:, None] == position[None, :]).astype(jnp.float32)
    diagonal = sum_values + face_count
    system = (
        coupling[None]
        + identity[None] * (diagonal[None, :] + volume * slot_shift[:, None])[:, None, :]
    )
    factor = jnp.linalg.cholesky(system)
    right_side = jnp.transpose(shared_right, (0, 2, 1))
    forward_sub = lax.linalg.triangular_solve(factor, right_side, left_side=True, lower=True)
    coarse = lax.linalg.triangular_solve(
        factor, forward_sub, left_side=True, lower=True, transpose_a=True
    )
    solved = jnp.transpose(coarse, (0, 2, 1))
    returned = lax.all_to_all(solved, ("sx", "sy"), split_axis=2, concat_axis=0, tiled=True)
    own_coarse = returned[:moment_count]
    local_part = jnp.transpose(own_coarse, (1, 0, 2)).reshape(
        2, moment_count, 1, first_axis_teams, 1, second_axis_teams, 1
    )
    spread_values = jnp.broadcast_to(
        local_part,
        (
            2,
            moment_count,
            third_axis_count,
            first_axis_teams,
            AGGREGATE_XCELLS,
            second_axis_teams,
            AGGREGATE_YCELLS,
        ),
    )
    present_guess = present_guess + spread_values.reshape(
        2, moment_count, third_axis_count, first_axis_count, second_axis_count
    )
    unrolled_array = present_guess.reshape(2, moment_count, unknowns_in_tile)

    def backward(running, segment, offset):
        return matmul(cos_rows, segment[0]) - matmul(sin_rows, segment[1])

    result = (
        backward(
            jnp.zeros((moment_count, unknowns_in_tile), jnp.float32),
            lax.all_gather(unrolled_array, "tm", axis=1, tiled=True),
            jnp.int32(0),
        )
        / cycle_duration
    )
    return result.reshape(driving_input.shape)


def time_tables(count):
    half = count // 2
    lane = np.arange(count)
    frequency = np.where(lane <= half, lane, lane - half)
    imaginary = lane > half
    moment = np.arange(count)
    angle = 2.0 * np.pi * (moment[:, None] * frequency[None, :] % count) / count
    forward = np.where(imaginary[None, :], -np.sin(angle), np.cos(angle))
    weight = np.where((lane == 0) | (lane == half), 1.0, 2.0) / count
    theta = 2.0 * np.pi * frequency / count
    signed = np.where(lane % half == 0, 0.0, np.sin(theta)) * np.where(lane < half, 1.0, -1.0)
    shift = np.zeros((8, count))
    shift[0] = 1.0 - np.cos(theta)
    shift[1] = signed
    return np.concatenate([forward, forward * weight[None, :], shift]).astype(np.float32)


def fused_kernel(
    sizes,
    rates_ref,
    field_hbm,
    regime_hbm,
    table_hbm,
    out_ref,
    field_ref,
    regime_ref,
    table_ref,
    rate_tiles,
    coarse_tiles,
    solved_tiles,
    added_ref,
    layer_sums,
    iterate_0,
    iterate_1,
    iterate_2,
    iterate_3,
    lasts,
    x_edges,
    x_halos,
    y_edges,
    y_halos,
    load_sem,
    last_send,
    last_recv,
    rate_send,
    rate_recv,
    coarse_send,
    coarse_recv,
    halo_send,
    halo_recv,
):
    teams, nsx, nsy, moments, nz, nx, lanes, width = sizes
    total = teams * moments
    strips = lanes // width
    plane = nz * nx
    spatial = nsx * nsy
    devices = teams * spatial
    highest = lax.Precision.HIGHEST
    tm = lax.axis_index("tm")
    ix = lax.axis_index("sx")
    iy = lax.axis_index("sy")
    here = ix * nsy + iy
    me = tm * spatial + here

    loads = [
        pltpu.make_async_copy(regime_hbm, regime_ref, load_sem.at[0]),
        pltpu.make_async_copy(field_hbm, field_ref, load_sem.at[1]),
        pltpu.make_async_copy(table_hbm, table_ref, load_sem.at[2]),
    ]
    for load in loads:
        load.start()

    def place(rank):
        return {
            "tm": rank // spatial,
            "sx": (rank % spatial) // nsy,
            "sy": rank % nsy,
        }

    barrier = pltpu.get_barrier_semaphore()

    def greet(offset, carry):
        pl.semaphore_signal(
            barrier,
            inc=1,
            device_id=place((me + offset) % devices),
            device_id_type=pl.DeviceIdType.MESH,
        )
        return carry

    lax.fori_loop(1, devices, greet, 0)

    loads[0].wait()
    rates = jnp.zeros(regime_ref.shape, jnp.float32)
    regime = regime_ref[...]
    for number in range(rates_ref.shape[0]):
        rates = rates + jnp.where(regime == number, rates_ref[number], 0.0)
    rate_tiles[here] = jnp.sum(rates, axis=0)
    decay = 1.0 / (rates + 7.0)
    decay_block = jnp.ones_like(decay)
    power, left = decay, moments
    while left:
        if left & 1:
            decay_block = decay_block * power
        power = power * power
        left //= 2
    decay_round = jnp.ones_like(decay)
    for _ in range(teams):
        decay_round = decay_round * decay_block
    closing = 1.0 / (1.0 - decay_round)

    has = (ix > 0, ix < nsx - 1, iy > 0, iy < nsy - 1)
    neighbour = (
        {"tm": tm, "sx": (ix + nsx - 1) % nsx, "sy": iy},
        {"tm": tm, "sx": (ix + 1) % nsx, "sy": iy},
        {"tm": tm, "sx": ix, "sy": (iy + nsy - 1) % nsy},
        {"tm": tm, "sx": ix, "sy": (iy + 1) % nsy},
    )
    for number in range(3):
        for side in range(4):

            @pl.when(jnp.logical_not(has[side]))
            def _(halo=(x_halos if side < 2 else y_halos).at[number, side % 2]):
                halo[...] = jnp.zeros(halo.shape, jnp.float32)

    def halo_copies(number):
        copies = []
        for side in range(4):
            if side < 2:
                source = x_edges.at[number, side]
                target = x_halos.at[number, 1 - side]
            else:
                source = y_edges.at[number]
                target = y_halos.at[number, 3 - side]
            copies.append(
                pltpu.make_async_remote_copy(
                    src_ref=source,
                    dst_ref=target,
                    send_sem=halo_send.at[number * 4 + side],
                    recv_sem=halo_recv.at[number * 4 + (side ^ 1)],
                    device_id=neighbour[side],
                    device_id_type=pl.DeviceIdType.MESH,
                )
            )
        return copies

    def exchange_start(number):
        for side, copy in enumerate(halo_copies(number)):

            @pl.when(has[side])
            def _(copy=copy):
                copy.start()

    def exchange_wait(number):
        copies = halo_copies(number)
        for side in range(4):

            @pl.when(has[side])
            def _(side=side):
                copies[side].wait_send()
                copies[side ^ 1].wait_recv()

    def rate_copy(offset):
        peer = (here + offset) % spatial
        return pltpu.make_async_remote_copy(
            src_ref=rate_tiles.at[here],
            dst_ref=rate_tiles.at[here],
            send_sem=rate_send.at[offset],
            recv_sem=rate_recv.at[offset],
            device_id={"tm": tm, "sx": peer // nsy, "sy": peer % nsy},
            device_id_type=pl.DeviceIdType.MESH,
        )

    def last_copy(number, offset):
        return pltpu.make_async_remote_copy(
            src_ref=lasts.at[number, tm],
            dst_ref=lasts.at[number, tm],
            send_sem=last_send.at[number * teams + offset],
            recv_sem=last_recv.at[number * teams + offset],
            device_id={"tm": (tm + offset) % teams, "sx": ix, "sy": iy},
            device_id_type=pl.DeviceIdType.MESH,
        )

    iterates = (iterate_0, iterate_1, iterate_2, iterate_3)
    chunk = lanes // 2 // nz
    row_id = lax.broadcasted_iota(jnp.int32, (nx, lanes), 0)
    lane_id = lax.broadcasted_iota(jnp.int32, (nx, lanes), 1)
    first_row, last_row = row_id == 0, row_id == nx - 1
    first_lane, last_lane = lane_id == 0, lane_id == lanes - 1
    odd_lane = lane_id % 2 == 1
    pair = (lane_id + 1) % lanes // 2

    def recurrence(number):
        def body(block, state):
            if number:
                high = y_halos[number - 1, 1, block]
                low = pltpu.roll(y_halos[number - 1, 0, block], 2, 1)
                ends = jnp.where(odd_lane, low, high)
                old = iterates[number - 1]
            state = list(state)
            for inner in range(chunk):
                moment = block * chunk + inner
                if number:
                    cells = [old[moment, z] for z in range(nz)]
                for z in range(nz):
                    values = field_ref[moment, z]
                    if number:
                        here_cell = cells[z]
                        slot = inner * nz + z
                        turned = pltpu.roll(ends, (lanes - 2 * slot - 1) % lanes, 1)
                        row = moment * nz + z
                        low_row = x_halos[number - 1, 0, pl.ds(row, 1), :]
                        high_row = x_halos[number - 1, 1, pl.ds(row, 1), :]
                        values = values + cells[z - 1] + cells[(z + 1) % nz]
                        values = values + jnp.where(
                            first_row, low_row, pltpu.roll(here_cell, 1, 0)
                        )
                        values = values + jnp.where(
                            last_row, high_row, pltpu.roll(here_cell, nx - 1, 0)
                        )
                        values = values + jnp.where(
                            first_lane, turned, pltpu.roll(here_cell, 1, 1)
                        )
                        values = values + jnp.where(
                            last_lane, turned, pltpu.roll(here_cell, lanes - 1, 1)
                        )
                    state[z] = decay[z] * (values + state[z])
                    iterates[number][moment, z] = state[z]
            return tuple(state)

        start = tuple(jnp.zeros((nx, lanes), jnp.float32) for _ in range(nz))
        state = lax.fori_loop(0, moments // chunk, body, start)
        for z in range(nz):
            lasts[number, tm, z] = state[z]

    def history(number):
        value = lasts[number, tm]
        for offset in range(1, teams):
            value = lasts[number, (tm + offset) % teams] + decay_block * value
        return value * closing

    def complete(number, entry):
        def body(block, state):
            state = list(state)
            packed = jnp.zeros((nx, lanes), jnp.float32)
            for inner in range(chunk):
                moment = block * chunk + inner
                for z in range(nz):
                    state[z] = decay[z] * state[z]
                    values = iterates[number][moment, z] + state[z]
                    iterates[number][moment, z] = values
                    slot = inner * nz + z
                    packed = jnp.where(pair == slot, pltpu.roll(values, 2 * slot, 1), packed)
                    row = moment * nz + z
                    x_edges[number, 0, pl.ds(row, 1), :] = values[0:1]
                    x_edges[number, 1, pl.ds(row, 1), :] = values[nx - 1 : nx]
            y_edges[number, block] = packed
            return tuple(state)

        lax.fori_loop(0, moments // chunk, body, tuple(entry[z] for z in range(nz)))

    loads[1].wait()
    recurrence(0)
    pl.semaphore_wait(barrier, devices - 1)
    for offset in range(1, teams):
        last_copy(0, offset).start()
    for offset in range(1, spatial):
        rate_copy(offset).start()
    for offset in range(1, teams):
        last_copy(0, offset).wait()
    complete(0, history(0))
    exchange_start(0)

    for offset in range(1, spatial):
        rate_copy(offset).wait()
    loads[2].wait()
    shift_real = table_ref[2 * total : 2 * total + 1, :]
    ncy = nsy * strips
    strip_block = lax.broadcasted_iota(jnp.int32, (nx, lanes), 1) // width
    faces = 2 * (width * nz + nx * nz)
    couple_x = -float(width * nz)
    couple_y = -float(nx * nz)
    unknowns = ncy * nsx
    band = [[None] * (nsx + 1) for _ in range(unknowns)]
    for gy in range(ncy):
        for gx in range(nsx):
            number = gy * nsx + gx
            tile = rate_tiles[gx * nsy + gy // strips]
            amount = jnp.sum(jnp.where(strip_block == gy % strips, tile, 0.0), axis=0, keepdims=True)
            amount = jnp.sum(amount, axis=1, keepdims=True)
            band[number][0] = amount + faces + float(nx * width * nz) * shift_real
            if gx + 1 < nsx:
                band[number][1] = jnp.full((1, total), couple_x, jnp.float32)
            if gy + 1 < ncy:
                extra = jnp.full((1, total), couple_y, jnp.float32)
                before = band[number][nsx]
                band[number][nsx] = extra if before is None else before + extra
    inverses = []
    ratios = []
    for i in range(unknowns):
        inverse = 1.0 / band[i][0]
        inverses.append(inverse)
        ratios.append([None] * (nsx + 1))
        for a in range(1, nsx + 1):
            if band[i][a] is None or i + a >= unknowns:
                continue
            ratio = band[i][a] * inverse
            ratios[i][a] = ratio
            for b in range(a, nsx + 1):
                if band[i][b] is None or i + b >= unknowns:
                    continue
                term = ratio * band[i][b]
                before = band[i + a][b - a]
                band[i + a][b - a] = -term if before is None else before - term


    exchange_wait(0)
    for number in range(1, 4):
        recurrence(number)
        for offset in range(1, teams):
            last_copy(number, offset).start()
        for offset in range(1, teams):
            last_copy(number, offset).wait()
        if number < 3:
            complete(number, history(number))
            exchange_start(number)
            exchange_wait(number)

    entry = history(3)

    def finish(moment, state):
        state = list(state)
        layer = jnp.zeros((nx, lanes), jnp.float32)
        for z in range(nz):
            state[z] = decay[z] * state[z]
            values = iterate_3[moment, z] + state[z]
            iterate_3[moment, z] = values
            layer = layer + (values - iterate_2[moment, z])
        layer_sums[pl.ds(pl.multiple_of(moment * nx, nx), nx), :] = layer
        return tuple(state)

    lax.fori_loop(0, moments, finish, tuple(entry[z] for z in range(nz)), unroll=4)
    by_row = [layer_sums[pl.ds(x, moments, stride=nx), :] for x in range(nx)]
    columns = sum(by_row[1:], by_row[0])
    moment_lane = lax.broadcasted_iota(jnp.int32, (moments, lanes), 1)
    balance = 4.0 * columns - by_row[0] - by_row[nx - 1]
    balance = balance + jnp.where(moment_lane > 0, pltpu.roll(columns, 1, 1), 0.0)
    balance = balance + jnp.where(
        moment_lane < lanes - 1, pltpu.roll(columns, lanes - 1, 1), 0.0
    )
    stacked = jnp.concatenate([balance, by_row[0], by_row[nx - 1], columns], axis=0)
    member = (lane_id // width == row_id).astype(jnp.float32)
    ends = jnp.where(
        row_id == 0, first_lane.astype(jnp.float32), last_lane.astype(jnp.float32)
    )
    ends = jnp.where(row_id < 2, ends, 0.0)

    def against(left_side, right_side):
        return lax.dot_general(
            left_side,
            right_side,
            (((1,), (1,)), ((), ())),
            precision=highest,
            preferred_element_type=jnp.float32,
        )

    coarse_tiles[me] = jnp.where(
        lane_id < 3 * moments, against(member, stacked), against(ends, stacked)
    )

    def coarse_copy(offset):
        return pltpu.make_async_remote_copy(
            src_ref=coarse_tiles.at[me],
            dst_ref=coarse_tiles.at[me],
            send_sem=coarse_send.at[offset],
            recv_sem=coarse_recv.at[offset],
            device_id=place((me + offset) % devices),
            device_id_type=pl.DeviceIdType.MESH,
        )

    def coarse_start(offset, carry):
        coarse_copy(offset).start()
        return carry

    def coarse_wait(offset, carry):
        coarse_copy(offset).wait()
        return carry

    lax.fori_loop(1, devices, coarse_start, 0)
    lax.fori_loop(1, devices, coarse_wait, 0)

    kinds = [[None] * spatial for _ in range(4)]
    quarter = lane_id // moments
    for slot in range(spatial):
        for kind in range(4):
            merged = None
            for team in range(teams):
                tile = coarse_tiles[team * spatial + slot]
                turn = (moments * (team - kind)) % lanes
                turned = pltpu.roll(tile, turn, 1) if turn else tile
                merged = turned if team == 0 else jnp.where(quarter == team, turned, merged)
            kinds[kind][slot] = merged
    tiles = []
    for gx in range(nsx):
        for gy in range(nsy):
            slot = gx * nsy + gy
            tile = kinds[0][slot]
            if gx + 1 < nsx:
                tile = tile + kinds[1][slot + nsy]
            if gx > 0:
                tile = tile + kinds[2][slot - nsy]
            if gy > 0:
                tile = tile + jnp.where(row_id == 0, kinds[3][slot - 1][1:2], 0.0)
            if gy + 1 < nsy:
                tile = tile + jnp.where(row_id == strips - 1, kinds[3][slot + 1][0:1], 0.0)
            tiles.append(tile)
    spectrum = jnp.dot(
        jnp.concatenate(tiles, axis=0),
        table_ref[0:total, :],
        precision=highest,
        preferred_element_type=jnp.float32,
    )
    right = []
    for gy in range(ncy):
        for gx in range(nsx):
            row = (gx * nsy + gy // strips) * nx + gy % strips
            right.append(spectrum[row : row + 1])
    for i in range(unknowns):
        for a in range(1, nsx + 1):
            if ratios[i][a] is not None:
                right[i + a] = right[i + a] - ratios[i][a] * right[i]
    for i in reversed(range(unknowns)):
        value = right[i] * inverses[i]
        for a in range(1, nsx + 1):
            if ratios[i][a] is not None:
                value = value - ratios[i][a] * right[i + a]
        right[i] = value
    for gx in range(nsx):
        for block in range(nsy):
            for d in range(strips):
                number = (block * strips + d) * nsx + gx
                solved_tiles[gx * nsy + block, d : d + 1, :] = right[number]
    own_rows = solved_tiles[here]
    spread = jnp.concatenate(
        [jnp.broadcast_to(own_rows[d : d + 1], (width, total)) for d in range(strips)], axis=0
    )
    own_moments = pl.ds(pl.multiple_of(total + tm * moments, moments), moments)
    added_ref[...] = against(table_ref[own_moments, :], spread)

    def write(moment, carry):
        added = added_ref[pl.ds(moment, 1), :]
        for z in range(nz):
            out_ref[moment, z] = iterate_3[moment, z] + added
        return carry

    lax.fori_loop(0, moments, write, 0, unroll=4)


def local_fused(teams, nsx, nsy, driving_input, regime, reaction_rates):
    moments, nz, nx, lanes = driving_input.shape
    width = AGGREGATE_YCELLS
    total = teams * moments
    table = time_tables(total)
    sizes = (teams, nsx, nsy, moments, nz, nx, lanes, width)
    devices = teams * nsx * nsy
    blocks = 2 * moments * nz // lanes
    f32 = jnp.float32
    whole = pltpu.VMEM(driving_input.shape, f32)
    in_hbm = pl.BlockSpec(memory_space=pltpu.HBM)
    dma = pltpu.SemaphoreType.DMA
    return pl.pallas_call(
        functools.partial(fused_kernel, sizes),
        out_shape=jax.ShapeDtypeStruct(driving_input.shape, f32),
        in_specs=[pl.BlockSpec(memory_space=pltpu.SMEM)] + [in_hbm] * 3,
        out_specs=pl.BlockSpec(memory_space=pltpu.VMEM),
        scratch_shapes=[
            whole,
            pltpu.VMEM(regime.shape, jnp.int32),
            pltpu.VMEM(table.shape, f32),
            pltpu.VMEM((nsx * nsy, nx, lanes), f32),
            pltpu.VMEM((devices, 8, total), f32),
            pltpu.VMEM((nsx * nsy, max(lanes // width, 8), total), f32),
            pltpu.VMEM((moments, lanes), f32),
            pltpu.VMEM((moments * nx, lanes), f32),
            whole,
            whole,
            whole,
            whole,
            pltpu.VMEM((4, teams, nz, nx, lanes), f32),
            pltpu.VMEM((3, 2, moments * nz, lanes), f32),
            pltpu.VMEM((3, 2, moments * nz, lanes), f32),
            pltpu.VMEM((3, blocks, nx, lanes), f32),
            pltpu.VMEM((3, 2, blocks, nx, lanes), f32),
            dma((3,)),
            dma((4 * teams,)),
            dma((4 * teams,)),
            dma((nsx * nsy,)),
            dma((nsx * nsy,)),
            dma((devices,)),
            dma((devices,)),
            dma((12,)),
            dma((12,)),
        ],
        compiler_params=pltpu.CompilerParams(
            collective_id=0, has_side_effects=True, vmem_limit_bytes=32 * 1024 * 1024
        ),
    )(reaction_rates, driving_input, regime, jnp.asarray(table))


def local(driving_input, regime, reaction_rates):
    moments, nz, nx, lanes = driving_input.shape
    teams, nsx, nsy = (lax.axis_size(axis) for axis in ("tm", "sx", "sy"))
    strips = lanes // AGGREGATE_YCELLS
    whole_strips = nx == AGGREGATE_XCELLS and strips * AGGREGATE_YCELLS == lanes and strips <= 8
    tiled = nx == 8 and nz == 8 and lanes == 128 and moments % 8 == 0
    if whole_strips and tiled and teams * moments == 128 and 4 * moments == 128 and SWEEPS == 4:
        return local_fused(teams, nsx, nsy, driving_input, regime, reaction_rates)
    return local_general(driving_input, regime, reaction_rates)


def solution(mesh):
    placed = (P("tm", None, "sx", "sy"), P(None, "sx", "sy"), P())
    return jax.shard_map(
        local, mesh=mesh, in_specs=placed, out_specs=P("tm", None, "sx", "sy"), check_vma=False
    )
```

```python
import functools

import jax
import jax.numpy as jnp
import numpy as np
from jax import lax
from jax.experimental import pallas as pl
from jax.experimental.pallas import tpu as pltpu
from jax.sharding import PartitionSpec as P

AGGREGATE_XCELLS = 8
AGGREGATE_YCELLS = 32
SWEEPS = 4


TWO_PI = 2.0 * 3.141592653589793


def extended(block, sides, width):
    for axis, dim in sides:
        count = lax.axis_size(axis)
        forward = [(i, i + 1) for i in range(count - 1)]
        backward = [(target, source) for source, target in forward]
        low = lax.ppermute(
            lax.slice_in_dim(block, block.shape[dim] - width, None, axis=dim), axis, forward
        )
        high = lax.ppermute(lax.slice_in_dim(block, 0, width, axis=dim), axis, backward)
        block = jnp.concatenate([low, block, high], axis=dim)
    return block


def angle_table(row_index, col_index, cycle_duration):
    product = row_index[:, None] * col_index[None, :] % cycle_duration
    angles = product.astype(jnp.float32) * (TWO_PI / cycle_duration)
    return (jnp.cos(angles), jnp.sin(angles))


def matmul(left_side, right_side):
    return jnp.dot(
        left_side, right_side, precision=lax.Precision.HIGHEST, preferred_element_type=jnp.float32
    )


def complex_mul(left_real, left_imag, pair):
    return jnp.stack(
        [left_real * pair[0] - left_imag * pair[1], left_real * pair[1] + left_imag * pair[0]]
    )


def neighbors(present_guess):
    padded = extended(present_guess, (("sx", 3), ("sy", 4)), 1)
    running = padded[:, :, :, 2:, 1:-1] + padded[:, :, :, :-2, 1:-1]
    running = running + padded[:, :, :, 1:-1, 2:] + padded[:, :, :, 1:-1, :-2]
    running = running + jnp.roll(present_guess, 1, axis=2) + jnp.roll(present_guess, -1, axis=2)
    return running


def local_general(driving_input, regime, reaction_rates):
    moment_count, third_axis_count, first_axis_count, second_axis_count = driving_input.shape
    temporal_spacing = lax.axis_size("tm")
    sy_size = lax.axis_size("sy")
    cycle_duration = moment_count * temporal_spacing
    unknowns_in_tile = third_axis_count * first_axis_count * second_axis_count
    processor_lines = driving_input.reshape(moment_count, unknowns_in_tile)
    owned_slice_number = lax.axis_index("tm") * moment_count + jnp.arange(
        moment_count, dtype=jnp.int32
    )
    all_index = jnp.arange(cycle_duration, dtype=jnp.int32)
    cos_rows, sin_rows = angle_table(owned_slice_number, all_index, cycle_duration)

    def forward(running, segment, offset):
        return jnp.stack([matmul(cos_rows, segment), -matmul(sin_rows, segment)])

    eigen_spectra = forward(
        jnp.zeros((2, moment_count, unknowns_in_tile), jnp.float32),
        lax.all_gather(processor_lines, "tm", axis=0, tiled=True),
        jnp.int32(0),
    )
    source_term = eigen_spectra.reshape(
        2, moment_count, third_axis_count, first_axis_count, second_axis_count
    )
    phase_angle = owned_slice_number.astype(jnp.float32) * (TWO_PI / cycle_duration)
    shift_real = (1.0 - jnp.cos(phase_angle))[:, None, None, None]
    shift_imag = jnp.sin(phase_angle)[:, None, None, None]
    reaction = jnp.zeros(regime.shape, jnp.float32)
    for regime_no in range(reaction_rates.shape[0]):
        reaction = reaction + jnp.where(
            regime == regime_no, reaction_rates[regime_no], jnp.zeros((), jnp.float32)
        )
    diag_real = reaction[None] + 6.0 + shift_real
    diag_imag = jnp.zeros_like(diag_real) + shift_imag
    modulus = diag_real * diag_real + diag_imag * diag_imag
    inverse_real = diag_real / modulus
    inverse_imag = -diag_imag / modulus
    present_guess = complex_mul(inverse_real, inverse_imag, source_term)
    for sweep_no in range(SWEEPS - 1):
        present_guess = complex_mul(
            inverse_real, inverse_imag, source_term + neighbors(present_guess)
        )
    applied = complex_mul(diag_real, diag_imag, present_guess) - neighbors(present_guess)
    residual = source_term - applied
    first_axis_teams = first_axis_count // AGGREGATE_XCELLS
    second_axis_teams = second_axis_count // AGGREGATE_YCELLS
    per_device = first_axis_teams * second_axis_teams

    def aggregate(values):
        leading = values.shape[:-3]
        blocks = values.reshape(
            leading
            + (
                third_axis_count,
                first_axis_teams,
                AGGREGATE_XCELLS,
                second_axis_teams,
                AGGREGATE_YCELLS,
            )
        )
        return jnp.sum(blocks, axis=(-5, -3, -1)).reshape(leading + (per_device,))

    coarse_right = jnp.transpose(aggregate(residual), (1, 0, 2))
    rate_sums = aggregate(reaction)
    shift_column = 1.0 - jnp.cos(phase_angle)
    face_count = 2 * (AGGREGATE_YCELLS * third_axis_count + AGGREGATE_XCELLS * third_axis_count)
    volume = AGGREGATE_XCELLS * AGGREGATE_YCELLS * third_axis_count
    spatial = lax.axis_size("sx") * sy_size
    slot_count = -(-moment_count // spatial)
    padding_rows = slot_count * spatial - moment_count
    padded_right = jnp.pad(coarse_right, ((0, padding_rows), (0, 0), (0, 0)))
    sum_copies = jnp.broadcast_to(rate_sums[None, None, :], (spatial, 1, per_device))
    shared_right, shared_sums = (
        lax.all_to_all(padded_right, ("sx", "sy"), split_axis=0, concat_axis=2, tiled=True),
        lax.all_to_all(sum_copies, ("sx", "sy"), split_axis=0, concat_axis=2, tiled=True),
    )
    spatial_rank = lax.axis_index("sx") * sy_size + lax.axis_index("sy")
    padded_shift = jnp.pad(shift_column, (0, padding_rows))
    slot_shift = lax.dynamic_slice_in_dim(padded_shift, spatial_rank * slot_count, slot_count, 0)
    sum_values = shared_sums[0, 0]
    coarse_total = sum_values.shape[0]
    position = jnp.arange(coarse_total, dtype=jnp.int32)
    device = position // per_device
    within = position % per_device
    coarse_x = device // sy_size * first_axis_teams + within // second_axis_teams
    coarse_y = device % sy_size * second_axis_teams + within % second_axis_teams
    x_gap = jnp.abs(coarse_x[:, None] - coarse_x[None, :])
    y_gap = jnp.abs(coarse_y[:, None] - coarse_y[None, :])
    coupling = -(AGGREGATE_YCELLS * third_axis_count) * ((x_gap == 1) & (y_gap == 0)).astype(
        jnp.float32
    )
    coupling = coupling - AGGREGATE_XCELLS * third_axis_count * (
        (x_gap == 0) & (y_gap == 1)
    ).astype(jnp.float32)
    identity = (position[:, None] == position[None, :]).astype(jnp.float32)
    diagonal = sum_values + face_count
    system = (
        coupling[None]
        + identity[None] * (diagonal[None, :] + volume * slot_shift[:, None])[:, None, :]
    )
    factor = jnp.linalg.cholesky(system)
    right_side = jnp.transpose(shared_right, (0, 2, 1))
    forward_sub = lax.linalg.triangular_solve(factor, right_side, left_side=True, lower=True)
    coarse = lax.linalg.triangular_solve(
        factor, forward_sub, left_side=True, lower=True, transpose_a=True
    )
    solved = jnp.transpose(coarse, (0, 2, 1))
    returned = lax.all_to_all(solved, ("sx", "sy"), split_axis=2, concat_axis=0, tiled=True)
    own_coarse = returned[:moment_count]
    local_part = jnp.transpose(own_coarse, (1, 0, 2)).reshape(
        2, moment_count, 1, first_axis_teams, 1, second_axis_teams, 1
    )
    spread_values = jnp.broadcast_to(
        local_part,
        (
            2,
            moment_count,
            third_axis_count,
            first_axis_teams,
            AGGREGATE_XCELLS,
            second_axis_teams,
            AGGREGATE_YCELLS,
        ),
    )
    present_guess = present_guess + spread_values.reshape(
        2, moment_count, third_axis_count, first_axis_count, second_axis_count
    )
    unrolled_array = present_guess.reshape(2, moment_count, unknowns_in_tile)

    def backward(running, segment, offset):
        return matmul(cos_rows, segment[0]) - matmul(sin_rows, segment[1])

    result = (
        backward(
            jnp.zeros((moment_count, unknowns_in_tile), jnp.float32),
            lax.all_gather(unrolled_array, "tm", axis=1, tiled=True),
            jnp.int32(0),
        )
        / cycle_duration
    )
    return result.reshape(driving_input.shape)


def time_tables(count):
    half = count // 2
    lane = np.arange(count)
    frequency = np.where(lane <= half, lane, lane - half)
    imaginary = lane > half
    moment = np.arange(count)
    angle = 2.0 * np.pi * (moment[:, None] * frequency[None, :] % count) / count
    forward = np.where(imaginary[None, :], -np.sin(angle), np.cos(angle))
    weight = np.where((lane == 0) | (lane == half), 1.0, 2.0) / count
    theta = 2.0 * np.pi * frequency / count
    signed = np.where(lane % half == 0, 0.0, np.sin(theta)) * np.where(lane < half, 1.0, -1.0)
    shift = np.zeros((8, count))
    shift[0] = 1.0 - np.cos(theta)
    shift[1] = signed
    return np.concatenate([forward, forward * weight[None, :], shift]).astype(np.float32)


def fused_kernel(
    sizes,
    rates_ref,
    field_hbm,
    regime_hbm,
    table_hbm,
    out_ref,
    field_ref,
    regime_ref,
    table_ref,
    rate_tiles,
    coarse_tiles,
    solved_tiles,
    added_ref,
    layer_sums,
    iterate_0,
    iterate_1,
    iterate_2,
    iterate_3,
    lasts,
    x_edges,
    x_halos,
    y_edges,
    y_halos,
    y_ends,
    x_lasts,
    y_lasts,
    x_edge_decay,
    x_halo_decay,
    y_edge_decay,
    y_halo_decay,
    load_sem,
    last_send,
    last_recv,
    rate_send,
    rate_recv,
    coarse_send,
    coarse_recv,
    halo_send,
    halo_recv,
    diagonal_send,
    diagonal_recv,
    decay_send,
    decay_recv,
):
    teams, nsx, nsy, moments, nz, nx, lanes, width = sizes
    total = teams * moments
    strips = lanes // width
    plane = nz * nx
    spatial = nsx * nsy
    devices = teams * spatial
    highest = lax.Precision.HIGHEST
    tm = lax.axis_index("tm")
    ix = lax.axis_index("sx")
    iy = lax.axis_index("sy")
    here = ix * nsy + iy
    me = tm * spatial + here

    loads = [
        pltpu.make_async_copy(regime_hbm, regime_ref, load_sem.at[0]),
        pltpu.make_async_copy(field_hbm, field_ref, load_sem.at[1]),
        pltpu.make_async_copy(table_hbm, table_ref, load_sem.at[2]),
    ]
    for load in loads:
        load.start()

    def place(rank):
        return {
            "tm": rank // spatial,
            "sx": (rank % spatial) // nsy,
            "sy": rank % nsy,
        }

    barrier = pltpu.get_barrier_semaphore()

    def greet(offset, carry):
        pl.semaphore_signal(
            barrier,
            inc=1,
            device_id=place((me + offset) % devices),
            device_id_type=pl.DeviceIdType.MESH,
        )
        return carry

    lax.fori_loop(1, devices, greet, 0)

    loads[0].wait()
    rates = jnp.zeros(regime_ref.shape, jnp.float32)
    regime = regime_ref[...]
    for number in range(rates_ref.shape[0]):
        rates = rates + jnp.where(regime == number, rates_ref[number], 0.0)
    rate_tiles[here] = jnp.sum(rates, axis=0)
    decay = 1.0 / (rates + 7.0)

    def raised(value, exponent):
        result = jnp.ones_like(value)
        while exponent:
            if exponent & 1:
                result = result * value
            value = value * value
            exponent //= 2
        return result

    def history(decay_of, part):
        decay_block = raised(decay_of, moments)
        value = part(0)
        for offset in range(1, teams):
            value = part(offset) + decay_block * value
        return value / (1.0 - raised(decay_block, teams))

    has = (ix > 0, ix < nsx - 1, iy > 0, iy < nsy - 1)
    neighbour = (
        {"tm": tm, "sx": (ix + nsx - 1) % nsx, "sy": iy},
        {"tm": tm, "sx": (ix + 1) % nsx, "sy": iy},
        {"tm": tm, "sx": ix, "sy": (iy + nsy - 1) % nsy},
        {"tm": tm, "sx": ix, "sy": (iy + 1) % nsy},
    )
    for number in range(3):
        for side in range(4):

            @pl.when(jnp.logical_not(has[side]))
            def _(halo=(x_halos if side < 2 else y_halos).at[number, side % 2]):
                halo[...] = jnp.zeros(halo.shape, jnp.float32)

    for side in (2, 3):

        @pl.when(jnp.logical_not(has[side]))
        def _(side=side):
            y_halo_decay[side % 2] = jnp.zeros((nx, lanes), jnp.float32)
            for number in range(3):
                y_lasts[number, side % 2] = jnp.zeros((teams, nx, lanes), jnp.float32)

    def halo_copies(number):
        copies = []
        for side in range(4):
            if side < 2:
                source = x_edges.at[number, side]
                target = x_halos.at[number, 1 - side]
            else:
                source = y_edges.at[number]
                target = y_halos.at[number, 3 - side]
            copies.append(
                pltpu.make_async_remote_copy(
                    src_ref=source,
                    dst_ref=target,
                    send_sem=halo_send.at[number * 4 + side],
                    recv_sem=halo_recv.at[number * 4 + (side ^ 1)],
                    device_id=neighbour[side],
                    device_id_type=pl.DeviceIdType.MESH,
                )
            )
        return copies

    def decay_copies():
        copies = []
        for side in range(4):
            if side < 2:
                source = x_edge_decay.at[side]
                target = x_halo_decay.at[1 - side]
            else:
                source = y_edge_decay
                target = y_halo_decay.at[3 - side]
            copies.append(
                pltpu.make_async_remote_copy(
                    src_ref=source,
                    dst_ref=target,
                    send_sem=decay_send.at[side],
                    recv_sem=decay_recv.at[side ^ 1],
                    device_id=neighbour[side],
                    device_id_type=pl.DeviceIdType.MESH,
                )
            )
        return copies

    def diagonal_copies(number, offset):
        copies = []
        for side in range(4):
            if side < 2:
                source = x_edges.at[number, side, pl.ds((moments - 1) * nz, nz)]
                target = x_lasts.at[number, 1 - side, tm]
            else:
                source = y_edges.at[number, moments // chunk - 1]
                target = y_lasts.at[number, 3 - side, tm]
            copies.append(
                pltpu.make_async_remote_copy(
                    src_ref=source,
                    dst_ref=target,
                    send_sem=diagonal_send.at[(number * 4 + side) * teams + offset],
                    recv_sem=diagonal_recv.at[(number * 4 + (side ^ 1)) * teams + offset],
                    device_id={**neighbour[side], "tm": (tm + offset) % teams},
                    device_id_type=pl.DeviceIdType.MESH,
                )
            )
        return copies

    def start_all(copies):
        for side, copy in enumerate(copies):

            @pl.when(has[side])
            def _(copy=copy):
                copy.start()

    def wait_all(copies):
        for side in range(4):

            @pl.when(has[side])
            def _(side=side):
                copies[side].wait_send()
                copies[side ^ 1].wait_recv()

    def rate_copy(offset):
        peer = (here + offset) % spatial
        return pltpu.make_async_remote_copy(
            src_ref=rate_tiles.at[here],
            dst_ref=rate_tiles.at[here],
            send_sem=rate_send.at[offset],
            recv_sem=rate_recv.at[offset],
            device_id={"tm": tm, "sx": peer // nsy, "sy": peer % nsy},
            device_id_type=pl.DeviceIdType.MESH,
        )

    def last_copy(number, offset):
        return pltpu.make_async_remote_copy(
            src_ref=lasts.at[number, tm],
            dst_ref=lasts.at[number, tm],
            send_sem=last_send.at[number * teams + offset],
            recv_sem=last_recv.at[number * teams + offset],
            device_id={"tm": (tm + offset) % teams, "sx": ix, "sy": iy},
            device_id_type=pl.DeviceIdType.MESH,
        )

    iterates = (iterate_0, iterate_1, iterate_2, iterate_3)
    chunk = lanes // 2 // nz
    row_id = lax.broadcasted_iota(jnp.int32, (nx, lanes), 0)
    lane_id = lax.broadcasted_iota(jnp.int32, (nx, lanes), 1)
    first_row, last_row = row_id == 0, row_id == nx - 1
    first_lane, last_lane = lane_id == 0, lane_id == lanes - 1
    odd_lane = lane_id % 2 == 1
    pair = (lane_id + 1) % lanes // 2

    def recurrence(number):
        def body(block, state):
            if number:
                ends = y_ends[block]
                old = iterates[number - 1]
            state = list(state)
            packed = jnp.zeros((nx, lanes), jnp.float32)
            for inner in range(chunk):
                moment = block * chunk + inner
                if number:
                    cells = [old[moment, z] for z in range(nz)]
                for z in range(nz):
                    values = field_ref[moment, z]
                    slot = inner * nz + z
                    row = moment * nz + z
                    if number:
                        here_cell = cells[z]
                        turned = pltpu.roll(ends, (lanes - 2 * slot - 1) % lanes, 1)
                        low_row = x_halos[number - 1, 0, pl.ds(row, 1), :]
                        high_row = x_halos[number - 1, 1, pl.ds(row, 1), :]
                        values = values + cells[z - 1] + cells[(z + 1) % nz]
                        values = values + jnp.where(
                            first_row, low_row, pltpu.roll(here_cell, 1, 0)
                        )
                        values = values + jnp.where(
                            last_row, high_row, pltpu.roll(here_cell, nx - 1, 0)
                        )
                        values = values + jnp.where(
                            first_lane, turned, pltpu.roll(here_cell, 1, 1)
                        )
                        values = values + jnp.where(
                            last_lane, turned, pltpu.roll(here_cell, lanes - 1, 1)
                        )
                    state[z] = decay[z] * (values + state[z])
                    iterates[number][moment, z] = state[z]
                    if number < 3:
                        packed = jnp.where(
                            pair == slot, pltpu.roll(state[z], 2 * slot, 1), packed
                        )
                        x_edges[number, 0, pl.ds(row, 1), :] = state[z][0:1]
                        x_edges[number, 1, pl.ds(row, 1), :] = state[z][nx - 1 : nx]
            if number < 3:
                y_edges[number, block] = packed
            return tuple(state)

        start = tuple(jnp.zeros((nx, lanes), jnp.float32) for _ in range(nz))
        state = lax.fori_loop(0, moments // chunk, body, start)
        for z in range(nz):
            lasts[number, tm, z] = state[z]

    def own_history(number):
        return history(decay, lambda offset: lasts[number, (tm + offset) % teams])

    def complete(number):
        entry = own_history(number)

        def body(moment, state):
            state = list(state)
            for z in range(nz):
                state[z] = decay[z] * state[z]
                iterates[number][moment, z] = iterates[number][moment, z] + state[z]
            return tuple(state)

        lax.fori_loop(0, moments, body, tuple(entry[z] for z in range(nz)), unroll=4)

    def merge(low, high):
        return jnp.where(odd_lane, pltpu.roll(low, 2, 1), high)

    def repeat(values):
        values = jnp.where(lane_id // (2 * nz) == chunk - 1, values, 0.0)
        turn = 2 * nz
        while turn < lanes:
            values = values + pltpu.roll(values, turn, 1)
            turn *= 2
        return values

    def correct_halos(number):
        for side in range(2):

            @pl.when(has[side])
            def _(side=side):
                decay_of = x_halo_decay[side]

                def part(offset):
                    if offset == 0:
                        return x_halos[number, side, pl.ds((moments - 1) * nz, nz), :]
                    return x_lasts[number, side, (tm + offset) % teams]

                def body(moment, state):
                    state = decay_of * state
                    at = pl.ds(pl.multiple_of(moment * nz, nz), nz)
                    x_halos[number, side, at, :] = x_halos[number, side, at, :] + state
                    return state

                lax.fori_loop(0, moments, body, history(decay_of, part), unroll=8)

        final = moments // chunk - 1
        decay_of = repeat(merge(y_halo_decay[0], y_halo_decay[1]))

        def part(offset):
            if offset == 0:
                return merge(y_halos[number, 0, final], y_halos[number, 1, final])
            team = (tm + offset) % teams
            return merge(y_lasts[number, 0, team], y_lasts[number, 1, team])

        entry = repeat(history(decay_of, part))
        power = decay_of
        for inner in range(1, chunk):
            power = jnp.where(lane_id // (2 * nz) >= inner, power * decay_of, power)
        state = power * entry
        for block in range(moments // chunk):
            y_ends[block] = merge(y_halos[number, 0, block], y_halos[number, 1, block]) + state
            state = state * raised(decay_of, chunk)

    def send(number):
        start_all(halo_copies(number))
        for offset in range(1, teams):
            last_copy(number, offset).start()
        for offset in range(1, teams):
            start_all(diagonal_copies(number, offset))

    def receive_lasts(number):
        for offset in range(1, teams):
            last_copy(number, offset).wait()

    def receive_halos(number):
        wait_all(halo_copies(number))
        for offset in range(1, teams):
            wait_all(diagonal_copies(number, offset))
        correct_halos(number)

    packed_decay = jnp.zeros((nx, lanes), jnp.float32)
    for z in range(nz):
        x_edge_decay[0, z : z + 1, :] = decay[z, 0:1]
        x_edge_decay[1, z : z + 1, :] = decay[z, nx - 1 : nx]
        slot = (chunk - 1) * nz + z
        packed_decay = jnp.where(
            pair == slot, pltpu.roll(decay[z], 2 * slot, 1), packed_decay
        )
    y_edge_decay[...] = packed_decay
    loads[1].wait()
    recurrence(0)
    pl.semaphore_wait(barrier, devices - 1)
    send(0)
    start_all(decay_copies())
    for offset in range(1, spatial):
        rate_copy(offset).start()
    receive_lasts(0)
    complete(0)
    for offset in range(1, spatial):
        rate_copy(offset).wait()
    loads[2].wait()
    shift_real = table_ref[2 * total : 2 * total + 1, :]
    ncy = nsy * strips
    strip_block = lax.broadcasted_iota(jnp.int32, (nx, lanes), 1) // width
    faces = 2 * (width * nz + nx * nz)
    couple_x = -float(width * nz)
    couple_y = -float(nx * nz)
    unknowns = ncy * nsx
    band = [[None] * (nsx + 1) for _ in range(unknowns)]
    for gy in range(ncy):
        for gx in range(nsx):
            number = gy * nsx + gx
            tile = rate_tiles[gx * nsy + gy // strips]
            amount = jnp.sum(jnp.where(strip_block == gy % strips, tile, 0.0), axis=0, keepdims=True)
            amount = jnp.sum(amount, axis=1, keepdims=True)
            band[number][0] = amount + faces + float(nx * width * nz) * shift_real
            if gx + 1 < nsx:
                band[number][1] = jnp.full((1, total), couple_x, jnp.float32)
            if gy + 1 < ncy:
                extra = jnp.full((1, total), couple_y, jnp.float32)
                before = band[number][nsx]
                band[number][nsx] = extra if before is None else before + extra
    inverses = []
    ratios = []
    for i in range(unknowns):
        inverse = 1.0 / band[i][0]
        inverses.append(inverse)
        ratios.append([None] * (nsx + 1))
        for a in range(1, nsx + 1):
            if band[i][a] is None or i + a >= unknowns:
                continue
            ratio = band[i][a] * inverse
            ratios[i][a] = ratio
            for b in range(a, nsx + 1):
                if band[i][b] is None or i + b >= unknowns:
                    continue
                term = ratio * band[i][b]
                before = band[i + a][b - a]
                band[i + a][b - a] = -term if before is None else before - term


    wait_all(decay_copies())
    receive_halos(0)
    for number in range(1, 3):
        recurrence(number)
        send(number)
        receive_lasts(number)
        complete(number)
        receive_halos(number)
    recurrence(3)
    for offset in range(1, teams):
        last_copy(3, offset).start()
    receive_lasts(3)
    entry = own_history(3)

    def finish(moment, state):
        state = list(state)
        layer = jnp.zeros((nx, lanes), jnp.float32)
        for z in range(nz):
            state[z] = decay[z] * state[z]
            values = iterate_3[moment, z] + state[z]
            iterate_3[moment, z] = values
            layer = layer + (values - iterate_2[moment, z])
        layer_sums[pl.ds(pl.multiple_of(moment * nx, nx), nx), :] = layer
        return tuple(state)

    lax.fori_loop(0, moments, finish, tuple(entry[z] for z in range(nz)), unroll=4)
    by_row = [layer_sums[pl.ds(x, moments, stride=nx), :] for x in range(nx)]
    columns = sum(by_row[1:], by_row[0])
    moment_lane = lax.broadcasted_iota(jnp.int32, (moments, lanes), 1)
    balance = 4.0 * columns - by_row[0] - by_row[nx - 1]
    balance = balance + jnp.where(moment_lane > 0, pltpu.roll(columns, 1, 1), 0.0)
    balance = balance + jnp.where(
        moment_lane < lanes - 1, pltpu.roll(columns, lanes - 1, 1), 0.0
    )
    stacked = jnp.concatenate([balance, by_row[0], by_row[nx - 1], columns], axis=0)
    member = (lane_id // width == row_id).astype(jnp.float32)
    ends = jnp.where(
        row_id == 0, first_lane.astype(jnp.float32), last_lane.astype(jnp.float32)
    )
    ends = jnp.where(row_id < 2, ends, 0.0)

    def against(left_side, right_side):
        return lax.dot_general(
            left_side,
            right_side,
            (((1,), (1,)), ((), ())),
            precision=highest,
            preferred_element_type=jnp.float32,
        )

    coarse_tiles[me] = jnp.where(
        lane_id < 3 * moments, against(member, stacked), against(ends, stacked)
    )

    def coarse_copy(offset):
        return pltpu.make_async_remote_copy(
            src_ref=coarse_tiles.at[me],
            dst_ref=coarse_tiles.at[me],
            send_sem=coarse_send.at[offset],
            recv_sem=coarse_recv.at[offset],
            device_id=place((me + offset) % devices),
            device_id_type=pl.DeviceIdType.MESH,
        )

    def coarse_start(offset, carry):
        coarse_copy(offset).start()
        return carry

    def coarse_wait(offset, carry):
        coarse_copy(offset).wait()
        return carry

    lax.fori_loop(1, devices, coarse_start, 0)
    lax.fori_loop(1, devices, coarse_wait, 0)

    kinds = [[None] * spatial for _ in range(4)]
    quarter = lane_id // moments
    for slot in range(spatial):
        for kind in range(4):
            merged = None
            for team in range(teams):
                tile = coarse_tiles[team * spatial + slot]
                turn = (moments * (team - kind)) % lanes
                turned = pltpu.roll(tile, turn, 1) if turn else tile
                merged = turned if team == 0 else jnp.where(quarter == team, turned, merged)
            kinds[kind][slot] = merged
    tiles = []
    for gx in range(nsx):
        for gy in range(nsy):
            slot = gx * nsy + gy
            tile = kinds[0][slot]
            if gx + 1 < nsx:
                tile = tile + kinds[1][slot + nsy]
            if gx > 0:
                tile = tile + kinds[2][slot - nsy]
            if gy > 0:
                tile = tile + jnp.where(row_id == 0, kinds[3][slot - 1][1:2], 0.0)
            if gy + 1 < nsy:
                tile = tile + jnp.where(row_id == strips - 1, kinds[3][slot + 1][0:1], 0.0)
            tiles.append(tile)
    spectrum = jnp.dot(
        jnp.concatenate(tiles, axis=0),
        table_ref[0:total, :],
        precision=highest,
        preferred_element_type=jnp.float32,
    )
    right = []
    for gy in range(ncy):
        for gx in range(nsx):
            row = (gx * nsy + gy // strips) * nx + gy % strips
            right.append(spectrum[row : row + 1])
    for i in range(unknowns):
        for a in range(1, nsx + 1):
            if ratios[i][a] is not None:
                right[i + a] = right[i + a] - ratios[i][a] * right[i]
    for i in reversed(range(unknowns)):
        value = right[i] * inverses[i]
        for a in range(1, nsx + 1):
            if ratios[i][a] is not None:
                value = value - ratios[i][a] * right[i + a]
        right[i] = value
    for gx in range(nsx):
        for block in range(nsy):
            for d in range(strips):
                number = (block * strips + d) * nsx + gx
                solved_tiles[gx * nsy + block, d : d + 1, :] = right[number]
    own_rows = solved_tiles[here]
    spread = jnp.concatenate(
        [jnp.broadcast_to(own_rows[d : d + 1], (width, total)) for d in range(strips)], axis=0
    )
    own_moments = pl.ds(pl.multiple_of(total + tm * moments, moments), moments)
    added_ref[...] = against(table_ref[own_moments, :], spread)

    def write(moment, carry):
        added = added_ref[pl.ds(moment, 1), :]
        for z in range(nz):
            out_ref[moment, z] = iterate_3[moment, z] + added
        return carry

    lax.fori_loop(0, moments, write, 0, unroll=4)


def local_fused(teams, nsx, nsy, driving_input, regime, reaction_rates):
    moments, nz, nx, lanes = driving_input.shape
    width = AGGREGATE_YCELLS
    total = teams * moments
    table = time_tables(total)
    sizes = (teams, nsx, nsy, moments, nz, nx, lanes, width)
    devices = teams * nsx * nsy
    blocks = 2 * moments * nz // lanes
    f32 = jnp.float32
    whole = pltpu.VMEM(driving_input.shape, f32)
    in_hbm = pl.BlockSpec(memory_space=pltpu.HBM)
    dma = pltpu.SemaphoreType.DMA
    return pl.pallas_call(
        functools.partial(fused_kernel, sizes),
        out_shape=jax.ShapeDtypeStruct(driving_input.shape, f32),
        in_specs=[pl.BlockSpec(memory_space=pltpu.SMEM)] + [in_hbm] * 3,
        out_specs=pl.BlockSpec(memory_space=pltpu.VMEM),
        scratch_shapes=[
            whole,
            pltpu.VMEM(regime.shape, jnp.int32),
            pltpu.VMEM(table.shape, f32),
            pltpu.VMEM((nsx * nsy, nx, lanes), f32),
            pltpu.VMEM((devices, 8, total), f32),
            pltpu.VMEM((nsx * nsy, max(lanes // width, 8), total), f32),
            pltpu.VMEM((moments, lanes), f32),
            pltpu.VMEM((moments * nx, lanes), f32),
            whole,
            whole,
            whole,
            whole,
            pltpu.VMEM((4, teams, nz, nx, lanes), f32),
            pltpu.VMEM((3, 2, moments * nz, lanes), f32),
            pltpu.VMEM((3, 2, moments * nz, lanes), f32),
            pltpu.VMEM((3, blocks, nx, lanes), f32),
            pltpu.VMEM((3, 2, blocks, nx, lanes), f32),
            pltpu.VMEM((blocks, nx, lanes), f32),
            pltpu.VMEM((3, 2, teams, nz, lanes), f32),
            pltpu.VMEM((3, 2, teams, nx, lanes), f32),
            pltpu.VMEM((2, nz, lanes), f32),
            pltpu.VMEM((2, nz, lanes), f32),
            pltpu.VMEM((nx, lanes), f32),
            pltpu.VMEM((2, nx, lanes), f32),
            dma((3,)),
            dma((4 * teams,)),
            dma((4 * teams,)),
            dma((nsx * nsy,)),
            dma((nsx * nsy,)),
            dma((devices,)),
            dma((devices,)),
            dma((12,)),
            dma((12,)),
            dma((12 * teams,)),
            dma((12 * teams,)),
            dma((4,)),
            dma((4,)),
        ],
        compiler_params=pltpu.CompilerParams(
            collective_id=0, has_side_effects=True, vmem_limit_bytes=62 * 1024 * 1024
        ),
    )(reaction_rates, driving_input, regime, jnp.asarray(table))


def local(driving_input, regime, reaction_rates):
    moments, nz, nx, lanes = driving_input.shape
    teams, nsx, nsy = (lax.axis_size(axis) for axis in ("tm", "sx", "sy"))
    strips = lanes // AGGREGATE_YCELLS
    whole_strips = nx == AGGREGATE_XCELLS and strips * AGGREGATE_YCELLS == lanes and strips <= 8
    tiled = nx == 8 and nz == 8 and lanes == 128 and moments % 8 == 0
    if whole_strips and tiled and teams * moments == 128 and 4 * moments == 128 and SWEEPS == 4:
        return local_fused(teams, nsx, nsy, driving_input, regime, reaction_rates)
    return local_general(driving_input, regime, reaction_rates)


def solution(mesh):
    placed = (P("tm", None, "sx", "sy"), P(None, "sx", "sy"), P())
    return jax.shard_map(
        local, mesh=mesh, in_specs=placed, out_specs=P("tm", None, "sx", "sy"), check_vma=False
    )
```

```python
import functools

import jax
import jax.numpy as jnp
import numpy as np
from jax import lax
from jax.experimental import pallas as pl
from jax.experimental.pallas import tpu as pltpu
from jax.sharding import PartitionSpec as P

AGGREGATE_XCELLS = 8
AGGREGATE_YCELLS = 32
SWEEPS = 4


TWO_PI = 2.0 * 3.141592653589793


def extended(block, sides, width):
    for axis, dim in sides:
        count = lax.axis_size(axis)
        forward = [(i, i + 1) for i in range(count - 1)]
        backward = [(target, source) for source, target in forward]
        low = lax.ppermute(
            lax.slice_in_dim(block, block.shape[dim] - width, None, axis=dim), axis, forward
        )
        high = lax.ppermute(lax.slice_in_dim(block, 0, width, axis=dim), axis, backward)
        block = jnp.concatenate([low, block, high], axis=dim)
    return block


def angle_table(row_index, col_index, cycle_duration):
    product = row_index[:, None] * col_index[None, :] % cycle_duration
    angles = product.astype(jnp.float32) * (TWO_PI / cycle_duration)
    return (jnp.cos(angles), jnp.sin(angles))


def matmul(left_side, right_side):
    return jnp.dot(
        left_side, right_side, precision=lax.Precision.HIGHEST, preferred_element_type=jnp.float32
    )


def complex_mul(left_real, left_imag, pair):
    return jnp.stack(
        [left_real * pair[0] - left_imag * pair[1], left_real * pair[1] + left_imag * pair[0]]
    )


def neighbors(present_guess):
    padded = extended(present_guess, (("sx", 3), ("sy", 4)), 1)
    running = padded[:, :, :, 2:, 1:-1] + padded[:, :, :, :-2, 1:-1]
    running = running + padded[:, :, :, 1:-1, 2:] + padded[:, :, :, 1:-1, :-2]
    running = running + jnp.roll(present_guess, 1, axis=2) + jnp.roll(present_guess, -1, axis=2)
    return running


def local_general(driving_input, regime, reaction_rates):
    moment_count, third_axis_count, first_axis_count, second_axis_count = driving_input.shape
    temporal_spacing = lax.axis_size("tm")
    sy_size = lax.axis_size("sy")
    cycle_duration = moment_count * temporal_spacing
    unknowns_in_tile = third_axis_count * first_axis_count * second_axis_count
    processor_lines = driving_input.reshape(moment_count, unknowns_in_tile)
    owned_slice_number = lax.axis_index("tm") * moment_count + jnp.arange(
        moment_count, dtype=jnp.int32
    )
    all_index = jnp.arange(cycle_duration, dtype=jnp.int32)
    cos_rows, sin_rows = angle_table(owned_slice_number, all_index, cycle_duration)

    def forward(running, segment, offset):
        return jnp.stack([matmul(cos_rows, segment), -matmul(sin_rows, segment)])

    eigen_spectra = forward(
        jnp.zeros((2, moment_count, unknowns_in_tile), jnp.float32),
        lax.all_gather(processor_lines, "tm", axis=0, tiled=True),
        jnp.int32(0),
    )
    source_term = eigen_spectra.reshape(
        2, moment_count, third_axis_count, first_axis_count, second_axis_count
    )
    phase_angle = owned_slice_number.astype(jnp.float32) * (TWO_PI / cycle_duration)
    shift_real = (1.0 - jnp.cos(phase_angle))[:, None, None, None]
    shift_imag = jnp.sin(phase_angle)[:, None, None, None]
    reaction = jnp.zeros(regime.shape, jnp.float32)
    for regime_no in range(reaction_rates.shape[0]):
        reaction = reaction + jnp.where(
            regime == regime_no, reaction_rates[regime_no], jnp.zeros((), jnp.float32)
        )
    diag_real = reaction[None] + 6.0 + shift_real
    diag_imag = jnp.zeros_like(diag_real) + shift_imag
    modulus = diag_real * diag_real + diag_imag * diag_imag
    inverse_real = diag_real / modulus
    inverse_imag = -diag_imag / modulus
    present_guess = complex_mul(inverse_real, inverse_imag, source_term)
    for sweep_no in range(SWEEPS - 1):
        present_guess = complex_mul(
            inverse_real, inverse_imag, source_term + neighbors(present_guess)
        )
    applied = complex_mul(diag_real, diag_imag, present_guess) - neighbors(present_guess)
    residual = source_term - applied
    first_axis_teams = first_axis_count // AGGREGATE_XCELLS
    second_axis_teams = second_axis_count // AGGREGATE_YCELLS
    per_device = first_axis_teams * second_axis_teams

    def aggregate(values):
        leading = values.shape[:-3]
        blocks = values.reshape(
            leading
            + (
                third_axis_count,
                first_axis_teams,
                AGGREGATE_XCELLS,
                second_axis_teams,
                AGGREGATE_YCELLS,
            )
        )
        return jnp.sum(blocks, axis=(-5, -3, -1)).reshape(leading + (per_device,))

    coarse_right = jnp.transpose(aggregate(residual), (1, 0, 2))
    rate_sums = aggregate(reaction)
    shift_column = 1.0 - jnp.cos(phase_angle)
    face_count = 2 * (AGGREGATE_YCELLS * third_axis_count + AGGREGATE_XCELLS * third_axis_count)
    volume = AGGREGATE_XCELLS * AGGREGATE_YCELLS * third_axis_count
    spatial = lax.axis_size("sx") * sy_size
    slot_count = -(-moment_count // spatial)
    padding_rows = slot_count * spatial - moment_count
    padded_right = jnp.pad(coarse_right, ((0, padding_rows), (0, 0), (0, 0)))
    sum_copies = jnp.broadcast_to(rate_sums[None, None, :], (spatial, 1, per_device))
    shared_right, shared_sums = (
        lax.all_to_all(padded_right, ("sx", "sy"), split_axis=0, concat_axis=2, tiled=True),
        lax.all_to_all(sum_copies, ("sx", "sy"), split_axis=0, concat_axis=2, tiled=True),
    )
    spatial_rank = lax.axis_index("sx") * sy_size + lax.axis_index("sy")
    padded_shift = jnp.pad(shift_column, (0, padding_rows))
    slot_shift = lax.dynamic_slice_in_dim(padded_shift, spatial_rank * slot_count, slot_count, 0)
    sum_values = shared_sums[0, 0]
    coarse_total = sum_values.shape[0]
    position = jnp.arange(coarse_total, dtype=jnp.int32)
    device = position // per_device
    within = position % per_device
    coarse_x = device // sy_size * first_axis_teams + within // second_axis_teams
    coarse_y = device % sy_size * second_axis_teams + within % second_axis_teams
    x_gap = jnp.abs(coarse_x[:, None] - coarse_x[None, :])
    y_gap = jnp.abs(coarse_y[:, None] - coarse_y[None, :])
    coupling = -(AGGREGATE_YCELLS * third_axis_count) * ((x_gap == 1) & (y_gap == 0)).astype(
        jnp.float32
    )
    coupling = coupling - AGGREGATE_XCELLS * third_axis_count * (
        (x_gap == 0) & (y_gap == 1)
    ).astype(jnp.float32)
    identity = (position[:, None] == position[None, :]).astype(jnp.float32)
    diagonal = sum_values + face_count
    system = (
        coupling[None]
        + identity[None] * (diagonal[None, :] + volume * slot_shift[:, None])[:, None, :]
    )
    factor = jnp.linalg.cholesky(system)
    right_side = jnp.transpose(shared_right, (0, 2, 1))
    forward_sub = lax.linalg.triangular_solve(factor, right_side, left_side=True, lower=True)
    coarse = lax.linalg.triangular_solve(
        factor, forward_sub, left_side=True, lower=True, transpose_a=True
    )
    solved = jnp.transpose(coarse, (0, 2, 1))
    returned = lax.all_to_all(solved, ("sx", "sy"), split_axis=2, concat_axis=0, tiled=True)
    own_coarse = returned[:moment_count]
    local_part = jnp.transpose(own_coarse, (1, 0, 2)).reshape(
        2, moment_count, 1, first_axis_teams, 1, second_axis_teams, 1
    )
    spread_values = jnp.broadcast_to(
        local_part,
        (
            2,
            moment_count,
            third_axis_count,
            first_axis_teams,
            AGGREGATE_XCELLS,
            second_axis_teams,
            AGGREGATE_YCELLS,
        ),
    )
    present_guess = present_guess + spread_values.reshape(
        2, moment_count, third_axis_count, first_axis_count, second_axis_count
    )
    unrolled_array = present_guess.reshape(2, moment_count, unknowns_in_tile)

    def backward(running, segment, offset):
        return matmul(cos_rows, segment[0]) - matmul(sin_rows, segment[1])

    result = (
        backward(
            jnp.zeros((moment_count, unknowns_in_tile), jnp.float32),
            lax.all_gather(unrolled_array, "tm", axis=1, tiled=True),
            jnp.int32(0),
        )
        / cycle_duration
    )
    return result.reshape(driving_input.shape)


def time_tables(count):
    half = count // 2
    lane = np.arange(count)
    frequency = np.where(lane <= half, lane, lane - half)
    imaginary = lane > half
    moment = np.arange(count)
    angle = 2.0 * np.pi * (moment[:, None] * frequency[None, :] % count) / count
    forward = np.where(imaginary[None, :], -np.sin(angle), np.cos(angle))
    weight = np.where((lane == 0) | (lane == half), 1.0, 2.0) / count
    theta = 2.0 * np.pi * frequency / count
    signed = np.where(lane % half == 0, 0.0, np.sin(theta)) * np.where(lane < half, 1.0, -1.0)
    shift = np.zeros((8, count))
    shift[0] = 1.0 - np.cos(theta)
    shift[1] = signed
    return np.concatenate([forward, forward * weight[None, :], shift]).astype(np.float32)


def fused_kernel(
    sizes,
    rates_ref,
    field_hbm,
    regime_hbm,
    table_hbm,
    out_hbm,
    added_ref,
    field_ref,
    regime_ref,
    table_ref,
    rate_tiles,
    coarse_tiles,
    all_kinds,
    solved_tiles,
    layer_sums,
    iterate_0,
    iterate_1,
    iterate_2,
    iterate_3,
    lasts,
    x_edges,
    x_halos,
    y_edges,
    y_halos,
    load_sem,
    store_sem,
    last_send,
    last_recv,
    rate_send,
    rate_recv,
    team_send,
    team_recv,
    kind_send,
    kind_recv,
    halo_send,
    halo_recv,
):
    teams, nsx, nsy, moments, nz, nx, lanes, width = sizes
    total = teams * moments
    strips = lanes // width
    plane = nz * nx
    spatial = nsx * nsy
    highest = lax.Precision.HIGHEST
    tm = lax.axis_index("tm")
    ix = lax.axis_index("sx")
    iy = lax.axis_index("sy")
    here = ix * nsy + iy

    loads = [
        pltpu.make_async_copy(regime_hbm, regime_ref, load_sem.at[0]),
        pltpu.make_async_copy(field_hbm, field_ref, load_sem.at[1]),
        pltpu.make_async_copy(table_hbm, table_ref, load_sem.at[2]),
    ]
    for load in loads:
        load.start()

    def peers(axis, index, size):
        return [{"tm": tm, "sx": ix, "sy": iy, axis: (index + o) % size} for o in range(1, size)]

    team_peers = peers("tm", tm, teams)
    row_peers = peers("sx", ix, nsx)
    strip_peers = peers("sy", iy, nsy)
    greeted = team_peers + row_peers + strip_peers
    barrier = pltpu.get_barrier_semaphore()
    for peer in greeted:
        pl.semaphore_signal(
            barrier, inc=1, device_id=peer, device_id_type=pl.DeviceIdType.MESH
        )

    def gather(ref, targets, send_sem, recv_sem, first):
        return [
            pltpu.make_async_remote_copy(
                src_ref=ref,
                dst_ref=ref,
                send_sem=send_sem.at[first + number],
                recv_sem=recv_sem.at[first + number],
                device_id=peer,
                device_id_type=pl.DeviceIdType.MESH,
            )
            for number, peer in enumerate(targets)
        ]

    def spatial_gather(ref, send_sem, recv_sem):
        def whole():
            for copy in gather(ref.at[iy, ix], row_peers, send_sem, recv_sem, 0):
                copy.start()
            for copy in gather(ref.at[iy, ix], row_peers, send_sem, recv_sem, 0):
                copy.wait()
            for copy in gather(ref.at[iy], strip_peers, send_sem, recv_sem, nsx):
                copy.start()

        def finish():
            for copy in gather(ref.at[iy], strip_peers, send_sem, recv_sem, nsx):
                copy.wait()

        return whole, finish

    loads[0].wait()
    rates = jnp.zeros(regime_ref.shape, jnp.float32)
    regime = regime_ref[...]
    for number in range(rates_ref.shape[0]):
        rates = rates + jnp.where(regime == number, rates_ref[number], 0.0)
    rate_tiles[iy, ix] = jnp.sum(rates, axis=0)
    pl.semaphore_wait(barrier, len(greeted))
    rates_begin, rates_end = spatial_gather(rate_tiles, rate_send, rate_recv)
    rates_begin()
    decay = 1.0 / (rates + 7.0)
    decay_block = jnp.ones_like(decay)
    power, left = decay, moments
    while left:
        if left & 1:
            decay_block = decay_block * power
        power = power * power
        left //= 2
    decay_round = jnp.ones_like(decay)
    for _ in range(teams):
        decay_round = decay_round * decay_block
    closing = 1.0 / (1.0 - decay_round)

    has = (ix > 0, ix < nsx - 1, iy > 0, iy < nsy - 1)
    neighbour = (
        {"tm": tm, "sx": (ix + nsx - 1) % nsx, "sy": iy},
        {"tm": tm, "sx": (ix + 1) % nsx, "sy": iy},
        {"tm": tm, "sx": ix, "sy": (iy + nsy - 1) % nsy},
        {"tm": tm, "sx": ix, "sy": (iy + 1) % nsy},
    )
    for number in range(3):
        for side in range(4):

            @pl.when(jnp.logical_not(has[side]))
            def _(halo=(x_halos if side < 2 else y_halos).at[number, side % 2]):
                halo[...] = jnp.zeros(halo.shape, jnp.float32)

    def halo_copies(number):
        copies = []
        for side in range(4):
            if side < 2:
                source = x_edges.at[number, side]
                target = x_halos.at[number, 1 - side]
            else:
                source = y_edges.at[number]
                target = y_halos.at[number, 3 - side]
            copies.append(
                pltpu.make_async_remote_copy(
                    src_ref=source,
                    dst_ref=target,
                    send_sem=halo_send.at[number * 4 + side],
                    recv_sem=halo_recv.at[number * 4 + (side ^ 1)],
                    device_id=neighbour[side],
                    device_id_type=pl.DeviceIdType.MESH,
                )
            )
        return copies

    def exchange_start(number):
        for side, copy in enumerate(halo_copies(number)):

            @pl.when(has[side])
            def _(copy=copy):
                copy.start()

    def exchange_wait(number):
        copies = halo_copies(number)
        for side in range(4):

            @pl.when(has[side])
            def _(side=side):
                copies[side].wait_send()
                copies[side ^ 1].wait_recv()

    def last_copy(number, offset):
        return pltpu.make_async_remote_copy(
            src_ref=lasts.at[number, tm],
            dst_ref=lasts.at[number, tm],
            send_sem=last_send.at[number * teams + offset],
            recv_sem=last_recv.at[number * teams + offset],
            device_id={"tm": (tm + offset) % teams, "sx": ix, "sy": iy},
            device_id_type=pl.DeviceIdType.MESH,
        )

    iterates = (iterate_0, iterate_1, iterate_2, iterate_3)
    chunk = lanes // 2 // nz
    row_id = lax.broadcasted_iota(jnp.int32, (nx, lanes), 0)
    lane_id = lax.broadcasted_iota(jnp.int32, (nx, lanes), 1)
    first_row, last_row = row_id == 0, row_id == nx - 1
    first_lane, last_lane = lane_id == 0, lane_id == lanes - 1
    odd_lane = lane_id % 2 == 1
    pair = (lane_id + 1) % lanes // 2

    def recurrence(number):
        def body(block, state):
            if number:
                high = y_halos[number - 1, 1, block]
                low = pltpu.roll(y_halos[number - 1, 0, block], 2, 1)
                ends = jnp.where(odd_lane, low, high)
                old = iterates[number - 1]
            state = list(state)
            for inner in range(chunk):
                moment = block * chunk + inner
                if number:
                    cells = [old[moment, z] for z in range(nz)]
                for z in range(nz):
                    values = field_ref[moment, z]
                    if number:
                        here_cell = cells[z]
                        slot = inner * nz + z
                        turned = pltpu.roll(ends, (lanes - 2 * slot - 1) % lanes, 1)
                        row = moment * nz + z
                        low_row = x_halos[number - 1, 0, pl.ds(row, 1), :]
                        high_row = x_halos[number - 1, 1, pl.ds(row, 1), :]
                        values = values + cells[z - 1] + cells[(z + 1) % nz]
                        values = values + jnp.where(
                            first_row, low_row, pltpu.roll(here_cell, 1, 0)
                        )
                        values = values + jnp.where(
                            last_row, high_row, pltpu.roll(here_cell, nx - 1, 0)
                        )
                        values = values + jnp.where(
                            first_lane, turned, pltpu.roll(here_cell, 1, 1)
                        )
                        values = values + jnp.where(
                            last_lane, turned, pltpu.roll(here_cell, lanes - 1, 1)
                        )
                    state[z] = decay[z] * (values + state[z])
                    iterates[number][moment, z] = state[z]
            return tuple(state)

        start = tuple(jnp.zeros((nx, lanes), jnp.float32) for _ in range(nz))
        state = lax.fori_loop(0, moments // chunk, body, start)
        for z in range(nz):
            lasts[number, tm, z] = state[z]

    def history(number):
        value = lasts[number, tm]
        for offset in range(1, teams):
            value = lasts[number, (tm + offset) % teams] + decay_block * value
        return value * closing

    def complete(number, entry):
        def body(block, state):
            state = list(state)
            packed = jnp.zeros((nx, lanes), jnp.float32)
            for inner in range(chunk):
                moment = block * chunk + inner
                for z in range(nz):
                    state[z] = decay[z] * state[z]
                    values = iterates[number][moment, z] + state[z]
                    iterates[number][moment, z] = values
                    slot = inner * nz + z
                    packed = jnp.where(pair == slot, pltpu.roll(values, 2 * slot, 1), packed)
                    row = moment * nz + z
                    x_edges[number, 0, pl.ds(row, 1), :] = values[0:1]
                    x_edges[number, 1, pl.ds(row, 1), :] = values[nx - 1 : nx]
            y_edges[number, block] = packed
            return tuple(state)

        lax.fori_loop(0, moments // chunk, body, tuple(entry[z] for z in range(nz)))

    loads[1].wait()
    recurrence(0)
    for offset in range(1, teams):
        last_copy(0, offset).start()
    for offset in range(1, teams):
        last_copy(0, offset).wait()
    complete(0, history(0))
    exchange_start(0)

    rates_end()
    loads[2].wait()
    shift_real = table_ref[2 * total : 2 * total + 1, :]
    ncy = nsy * strips
    strip_block = lax.broadcasted_iota(jnp.int32, (nx, lanes), 1) // width
    faces = 2 * (width * nz + nx * nz)
    couple_x = -float(width * nz)
    couple_y = -float(nx * nz)
    unknowns = ncy * nsx
    band = [[None] * (nsx + 1) for _ in range(unknowns)]
    for gy in range(ncy):
        for gx in range(nsx):
            number = gy * nsx + gx
            tile = rate_tiles[gy // strips, gx]
            amount = jnp.sum(jnp.where(strip_block == gy % strips, tile, 0.0), axis=0, keepdims=True)
            amount = jnp.sum(amount, axis=1, keepdims=True)
            band[number][0] = amount + faces + float(nx * width * nz) * shift_real
            if gx + 1 < nsx:
                band[number][1] = jnp.full((1, total), couple_x, jnp.float32)
            if gy + 1 < ncy:
                extra = jnp.full((1, total), couple_y, jnp.float32)
                before = band[number][nsx]
                band[number][nsx] = extra if before is None else before + extra
    inverses = []
    ratios = []
    for i in range(unknowns):
        inverse = 1.0 / band[i][0]
        inverses.append(inverse)
        ratios.append([None] * (nsx + 1))
        for a in range(1, nsx + 1):
            if band[i][a] is None or i + a >= unknowns:
                continue
            ratio = band[i][a] * inverse
            ratios[i][a] = ratio
            for b in range(a, nsx + 1):
                if band[i][b] is None or i + b >= unknowns:
                    continue
                term = ratio * band[i][b]
                before = band[i + a][b - a]
                band[i + a][b - a] = -term if before is None else before - term


    exchange_wait(0)
    for number in range(1, 4):
        recurrence(number)
        for offset in range(1, teams):
            last_copy(number, offset).start()
        for offset in range(1, teams):
            last_copy(number, offset).wait()
        if number < 3:
            complete(number, history(number))
            exchange_start(number)
            exchange_wait(number)

    entry = history(3)

    def finish(moment, state):
        state = list(state)
        layer = jnp.zeros((nx, lanes), jnp.float32)
        for z in range(nz):
            state[z] = decay[z] * state[z]
            values = iterate_3[moment, z] + state[z]
            iterate_3[moment, z] = values
            layer = layer + (values - iterate_2[moment, z])
        layer_sums[pl.ds(pl.multiple_of(moment * nx, nx), nx), :] = layer
        return tuple(state)

    lax.fori_loop(0, moments, finish, tuple(entry[z] for z in range(nz)), unroll=4)
    store = pltpu.make_async_copy(iterate_3, out_hbm, store_sem)
    store.start()
    by_row = [layer_sums[pl.ds(x, moments, stride=nx), :] for x in range(nx)]
    columns = sum(by_row[1:], by_row[0])
    moment_lane = lax.broadcasted_iota(jnp.int32, (moments, lanes), 1)
    balance = 4.0 * columns - by_row[0] - by_row[nx - 1]
    balance = balance + jnp.where(moment_lane > 0, pltpu.roll(columns, 1, 1), 0.0)
    balance = balance + jnp.where(
        moment_lane < lanes - 1, pltpu.roll(columns, lanes - 1, 1), 0.0
    )
    stacked = jnp.concatenate([balance, by_row[0], by_row[nx - 1], columns], axis=0)
    member = (lane_id // width == row_id).astype(jnp.float32)
    ends = jnp.where(
        row_id == 0, first_lane.astype(jnp.float32), last_lane.astype(jnp.float32)
    )
    ends = jnp.where(row_id < 2, ends, 0.0)

    def against(left_side, right_side):
        return lax.dot_general(
            left_side,
            right_side,
            (((1,), (1,)), ((), ())),
            precision=highest,
            preferred_element_type=jnp.float32,
        )

    coarse_tiles[tm] = jnp.where(
        lane_id < 3 * moments, against(member, stacked), against(ends, stacked)
    )
    for copy in gather(coarse_tiles.at[tm], team_peers, team_send, team_recv, 0):
        copy.start()
    for copy in gather(coarse_tiles.at[tm], team_peers, team_send, team_recv, 0):
        copy.wait()
    quarter = lane_id // moments
    for kind in range(4):
        merged = None
        for team in range(teams):
            tile = coarse_tiles[team]
            turn = (moments * (team - kind)) % lanes
            turned = pltpu.roll(tile, turn, 1) if turn else tile
            merged = turned if team == 0 else jnp.where(quarter == team, turned, merged)
        all_kinds[iy, ix, kind] = merged
    kinds_begin, kinds_end = spatial_gather(all_kinds, kind_send, kind_recv)
    kinds_begin()
    kinds_end()
    kinds = [
        [all_kinds[slot % nsy, slot // nsy, kind] for slot in range(spatial)]
        for kind in range(4)
    ]
    tiles = []
    for gx in range(nsx):
        for gy in range(nsy):
            slot = gx * nsy + gy
            tile = kinds[0][slot]
            if gx + 1 < nsx:
                tile = tile + kinds[1][slot + nsy]
            if gx > 0:
                tile = tile + kinds[2][slot - nsy]
            if gy > 0:
                tile = tile + jnp.where(row_id == 0, kinds[3][slot - 1][1:2], 0.0)
            if gy + 1 < nsy:
                tile = tile + jnp.where(row_id == strips - 1, kinds[3][slot + 1][0:1], 0.0)
            tiles.append(tile)
    spectrum = jnp.dot(
        jnp.concatenate(tiles, axis=0),
        table_ref[0:total, :],
        precision=highest,
        preferred_element_type=jnp.float32,
    )
    right = []
    for gy in range(ncy):
        for gx in range(nsx):
            row = (gx * nsy + gy // strips) * nx + gy % strips
            right.append(spectrum[row : row + 1])
    for i in range(unknowns):
        for a in range(1, nsx + 1):
            if ratios[i][a] is not None:
                right[i + a] = right[i + a] - ratios[i][a] * right[i]
    for i in reversed(range(unknowns)):
        value = right[i] * inverses[i]
        for a in range(1, nsx + 1):
            if ratios[i][a] is not None:
                value = value - ratios[i][a] * right[i + a]
        right[i] = value
    for gx in range(nsx):
        for block in range(nsy):
            for d in range(strips):
                number = (block * strips + d) * nsx + gx
                solved_tiles[gx * nsy + block, d : d + 1, :] = right[number]
    own_rows = solved_tiles[here]
    spread = jnp.concatenate(
        [jnp.broadcast_to(own_rows[d : d + 1], (width, total)) for d in range(strips)], axis=0
    )
    own_moments = pl.ds(pl.multiple_of(total + tm * moments, moments), moments)
    added_ref[...] = against(table_ref[own_moments, :], spread)

    store.wait()


def local_fused(teams, nsx, nsy, driving_input, regime, reaction_rates):
    moments, nz, nx, lanes = driving_input.shape
    width = AGGREGATE_YCELLS
    total = teams * moments
    table = time_tables(total)
    sizes = (teams, nsx, nsy, moments, nz, nx, lanes, width)
    blocks = 2 * moments * nz // lanes
    f32 = jnp.float32
    whole = pltpu.VMEM(driving_input.shape, f32)
    in_hbm = pl.BlockSpec(memory_space=pltpu.HBM)
    dma = pltpu.SemaphoreType.DMA
    field, added = pl.pallas_call(
        functools.partial(fused_kernel, sizes),
        out_shape=(
            jax.ShapeDtypeStruct(driving_input.shape, f32),
            jax.ShapeDtypeStruct((moments, lanes), f32),
        ),
        in_specs=[pl.BlockSpec(memory_space=pltpu.SMEM)] + [in_hbm] * 3,
        out_specs=(pl.BlockSpec(memory_space=pl.ANY), pl.BlockSpec(memory_space=pltpu.VMEM)),
        scratch_shapes=[
            whole,
            pltpu.VMEM(regime.shape, jnp.int32),
            pltpu.VMEM(table.shape, f32),
            pltpu.VMEM((nsy, nsx, nx, lanes), f32),
            pltpu.VMEM((teams, 8, total), f32),
            pltpu.VMEM((nsy, nsx, 4, 8, total), f32),
            pltpu.VMEM((nsx * nsy, max(lanes // width, 8), total), f32),
            pltpu.VMEM((moments * nx, lanes), f32),
            whole,
            whole,
            whole,
            whole,
            pltpu.VMEM((4, teams, nz, nx, lanes), f32),
            pltpu.VMEM((3, 2, moments * nz, lanes), f32),
            pltpu.VMEM((3, 2, moments * nz, lanes), f32),
            pltpu.VMEM((3, blocks, nx, lanes), f32),
            pltpu.VMEM((3, 2, blocks, nx, lanes), f32),
            dma((3,)),
            dma,
            dma((4 * teams,)),
            dma((4 * teams,)),
            dma((nsx + nsy,)),
            dma((nsx + nsy,)),
            dma((teams,)),
            dma((teams,)),
            dma((nsx + nsy,)),
            dma((nsx + nsy,)),
            dma((12,)),
            dma((12,)),
        ],
        compiler_params=pltpu.CompilerParams(
            collective_id=0, has_side_effects=True, vmem_limit_bytes=62 * 1024 * 1024
        ),
    )(reaction_rates, driving_input, regime, jnp.asarray(table))
    return field + added[:, None, None, :]


def local(driving_input, regime, reaction_rates):
    moments, nz, nx, lanes = driving_input.shape
    teams, nsx, nsy = (lax.axis_size(axis) for axis in ("tm", "sx", "sy"))
    strips = lanes // AGGREGATE_YCELLS
    whole_strips = nx == AGGREGATE_XCELLS and strips * AGGREGATE_YCELLS == lanes and strips <= 8
    tiled = nx == 8 and nz == 8 and lanes == 128 and moments % 8 == 0
    if whole_strips and tiled and teams * moments == 128 and 4 * moments == 128 and SWEEPS == 4:
        return local_fused(teams, nsx, nsy, driving_input, regime, reaction_rates)
    return local_general(driving_input, regime, reaction_rates)


def solution(mesh):
    placed = (P("tm", None, "sx", "sy"), P(None, "sx", "sy"), P())
    return jax.shard_map(
        local, mesh=mesh, in_specs=placed, out_specs=P("tm", None, "sx", "sy"), check_vma=False
    )
```

```python
import functools

import jax
import jax.numpy as jnp
import numpy as np
from jax import lax
from jax.experimental import pallas as pl
from jax.experimental.pallas import tpu as pltpu
from jax.sharding import PartitionSpec as P

AGGREGATE_XCELLS = 8
AGGREGATE_YCELLS = 32
SWEEPS = 4


TWO_PI = 2.0 * 3.141592653589793


def extended(block, sides, width):
    for axis, dim in sides:
        count = lax.axis_size(axis)
        forward = [(i, i + 1) for i in range(count - 1)]
        backward = [(target, source) for source, target in forward]
        low = lax.ppermute(
            lax.slice_in_dim(block, block.shape[dim] - width, None, axis=dim), axis, forward
        )
        high = lax.ppermute(lax.slice_in_dim(block, 0, width, axis=dim), axis, backward)
        block = jnp.concatenate([low, block, high], axis=dim)
    return block


def angle_table(row_index, col_index, cycle_duration):
    product = row_index[:, None] * col_index[None, :] % cycle_duration
    angles = product.astype(jnp.float32) * (TWO_PI / cycle_duration)
    return (jnp.cos(angles), jnp.sin(angles))


def matmul(left_side, right_side):
    return jnp.dot(
        left_side, right_side, precision=lax.Precision.HIGHEST, preferred_element_type=jnp.float32
    )


def complex_mul(left_real, left_imag, pair):
    return jnp.stack(
        [left_real * pair[0] - left_imag * pair[1], left_real * pair[1] + left_imag * pair[0]]
    )


def neighbors(present_guess):
    padded = extended(present_guess, (("sx", 3), ("sy", 4)), 1)
    running = padded[:, :, :, 2:, 1:-1] + padded[:, :, :, :-2, 1:-1]
    running = running + padded[:, :, :, 1:-1, 2:] + padded[:, :, :, 1:-1, :-2]
    running = running + jnp.roll(present_guess, 1, axis=2) + jnp.roll(present_guess, -1, axis=2)
    return running


def local_general(driving_input, regime, reaction_rates):
    moment_count, third_axis_count, first_axis_count, second_axis_count = driving_input.shape
    temporal_spacing = lax.axis_size("tm")
    sy_size = lax.axis_size("sy")
    cycle_duration = moment_count * temporal_spacing
    unknowns_in_tile = third_axis_count * first_axis_count * second_axis_count
    processor_lines = driving_input.reshape(moment_count, unknowns_in_tile)
    owned_slice_number = lax.axis_index("tm") * moment_count + jnp.arange(
        moment_count, dtype=jnp.int32
    )
    all_index = jnp.arange(cycle_duration, dtype=jnp.int32)
    cos_rows, sin_rows = angle_table(owned_slice_number, all_index, cycle_duration)

    def forward(running, segment, offset):
        return jnp.stack([matmul(cos_rows, segment), -matmul(sin_rows, segment)])

    eigen_spectra = forward(
        jnp.zeros((2, moment_count, unknowns_in_tile), jnp.float32),
        lax.all_gather(processor_lines, "tm", axis=0, tiled=True),
        jnp.int32(0),
    )
    source_term = eigen_spectra.reshape(
        2, moment_count, third_axis_count, first_axis_count, second_axis_count
    )
    phase_angle = owned_slice_number.astype(jnp.float32) * (TWO_PI / cycle_duration)
    shift_real = (1.0 - jnp.cos(phase_angle))[:, None, None, None]
    shift_imag = jnp.sin(phase_angle)[:, None, None, None]
    reaction = jnp.zeros(regime.shape, jnp.float32)
    for regime_no in range(reaction_rates.shape[0]):
        reaction = reaction + jnp.where(
            regime == regime_no, reaction_rates[regime_no], jnp.zeros((), jnp.float32)
        )
    diag_real = reaction[None] + 6.0 + shift_real
    diag_imag = jnp.zeros_like(diag_real) + shift_imag
    modulus = diag_real * diag_real + diag_imag * diag_imag
    inverse_real = diag_real / modulus
    inverse_imag = -diag_imag / modulus
    present_guess = complex_mul(inverse_real, inverse_imag, source_term)
    for sweep_no in range(SWEEPS - 1):
        present_guess = complex_mul(
            inverse_real, inverse_imag, source_term + neighbors(present_guess)
        )
    applied = complex_mul(diag_real, diag_imag, present_guess) - neighbors(present_guess)
    residual = source_term - applied
    first_axis_teams = first_axis_count // AGGREGATE_XCELLS
    second_axis_teams = second_axis_count // AGGREGATE_YCELLS
    per_device = first_axis_teams * second_axis_teams

    def aggregate(values):
        leading = values.shape[:-3]
        blocks = values.reshape(
            leading
            + (
                third_axis_count,
                first_axis_teams,
                AGGREGATE_XCELLS,
                second_axis_teams,
                AGGREGATE_YCELLS,
            )
        )
        return jnp.sum(blocks, axis=(-5, -3, -1)).reshape(leading + (per_device,))

    coarse_right = jnp.transpose(aggregate(residual), (1, 0, 2))
    rate_sums = aggregate(reaction)
    shift_column = 1.0 - jnp.cos(phase_angle)
    face_count = 2 * (AGGREGATE_YCELLS * third_axis_count + AGGREGATE_XCELLS * third_axis_count)
    volume = AGGREGATE_XCELLS * AGGREGATE_YCELLS * third_axis_count
    spatial = lax.axis_size("sx") * sy_size
    slot_count = -(-moment_count // spatial)
    padding_rows = slot_count * spatial - moment_count
    padded_right = jnp.pad(coarse_right, ((0, padding_rows), (0, 0), (0, 0)))
    sum_copies = jnp.broadcast_to(rate_sums[None, None, :], (spatial, 1, per_device))
    shared_right, shared_sums = (
        lax.all_to_all(padded_right, ("sx", "sy"), split_axis=0, concat_axis=2, tiled=True),
        lax.all_to_all(sum_copies, ("sx", "sy"), split_axis=0, concat_axis=2, tiled=True),
    )
    spatial_rank = lax.axis_index("sx") * sy_size + lax.axis_index("sy")
    padded_shift = jnp.pad(shift_column, (0, padding_rows))
    slot_shift = lax.dynamic_slice_in_dim(padded_shift, spatial_rank * slot_count, slot_count, 0)
    sum_values = shared_sums[0, 0]
    coarse_total = sum_values.shape[0]
    position = jnp.arange(coarse_total, dtype=jnp.int32)
    device = position // per_device
    within = position % per_device
    coarse_x = device // sy_size * first_axis_teams + within // second_axis_teams
    coarse_y = device % sy_size * second_axis_teams + within % second_axis_teams
    x_gap = jnp.abs(coarse_x[:, None] - coarse_x[None, :])
    y_gap = jnp.abs(coarse_y[:, None] - coarse_y[None, :])
    coupling = -(AGGREGATE_YCELLS * third_axis_count) * ((x_gap == 1) & (y_gap == 0)).astype(
        jnp.float32
    )
    coupling = coupling - AGGREGATE_XCELLS * third_axis_count * (
        (x_gap == 0) & (y_gap == 1)
    ).astype(jnp.float32)
    identity = (position[:, None] == position[None, :]).astype(jnp.float32)
    diagonal = sum_values + face_count
    system = (
        coupling[None]
        + identity[None] * (diagonal[None, :] + volume * slot_shift[:, None])[:, None, :]
    )
    factor = jnp.linalg.cholesky(system)
    right_side = jnp.transpose(shared_right, (0, 2, 1))
    forward_sub = lax.linalg.triangular_solve(factor, right_side, left_side=True, lower=True)
    coarse = lax.linalg.triangular_solve(
        factor, forward_sub, left_side=True, lower=True, transpose_a=True
    )
    solved = jnp.transpose(coarse, (0, 2, 1))
    returned = lax.all_to_all(solved, ("sx", "sy"), split_axis=2, concat_axis=0, tiled=True)
    own_coarse = returned[:moment_count]
    local_part = jnp.transpose(own_coarse, (1, 0, 2)).reshape(
        2, moment_count, 1, first_axis_teams, 1, second_axis_teams, 1
    )
    spread_values = jnp.broadcast_to(
        local_part,
        (
            2,
            moment_count,
            third_axis_count,
            first_axis_teams,
            AGGREGATE_XCELLS,
            second_axis_teams,
            AGGREGATE_YCELLS,
        ),
    )
    present_guess = present_guess + spread_values.reshape(
        2, moment_count, third_axis_count, first_axis_count, second_axis_count
    )
    unrolled_array = present_guess.reshape(2, moment_count, unknowns_in_tile)

    def backward(running, segment, offset):
        return matmul(cos_rows, segment[0]) - matmul(sin_rows, segment[1])

    result = (
        backward(
            jnp.zeros((moment_count, unknowns_in_tile), jnp.float32),
            lax.all_gather(unrolled_array, "tm", axis=1, tiled=True),
            jnp.int32(0),
        )
        / cycle_duration
    )
    return result.reshape(driving_input.shape)


def time_tables(count):
    half = count // 2
    lane = np.arange(count)
    frequency = np.where(lane <= half, lane, lane - half)
    imaginary = lane > half
    moment = np.arange(count)
    angle = 2.0 * np.pi * (moment[:, None] * frequency[None, :] % count) / count
    forward = np.where(imaginary[None, :], -np.sin(angle), np.cos(angle))
    weight = np.where((lane == 0) | (lane == half), 1.0, 2.0) / count
    theta = 2.0 * np.pi * frequency / count
    signed = np.where(lane % half == 0, 0.0, np.sin(theta)) * np.where(lane < half, 1.0, -1.0)
    shift = np.zeros((8, count))
    shift[0] = 1.0 - np.cos(theta)
    shift[1] = signed
    return np.concatenate([forward, forward * weight[None, :], shift]).astype(np.float32)


def fused_kernel(
    sizes,
    rates_ref,
    field_hbm,
    regime_hbm,
    table_hbm,
    out_hbm,
    added_ref,
    field_ref,
    regime_ref,
    table_ref,
    rate_tiles,
    coarse_tiles,
    solved_tiles,
    layer_sums,
    iterate_0,
    iterate_1,
    iterate_2,
    iterate_3,
    lasts,
    x_edges,
    x_halos,
    y_edges,
    y_halos,
    load_sem,
    store_sem,
    last_send,
    last_recv,
    rate_send,
    rate_recv,
    coarse_send,
    coarse_recv,
    halo_send,
    halo_recv,
):
    teams, nsx, nsy, moments, nz, nx, lanes, width = sizes
    total = teams * moments
    strips = lanes // width
    plane = nz * nx
    spatial = nsx * nsy
    devices = teams * spatial
    highest = lax.Precision.HIGHEST
    tm = lax.axis_index("tm")
    ix = lax.axis_index("sx")
    iy = lax.axis_index("sy")
    here = ix * nsy + iy
    me = tm * spatial + here

    loads = [
        pltpu.make_async_copy(regime_hbm, regime_ref, load_sem.at[0]),
        pltpu.make_async_copy(field_hbm, field_ref, load_sem.at[1]),
        pltpu.make_async_copy(table_hbm, table_ref, load_sem.at[2]),
    ]
    for load in loads:
        load.start()

    def place(rank):
        return {
            "tm": rank // spatial,
            "sx": (rank % spatial) // nsy,
            "sy": rank % nsy,
        }

    barrier = pltpu.get_barrier_semaphore()

    def greet(offset, carry):
        pl.semaphore_signal(
            barrier,
            inc=1,
            device_id=place((me + offset) % devices),
            device_id_type=pl.DeviceIdType.MESH,
        )
        return carry

    lax.fori_loop(1, devices, greet, 0)

    loads[0].wait()
    rates = jnp.zeros(regime_ref.shape, jnp.float32)
    regime = regime_ref[...]
    for number in range(rates_ref.shape[0]):
        rates = rates + jnp.where(regime == number, rates_ref[number], 0.0)
    rate_tiles[here] = jnp.sum(rates, axis=0)
    decay = 1.0 / (rates + 7.0)
    decay_block = jnp.ones_like(decay)
    power, left = decay, moments
    while left:
        if left & 1:
            decay_block = decay_block * power
        power = power * power
        left //= 2
    decay_round = jnp.ones_like(decay)
    for _ in range(teams):
        decay_round = decay_round * decay_block
    closing = 1.0 / (1.0 - decay_round)

    has = (ix > 0, ix < nsx - 1, iy > 0, iy < nsy - 1)
    neighbour = (
        {"tm": tm, "sx": (ix + nsx - 1) % nsx, "sy": iy},
        {"tm": tm, "sx": (ix + 1) % nsx, "sy": iy},
        {"tm": tm, "sx": ix, "sy": (iy + nsy - 1) % nsy},
        {"tm": tm, "sx": ix, "sy": (iy + 1) % nsy},
    )
    for number in range(3):
        for side in range(4):

            @pl.when(jnp.logical_not(has[side]))
            def _(halo=(x_halos if side < 2 else y_halos).at[number, side % 2]):
                halo[...] = jnp.zeros(halo.shape, jnp.float32)

    def halo_copies(number):
        copies = []
        for side in range(4):
            if side < 2:
                source = x_edges.at[number, side]
                target = x_halos.at[number, 1 - side]
            else:
                source = y_edges.at[number]
                target = y_halos.at[number, 3 - side]
            copies.append(
                pltpu.make_async_remote_copy(
                    src_ref=source,
                    dst_ref=target,
                    send_sem=halo_send.at[number * 4 + side],
                    recv_sem=halo_recv.at[number * 4 + (side ^ 1)],
                    device_id=neighbour[side],
                    device_id_type=pl.DeviceIdType.MESH,
                )
            )
        return copies

    def exchange_start(number):
        for side, copy in enumerate(halo_copies(number)):

            @pl.when(has[side])
            def _(copy=copy):
                copy.start()

    def exchange_wait(number):
        copies = halo_copies(number)
        for side in range(4):

            @pl.when(has[side])
            def _(side=side):
                copies[side].wait_send()
                copies[side ^ 1].wait_recv()

    def rate_copy(offset):
        peer = (here + offset) % spatial
        return pltpu.make_async_remote_copy(
            src_ref=rate_tiles.at[here],
            dst_ref=rate_tiles.at[here],
            send_sem=rate_send.at[offset],
            recv_sem=rate_recv.at[offset],
            device_id={"tm": tm, "sx": peer // nsy, "sy": peer % nsy},
            device_id_type=pl.DeviceIdType.MESH,
        )

    def last_copy(number, offset):
        return pltpu.make_async_remote_copy(
            src_ref=lasts.at[number, tm],
            dst_ref=lasts.at[number, tm],
            send_sem=last_send.at[number * teams + offset],
            recv_sem=last_recv.at[number * teams + offset],
            device_id={"tm": (tm + offset) % teams, "sx": ix, "sy": iy},
            device_id_type=pl.DeviceIdType.MESH,
        )

    def cell(moment, z):
        return pl.ds(pl.multiple_of((moment * nz + z) * nx, nx), nx)

    iterates = (iterate_0, iterate_1, iterate_2, iterate_3)
    chunk = lanes // 2 // nz
    row_id = lax.broadcasted_iota(jnp.int32, (nx, lanes), 0)
    lane_id = lax.broadcasted_iota(jnp.int32, (nx, lanes), 1)
    first_row, last_row = row_id == 0, row_id == nx - 1
    first_lane, last_lane = lane_id == 0, lane_id == lanes - 1
    odd_lane = lane_id % 2 == 1
    pair = (lane_id + 1) % lanes // 2

    def recurrence(number):
        def body(block, state):
            if number:
                high = y_halos[number - 1, 1, block]
                low = pltpu.roll(y_halos[number - 1, 0, block], 2, 1)
                ends = jnp.where(odd_lane, low, high)
                old = iterates[number - 1]
            state = list(state)
            for inner in range(chunk):
                moment = block * chunk + inner
                if number:
                    cells = [old[cell(moment, z), :] for z in range(nz)]
                for z in range(nz):
                    values = field_ref[moment, z]
                    if number:
                        here_cell = cells[z]
                        slot = inner * nz + z
                        turned = pltpu.roll(ends, (lanes - 2 * slot - 1) % lanes, 1)
                        low_row = x_halos[number - 1, 0, moment, z : z + 1, :]
                        high_row = x_halos[number - 1, 1, moment, z : z + 1, :]
                        values = values + cells[z - 1] + cells[(z + 1) % nz]
                        values = values + jnp.where(
                            first_row, low_row, pltpu.roll(here_cell, 1, 0)
                        )
                        values = values + jnp.where(
                            last_row, high_row, pltpu.roll(here_cell, nx - 1, 0)
                        )
                        values = values + jnp.where(
                            first_lane, turned, pltpu.roll(here_cell, 1, 1)
                        )
                        values = values + jnp.where(
                            last_lane, turned, pltpu.roll(here_cell, lanes - 1, 1)
                        )
                    state[z] = decay[z] * (values + state[z])
                    iterates[number][cell(moment, z), :] = state[z]
            return tuple(state)

        start = tuple(jnp.zeros((nx, lanes), jnp.float32) for _ in range(nz))
        state = lax.fori_loop(0, moments // chunk, body, start)
        for z in range(nz):
            lasts[number, tm, z] = state[z]

    def history(number):
        value = lasts[number, tm]
        for offset in range(1, teams):
            value = lasts[number, (tm + offset) % teams] + decay_block * value
        return value * closing

    def complete(number, entry):
        def body(block, state):
            state = list(state)
            packed = jnp.zeros((nx, lanes), jnp.float32)
            for inner in range(chunk):
                moment = block * chunk + inner
                for z in range(nz):
                    state[z] = decay[z] * state[z]
                    values = iterates[number][cell(moment, z), :] + state[z]
                    iterates[number][cell(moment, z), :] = values
                    slot = inner * nz + z
                    packed = jnp.where(pair == slot, pltpu.roll(values, 2 * slot, 1), packed)
                for side, edge_row in enumerate((0, nx - 1)):
                    rows = pl.ds(moment * plane + edge_row, nz, stride=nx)
                    x_edges[number, side, moment] = iterates[number][rows, :]
            y_edges[number, block] = packed
            return tuple(state)

        lax.fori_loop(0, moments // chunk, body, tuple(entry[z] for z in range(nz)))

    loads[1].wait()
    recurrence(0)
    pl.semaphore_wait(barrier, devices - 1)
    for offset in range(1, teams):
        last_copy(0, offset).start()
    for offset in range(1, spatial):
        rate_copy(offset).start()
    for offset in range(1, teams):
        last_copy(0, offset).wait()
    complete(0, history(0))
    exchange_start(0)

    for offset in range(1, spatial):
        rate_copy(offset).wait()
    loads[2].wait()
    shift_real = table_ref[2 * total : 2 * total + 1, :]
    ncy = nsy * strips
    strip_block = lax.broadcasted_iota(jnp.int32, (nx, lanes), 1) // width
    faces = 2 * (width * nz + nx * nz)
    couple_x = -float(width * nz)
    couple_y = -float(nx * nz)
    unknowns = ncy * nsx
    band = [[None] * (nsx + 1) for _ in range(unknowns)]
    for gy in range(ncy):
        for gx in range(nsx):
            number = gy * nsx + gx
            tile = rate_tiles[gx * nsy + gy // strips]
            amount = jnp.sum(jnp.where(strip_block == gy % strips, tile, 0.0), axis=0, keepdims=True)
            amount = jnp.sum(amount, axis=1, keepdims=True)
            band[number][0] = amount + faces + float(nx * width * nz) * shift_real
            if gx + 1 < nsx:
                band[number][1] = jnp.full((1, total), couple_x, jnp.float32)
            if gy + 1 < ncy:
                extra = jnp.full((1, total), couple_y, jnp.float32)
                before = band[number][nsx]
                band[number][nsx] = extra if before is None else before + extra
    inverses = []
    ratios = []
    for i in range(unknowns):
        inverse = 1.0 / band[i][0]
        inverses.append(inverse)
        ratios.append([None] * (nsx + 1))
        for a in range(1, nsx + 1):
            if band[i][a] is None or i + a >= unknowns:
                continue
            ratio = band[i][a] * inverse
            ratios[i][a] = ratio
            for b in range(a, nsx + 1):
                if band[i][b] is None or i + b >= unknowns:
                    continue
                term = ratio * band[i][b]
                before = band[i + a][b - a]
                band[i + a][b - a] = -term if before is None else before - term


    exchange_wait(0)
    for number in range(1, 4):
        recurrence(number)
        for offset in range(1, teams):
            last_copy(number, offset).start()
        for offset in range(1, teams):
            last_copy(number, offset).wait()
        if number < 3:
            complete(number, history(number))
            exchange_start(number)
            exchange_wait(number)

    entry = history(3)

    def finish(moment, state):
        state = list(state)
        layer = jnp.zeros((nx, lanes), jnp.float32)
        for z in range(nz):
            state[z] = decay[z] * state[z]
            values = iterate_3[cell(moment, z), :] + state[z]
            iterate_3[cell(moment, z), :] = values
            layer = layer + (values - iterate_2[cell(moment, z), :])
        layer_sums[pl.ds(pl.multiple_of(moment * nx, nx), nx), :] = layer
        return tuple(state)

    lax.fori_loop(0, moments, finish, tuple(entry[z] for z in range(nz)), unroll=4)
    store = pltpu.make_async_copy(iterate_3, out_hbm, store_sem)
    store.start()
    by_row = [layer_sums[pl.ds(x, moments, stride=nx), :] for x in range(nx)]
    columns = sum(by_row[1:], by_row[0])
    moment_lane = lax.broadcasted_iota(jnp.int32, (moments, lanes), 1)
    balance = 4.0 * columns - by_row[0] - by_row[nx - 1]
    balance = balance + jnp.where(moment_lane > 0, pltpu.roll(columns, 1, 1), 0.0)
    balance = balance + jnp.where(
        moment_lane < lanes - 1, pltpu.roll(columns, lanes - 1, 1), 0.0
    )
    stacked = jnp.concatenate([balance, by_row[0], by_row[nx - 1], columns], axis=0)
    member = (lane_id // width == row_id).astype(jnp.float32)
    ends = jnp.where(
        row_id == 0, first_lane.astype(jnp.float32), last_lane.astype(jnp.float32)
    )
    ends = jnp.where(row_id < 2, ends, 0.0)

    def against(left_side, right_side):
        return lax.dot_general(
            left_side,
            right_side,
            (((1,), (1,)), ((), ())),
            precision=highest,
            preferred_element_type=jnp.float32,
        )

    coarse_tiles[me] = jnp.where(
        lane_id < 3 * moments, against(member, stacked), against(ends, stacked)
    )

    def coarse_copy(offset):
        return pltpu.make_async_remote_copy(
            src_ref=coarse_tiles.at[me],
            dst_ref=coarse_tiles.at[me],
            send_sem=coarse_send.at[offset],
            recv_sem=coarse_recv.at[offset],
            device_id=place((me + offset) % devices),
            device_id_type=pl.DeviceIdType.MESH,
        )

    def coarse_start(offset, carry):
        coarse_copy(offset).start()
        return carry

    def coarse_wait(offset, carry):
        coarse_copy(offset).wait()
        return carry

    lax.fori_loop(1, devices, coarse_start, 0)
    lax.fori_loop(1, devices, coarse_wait, 0)

    kinds = [[None] * spatial for _ in range(4)]
    quarter = lane_id // moments
    for slot in range(spatial):
        for kind in range(4):
            merged = None
            for team in range(teams):
                tile = coarse_tiles[team * spatial + slot]
                turn = (moments * (team - kind)) % lanes
                turned = pltpu.roll(tile, turn, 1) if turn else tile
                merged = turned if team == 0 else jnp.where(quarter == team, turned, merged)
            kinds[kind][slot] = merged
    tiles = []
    for gx in range(nsx):
        for gy in range(nsy):
            slot = gx * nsy + gy
            tile = kinds[0][slot]
            if gx + 1 < nsx:
                tile = tile + kinds[1][slot + nsy]
            if gx > 0:
                tile = tile + kinds[2][slot - nsy]
            if gy > 0:
                tile = tile + jnp.where(row_id == 0, kinds[3][slot - 1][1:2], 0.0)
            if gy + 1 < nsy:
                tile = tile + jnp.where(row_id == strips - 1, kinds[3][slot + 1][0:1], 0.0)
            tiles.append(tile)
    spectrum = jnp.dot(
        jnp.concatenate(tiles, axis=0),
        table_ref[0:total, :],
        precision=highest,
        preferred_element_type=jnp.float32,
    )
    right = []
    for gy in range(ncy):
        for gx in range(nsx):
            row = (gx * nsy + gy // strips) * nx + gy % strips
            right.append(spectrum[row : row + 1])
    for i in range(unknowns):
        for a in range(1, nsx + 1):
            if ratios[i][a] is not None:
                right[i + a] = right[i + a] - ratios[i][a] * right[i]
    for i in reversed(range(unknowns)):
        value = right[i] * inverses[i]
        for a in range(1, nsx + 1):
            if ratios[i][a] is not None:
                value = value - ratios[i][a] * right[i + a]
        right[i] = value
    for gx in range(nsx):
        for block in range(nsy):
            for d in range(strips):
                number = (block * strips + d) * nsx + gx
                solved_tiles[gx * nsy + block, d : d + 1, :] = right[number]
    own_rows = solved_tiles[here]
    spread = jnp.concatenate(
        [jnp.broadcast_to(own_rows[d : d + 1], (width, total)) for d in range(strips)], axis=0
    )
    own_moments = pl.ds(pl.multiple_of(total + tm * moments, moments), moments)
    added_ref[...] = against(table_ref[own_moments, :], spread)

    store.wait()


def local_fused(teams, nsx, nsy, driving_input, regime, reaction_rates):
    moments, nz, nx, lanes = driving_input.shape
    width = AGGREGATE_YCELLS
    total = teams * moments
    table = time_tables(total)
    sizes = (teams, nsx, nsy, moments, nz, nx, lanes, width)
    devices = teams * nsx * nsy
    blocks = 2 * moments * nz // lanes
    f32 = jnp.float32
    whole = pltpu.VMEM(driving_input.shape, f32)
    flat = pltpu.VMEM((moments * nz * nx, lanes), f32)
    in_hbm = pl.BlockSpec(memory_space=pltpu.HBM)
    dma = pltpu.SemaphoreType.DMA
    field, added = pl.pallas_call(
        functools.partial(fused_kernel, sizes),
        out_shape=(
            pltpu.VMEM((moments * nz * nx, lanes), f32),
            pltpu.VMEM((moments, lanes), f32),
        ),
        in_specs=[pl.BlockSpec(memory_space=pltpu.SMEM)] + [in_hbm] * 3,
        out_specs=(pl.BlockSpec(memory_space=pl.ANY), pl.BlockSpec(memory_space=pltpu.VMEM)),
        scratch_shapes=[
            whole,
            pltpu.VMEM(regime.shape, jnp.int32),
            pltpu.VMEM(table.shape, f32),
            pltpu.VMEM((nsx * nsy, nx, lanes), f32),
            pltpu.VMEM((devices, 8, total), f32),
            pltpu.VMEM((nsx * nsy, max(lanes // width, 8), total), f32),
            pltpu.VMEM((moments * nx, lanes), f32),
            flat,
            flat,
            flat,
            flat,
            pltpu.VMEM((4, teams, nz, nx, lanes), f32),
            pltpu.VMEM((3, 2, moments, nz, lanes), f32),
            pltpu.VMEM((3, 2, moments, nz, lanes), f32),
            pltpu.VMEM((3, blocks, nx, lanes), f32),
            pltpu.VMEM((3, 2, blocks, nx, lanes), f32),
            dma((3,)),
            dma,
            dma((4 * teams,)),
            dma((4 * teams,)),
            dma((nsx * nsy,)),
            dma((nsx * nsy,)),
            dma((devices,)),
            dma((devices,)),
            dma((12,)),
            dma((12,)),
        ],
        compiler_params=pltpu.CompilerParams(
            collective_id=0, has_side_effects=True, vmem_limit_bytes=62 * 1024 * 1024
        ),
    )(reaction_rates, driving_input, regime, jnp.asarray(table))
    return field.reshape(driving_input.shape) + added[:, None, None, :]


def local(driving_input, regime, reaction_rates):
    moments, nz, nx, lanes = driving_input.shape
    teams, nsx, nsy = (lax.axis_size(axis) for axis in ("tm", "sx", "sy"))
    strips = lanes // AGGREGATE_YCELLS
    whole_strips = nx == AGGREGATE_XCELLS and strips * AGGREGATE_YCELLS == lanes and strips <= 8
    tiled = nx == 8 and nz == 8 and lanes == 128 and moments % 8 == 0
    if whole_strips and tiled and teams * moments == 128 and 4 * moments == 128 and SWEEPS == 4:
        return local_fused(teams, nsx, nsy, driving_input, regime, reaction_rates)
    return local_general(driving_input, regime, reaction_rates)


def solution(mesh):
    placed = (P("tm", None, "sx", "sy"), P(None, "sx", "sy"), P())
    return jax.shard_map(
        local, mesh=mesh, in_specs=placed, out_specs=P("tm", None, "sx", "sy"), check_vma=False
    )
```

```python
import functools

import jax
import jax.numpy as jnp
import numpy as np
from jax import lax
from jax.experimental import pallas as pl
from jax.experimental.pallas import tpu as pltpu
from jax.sharding import PartitionSpec as P

AGGREGATE_XCELLS = 8
AGGREGATE_YCELLS = 32
SWEEPS = 4


TWO_PI = 2.0 * 3.141592653589793


def extended(block, sides, width):
    for axis, dim in sides:
        count = lax.axis_size(axis)
        forward = [(i, i + 1) for i in range(count - 1)]
        backward = [(target, source) for source, target in forward]
        low = lax.ppermute(
            lax.slice_in_dim(block, block.shape[dim] - width, None, axis=dim), axis, forward
        )
        high = lax.ppermute(lax.slice_in_dim(block, 0, width, axis=dim), axis, backward)
        block = jnp.concatenate([low, block, high], axis=dim)
    return block


def angle_table(row_index, col_index, cycle_duration):
    product = row_index[:, None] * col_index[None, :] % cycle_duration
    angles = product.astype(jnp.float32) * (TWO_PI / cycle_duration)
    return (jnp.cos(angles), jnp.sin(angles))


def matmul(left_side, right_side):
    return jnp.dot(
        left_side, right_side, precision=lax.Precision.HIGHEST, preferred_element_type=jnp.float32
    )


def complex_mul(left_real, left_imag, pair):
    return jnp.stack(
        [left_real * pair[0] - left_imag * pair[1], left_real * pair[1] + left_imag * pair[0]]
    )


def neighbors(present_guess):
    padded = extended(present_guess, (("sx", 3), ("sy", 4)), 1)
    running = padded[:, :, :, 2:, 1:-1] + padded[:, :, :, :-2, 1:-1]
    running = running + padded[:, :, :, 1:-1, 2:] + padded[:, :, :, 1:-1, :-2]
    running = running + jnp.roll(present_guess, 1, axis=2) + jnp.roll(present_guess, -1, axis=2)
    return running


def local_general(driving_input, regime, reaction_rates):
    moment_count, third_axis_count, first_axis_count, second_axis_count = driving_input.shape
    temporal_spacing = lax.axis_size("tm")
    sy_size = lax.axis_size("sy")
    cycle_duration = moment_count * temporal_spacing
    unknowns_in_tile = third_axis_count * first_axis_count * second_axis_count
    processor_lines = driving_input.reshape(moment_count, unknowns_in_tile)
    owned_slice_number = lax.axis_index("tm") * moment_count + jnp.arange(
        moment_count, dtype=jnp.int32
    )
    all_index = jnp.arange(cycle_duration, dtype=jnp.int32)
    cos_rows, sin_rows = angle_table(owned_slice_number, all_index, cycle_duration)

    def forward(running, segment, offset):
        return jnp.stack([matmul(cos_rows, segment), -matmul(sin_rows, segment)])

    eigen_spectra = forward(
        jnp.zeros((2, moment_count, unknowns_in_tile), jnp.float32),
        lax.all_gather(processor_lines, "tm", axis=0, tiled=True),
        jnp.int32(0),
    )
    source_term = eigen_spectra.reshape(
        2, moment_count, third_axis_count, first_axis_count, second_axis_count
    )
    phase_angle = owned_slice_number.astype(jnp.float32) * (TWO_PI / cycle_duration)
    shift_real = (1.0 - jnp.cos(phase_angle))[:, None, None, None]
    shift_imag = jnp.sin(phase_angle)[:, None, None, None]
    reaction = jnp.zeros(regime.shape, jnp.float32)
    for regime_no in range(reaction_rates.shape[0]):
        reaction = reaction + jnp.where(
            regime == regime_no, reaction_rates[regime_no], jnp.zeros((), jnp.float32)
        )
    diag_real = reaction[None] + 6.0 + shift_real
    diag_imag = jnp.zeros_like(diag_real) + shift_imag
    modulus = diag_real * diag_real + diag_imag * diag_imag
    inverse_real = diag_real / modulus
    inverse_imag = -diag_imag / modulus
    present_guess = complex_mul(inverse_real, inverse_imag, source_term)
    for sweep_no in range(SWEEPS - 1):
        present_guess = complex_mul(
            inverse_real, inverse_imag, source_term + neighbors(present_guess)
        )
    applied = complex_mul(diag_real, diag_imag, present_guess) - neighbors(present_guess)
    residual = source_term - applied
    first_axis_teams = first_axis_count // AGGREGATE_XCELLS
    second_axis_teams = second_axis_count // AGGREGATE_YCELLS
    per_device = first_axis_teams * second_axis_teams

    def aggregate(values):
        leading = values.shape[:-3]
        blocks = values.reshape(
            leading
            + (
                third_axis_count,
                first_axis_teams,
                AGGREGATE_XCELLS,
                second_axis_teams,
                AGGREGATE_YCELLS,
            )
        )
        return jnp.sum(blocks, axis=(-5, -3, -1)).reshape(leading + (per_device,))

    coarse_right = jnp.transpose(aggregate(residual), (1, 0, 2))
    rate_sums = aggregate(reaction)
    shift_column = 1.0 - jnp.cos(phase_angle)
    face_count = 2 * (AGGREGATE_YCELLS * third_axis_count + AGGREGATE_XCELLS * third_axis_count)
    volume = AGGREGATE_XCELLS * AGGREGATE_YCELLS * third_axis_count
    spatial = lax.axis_size("sx") * sy_size
    slot_count = -(-moment_count // spatial)
    padding_rows = slot_count * spatial - moment_count
    padded_right = jnp.pad(coarse_right, ((0, padding_rows), (0, 0), (0, 0)))
    sum_copies = jnp.broadcast_to(rate_sums[None, None, :], (spatial, 1, per_device))
    shared_right, shared_sums = (
        lax.all_to_all(padded_right, ("sx", "sy"), split_axis=0, concat_axis=2, tiled=True),
        lax.all_to_all(sum_copies, ("sx", "sy"), split_axis=0, concat_axis=2, tiled=True),
    )
    spatial_rank = lax.axis_index("sx") * sy_size + lax.axis_index("sy")
    padded_shift = jnp.pad(shift_column, (0, padding_rows))
    slot_shift = lax.dynamic_slice_in_dim(padded_shift, spatial_rank * slot_count, slot_count, 0)
    sum_values = shared_sums[0, 0]
    coarse_total = sum_values.shape[0]
    position = jnp.arange(coarse_total, dtype=jnp.int32)
    device = position // per_device
    within = position % per_device
    coarse_x = device // sy_size * first_axis_teams + within // second_axis_teams
    coarse_y = device % sy_size * second_axis_teams + within % second_axis_teams
    x_gap = jnp.abs(coarse_x[:, None] - coarse_x[None, :])
    y_gap = jnp.abs(coarse_y[:, None] - coarse_y[None, :])
    coupling = -(AGGREGATE_YCELLS * third_axis_count) * ((x_gap == 1) & (y_gap == 0)).astype(
        jnp.float32
    )
    coupling = coupling - AGGREGATE_XCELLS * third_axis_count * (
        (x_gap == 0) & (y_gap == 1)
    ).astype(jnp.float32)
    identity = (position[:, None] == position[None, :]).astype(jnp.float32)
    diagonal = sum_values + face_count
    system = (
        coupling[None]
        + identity[None] * (diagonal[None, :] + volume * slot_shift[:, None])[:, None, :]
    )
    factor = jnp.linalg.cholesky(system)
    right_side = jnp.transpose(shared_right, (0, 2, 1))
    forward_sub = lax.linalg.triangular_solve(factor, right_side, left_side=True, lower=True)
    coarse = lax.linalg.triangular_solve(
        factor, forward_sub, left_side=True, lower=True, transpose_a=True
    )
    solved = jnp.transpose(coarse, (0, 2, 1))
    returned = lax.all_to_all(solved, ("sx", "sy"), split_axis=2, concat_axis=0, tiled=True)
    own_coarse = returned[:moment_count]
    local_part = jnp.transpose(own_coarse, (1, 0, 2)).reshape(
        2, moment_count, 1, first_axis_teams, 1, second_axis_teams, 1
    )
    spread_values = jnp.broadcast_to(
        local_part,
        (
            2,
            moment_count,
            third_axis_count,
            first_axis_teams,
            AGGREGATE_XCELLS,
            second_axis_teams,
            AGGREGATE_YCELLS,
        ),
    )
    present_guess = present_guess + spread_values.reshape(
        2, moment_count, third_axis_count, first_axis_count, second_axis_count
    )
    unrolled_array = present_guess.reshape(2, moment_count, unknowns_in_tile)

    def backward(running, segment, offset):
        return matmul(cos_rows, segment[0]) - matmul(sin_rows, segment[1])

    result = (
        backward(
            jnp.zeros((moment_count, unknowns_in_tile), jnp.float32),
            lax.all_gather(unrolled_array, "tm", axis=1, tiled=True),
            jnp.int32(0),
        )
        / cycle_duration
    )
    return result.reshape(driving_input.shape)


def time_tables(count):
    half = count // 2
    lane = np.arange(count)
    frequency = np.where(lane <= half, lane, lane - half)
    imaginary = lane > half
    moment = np.arange(count)
    angle = 2.0 * np.pi * (moment[:, None] * frequency[None, :] % count) / count
    forward = np.where(imaginary[None, :], -np.sin(angle), np.cos(angle))
    weight = np.where((lane == 0) | (lane == half), 1.0, 2.0) / count
    theta = 2.0 * np.pi * frequency / count
    signed = np.where(lane % half == 0, 0.0, np.sin(theta)) * np.where(lane < half, 1.0, -1.0)
    shift = np.zeros((8, count))
    shift[0] = 1.0 - np.cos(theta)
    shift[1] = signed
    return np.concatenate([forward, forward * weight[None, :], shift]).astype(np.float32)


def fused_kernel(
    sizes,
    rates_ref,
    field_hbm,
    regime_hbm,
    table_hbm,
    out_hbm,
    added_ref,
    field_ref,
    regime_ref,
    table_ref,
    rate_tiles,
    coarse_tiles,
    solved_tiles,
    layer_sums,
    iterate_0,
    iterate_1,
    iterate_2,
    iterate_3,
    lasts,
    x_edges,
    x_halos,
    y_edges,
    y_halos,
    load_sem,
    store_sem,
    last_send,
    last_recv,
    rate_send,
    rate_recv,
    coarse_send,
    coarse_recv,
    halo_send,
    halo_recv,
):
    teams, nsx, nsy, moments, nz, nx, lanes, width = sizes
    total = teams * moments
    strips = lanes // width
    plane = nz * nx
    spatial = nsx * nsy
    devices = teams * spatial
    highest = lax.Precision.HIGHEST
    tm = lax.axis_index("tm")
    ix = lax.axis_index("sx")
    iy = lax.axis_index("sy")
    here = ix * nsy + iy
    me = tm * spatial + here

    loads = [
        pltpu.make_async_copy(regime_hbm, regime_ref, load_sem.at[0]),
        pltpu.make_async_copy(field_hbm, field_ref, load_sem.at[1]),
        pltpu.make_async_copy(table_hbm, table_ref, load_sem.at[2]),
    ]
    for load in loads:
        load.start()

    def place(rank):
        return {
            "tm": rank // spatial,
            "sx": (rank % spatial) // nsy,
            "sy": rank % nsy,
        }

    barrier = pltpu.get_barrier_semaphore()

    def greet(offset, carry):
        pl.semaphore_signal(
            barrier,
            inc=1,
            device_id=place((me + offset) % devices),
            device_id_type=pl.DeviceIdType.MESH,
        )
        return carry

    lax.fori_loop(1, devices, greet, 0)

    loads[0].wait()
    rates = jnp.zeros(regime_ref.shape, jnp.float32)
    regime = regime_ref[...]
    for number in range(rates_ref.shape[0]):
        rates = rates + jnp.where(regime == number, rates_ref[number], 0.0)
    rate_tiles[here] = jnp.sum(rates, axis=0)
    decay = 1.0 / (rates + 7.0)
    decay_block = jnp.ones_like(decay)
    power, left = decay, moments
    while left:
        if left & 1:
            decay_block = decay_block * power
        power = power * power
        left //= 2
    decay_round = jnp.ones_like(decay)
    for _ in range(teams):
        decay_round = decay_round * decay_block
    closing = 1.0 / (1.0 - decay_round)

    has = (ix > 0, ix < nsx - 1, iy > 0, iy < nsy - 1)
    neighbour = (
        {"tm": tm, "sx": (ix + nsx - 1) % nsx, "sy": iy},
        {"tm": tm, "sx": (ix + 1) % nsx, "sy": iy},
        {"tm": tm, "sx": ix, "sy": (iy + nsy - 1) % nsy},
        {"tm": tm, "sx": ix, "sy": (iy + 1) % nsy},
    )
    for number in range(3):
        for side in range(4):

            @pl.when(jnp.logical_not(has[side]))
            def _(halo=(x_halos if side < 2 else y_halos).at[number, side % 2]):
                halo[...] = jnp.zeros(halo.shape, jnp.float32)

    def halo_copies(number):
        copies = []
        for side in range(4):
            if side < 2:
                source = x_edges.at[number, side]
                target = x_halos.at[number, 1 - side]
            else:
                source = y_edges.at[number]
                target = y_halos.at[number, 3 - side]
            copies.append(
                pltpu.make_async_remote_copy(
                    src_ref=source,
                    dst_ref=target,
                    send_sem=halo_send.at[number * 4 + side],
                    recv_sem=halo_recv.at[number * 4 + (side ^ 1)],
                    device_id=neighbour[side],
                    device_id_type=pl.DeviceIdType.MESH,
                )
            )
        return copies

    def exchange_start(number):
        for side, copy in enumerate(halo_copies(number)):

            @pl.when(has[side])
            def _(copy=copy):
                copy.start()

    def exchange_wait(number):
        copies = halo_copies(number)
        for side in range(4):

            @pl.when(has[side])
            def _(side=side):
                copies[side].wait_send()
                copies[side ^ 1].wait_recv()

    def rate_copy(offset):
        peer = (here + offset) % spatial
        return pltpu.make_async_remote_copy(
            src_ref=rate_tiles.at[here],
            dst_ref=rate_tiles.at[here],
            send_sem=rate_send.at[offset],
            recv_sem=rate_recv.at[offset],
            device_id={"tm": tm, "sx": peer // nsy, "sy": peer % nsy},
            device_id_type=pl.DeviceIdType.MESH,
        )

    part_planes = nz // 2
    parts = (0, 1)

    def planes(part):
        return range(part * part_planes, (part + 1) * part_planes)

    def last_copy(number, part, offset):
        block = lasts.at[number, tm, pl.ds(part * part_planes, part_planes)]
        return pltpu.make_async_remote_copy(
            src_ref=block,
            dst_ref=block,
            send_sem=last_send.at[(number * 2 + part) * teams + offset],
            recv_sem=last_recv.at[(number * 2 + part) * teams + offset],
            device_id={"tm": (tm + offset) % teams, "sx": ix, "sy": iy},
            device_id_type=pl.DeviceIdType.MESH,
        )

    def cell(moment, z):
        return pl.ds(pl.multiple_of((moment * nz + z) * nx, nx), nx)

    iterates = (iterate_0, iterate_1, iterate_2, iterate_3)
    chunk = lanes // 2 // nz
    row_id = lax.broadcasted_iota(jnp.int32, (nx, lanes), 0)
    lane_id = lax.broadcasted_iota(jnp.int32, (nx, lanes), 1)
    first_row, last_row = row_id == 0, row_id == nx - 1
    first_lane, last_lane = lane_id == 0, lane_id == lanes - 1
    odd_lane = lane_id % 2 == 1
    pair = (lane_id + 1) % lanes // 2

    def recurrence(number, part):
        def body(block, state):
            if number:
                high = y_halos[number - 1, 1, block]
                low = pltpu.roll(y_halos[number - 1, 0, block], 2, 1)
                ends = jnp.where(odd_lane, low, high)
                old = iterates[number - 1]
            state = list(state)
            for inner in range(chunk):
                moment = block * chunk + inner
                if number:
                    cells = {
                        z % nz: old[cell(moment, z % nz), :]
                        for z in range(part * part_planes - 1, (part + 1) * part_planes + 1)
                    }
                for number_in, z in enumerate(planes(part)):
                    values = field_ref[moment, z]
                    if number:
                        here_cell = cells[z]
                        slot = inner * nz + z
                        turned = pltpu.roll(ends, (lanes - 2 * slot - 1) % lanes, 1)
                        low_row = x_halos[number - 1, 0, moment, z : z + 1, :]
                        high_row = x_halos[number - 1, 1, moment, z : z + 1, :]
                        values = values + cells[(z - 1) % nz] + cells[(z + 1) % nz]
                        values = values + jnp.where(
                            first_row, low_row, pltpu.roll(here_cell, 1, 0)
                        )
                        values = values + jnp.where(
                            last_row, high_row, pltpu.roll(here_cell, nx - 1, 0)
                        )
                        values = values + jnp.where(
                            first_lane, turned, pltpu.roll(here_cell, 1, 1)
                        )
                        values = values + jnp.where(
                            last_lane, turned, pltpu.roll(here_cell, lanes - 1, 1)
                        )
                    state[number_in] = decay[z] * (values + state[number_in])
                    iterates[number][cell(moment, z), :] = state[number_in]
            return tuple(state)

        start = tuple(jnp.zeros((nx, lanes), jnp.float32) for _ in planes(part))
        state = lax.fori_loop(0, moments // chunk, body, start)
        for number_in, z in enumerate(planes(part)):
            lasts[number, tm, z] = state[number_in]
        for offset in range(1, teams):
            last_copy(number, part, offset).start()

    def history(number, part):
        at = slice(part * part_planes, (part + 1) * part_planes)
        value = lasts[number, tm, at]
        for offset in range(1, teams):
            value = lasts[number, (tm + offset) % teams, at] + decay_block[at] * value
        return value * closing[at]

    def complete(number, part):
        for offset in range(1, teams):
            last_copy(number, part, offset).wait()
        entry = history(number, part)

        def body(block, state):
            state = list(state)
            packed = y_edges[number, block] if part else jnp.zeros((nx, lanes), jnp.float32)
            for inner in range(chunk):
                moment = block * chunk + inner
                for number_in, z in enumerate(planes(part)):
                    state[number_in] = decay[z] * state[number_in]
                    values = iterates[number][cell(moment, z), :] + state[number_in]
                    iterates[number][cell(moment, z), :] = values
                    slot = inner * nz + z
                    packed = jnp.where(pair == slot, pltpu.roll(values, 2 * slot, 1), packed)
                for side, edge_row in enumerate((0, nx - 1) if part else ()):
                    rows = pl.ds(moment * plane + edge_row, nz, stride=nx)
                    x_edges[number, side, moment] = iterates[number][rows, :]
            y_edges[number, block] = packed
            return tuple(state)

        lax.fori_loop(0, moments // chunk, body, tuple(entry[z] for z in range(part_planes)))

    loads[1].wait()
    pl.semaphore_wait(barrier, devices - 1)
    for part in parts:
        recurrence(0, part)
    for offset in range(1, spatial):
        rate_copy(offset).start()
    for part in parts:
        complete(0, part)
    exchange_start(0)
    for offset in range(1, spatial):
        rate_copy(offset).wait()
    loads[2].wait()
    shift_real = table_ref[2 * total : 2 * total + 1, :]
    ncy = nsy * strips
    strip_block = lax.broadcasted_iota(jnp.int32, (nx, lanes), 1) // width
    faces = 2 * (width * nz + nx * nz)
    couple_x = -float(width * nz)
    couple_y = -float(nx * nz)
    unknowns = ncy * nsx
    band = [[None] * (nsx + 1) for _ in range(unknowns)]
    for gy in range(ncy):
        for gx in range(nsx):
            number = gy * nsx + gx
            tile = rate_tiles[gx * nsy + gy // strips]
            amount = jnp.sum(jnp.where(strip_block == gy % strips, tile, 0.0), axis=0, keepdims=True)
            amount = jnp.sum(amount, axis=1, keepdims=True)
            band[number][0] = amount + faces + float(nx * width * nz) * shift_real
            if gx + 1 < nsx:
                band[number][1] = jnp.full((1, total), couple_x, jnp.float32)
            if gy + 1 < ncy:
                extra = jnp.full((1, total), couple_y, jnp.float32)
                before = band[number][nsx]
                band[number][nsx] = extra if before is None else before + extra
    inverses = []
    ratios = []

    def factor(count):
        for i in range(len(inverses), min(unknowns, len(inverses) + count)):
            inverse = 1.0 / band[i][0]
            inverses.append(inverse)
            ratios.append([None] * (nsx + 1))
            for a in range(1, nsx + 1):
                if band[i][a] is None or i + a >= unknowns:
                    continue
                ratio = band[i][a] * inverse
                ratios[i][a] = ratio
                for b in range(a, nsx + 1):
                    if band[i][b] is None or i + b >= unknowns:
                        continue
                    term = ratio * band[i][b]
                    before = band[i + a][b - a]
                    band[i + a][b - a] = -term if before is None else before - term


    exchange_wait(0)
    share = -(-unknowns // 2)
    for number in range(1, 4):
        for part in parts:
            recurrence(number, part)
        if number < 3:
            for part in parts:
                complete(number, part)
            exchange_start(number)
            factor(share)
            exchange_wait(number)
    for part in parts:
        for offset in range(1, teams):
            last_copy(3, part, offset).wait()
    entry = jnp.concatenate([history(3, part) for part in parts], axis=0)

    def finish(moment, state):
        state = list(state)
        layer = jnp.zeros((nx, lanes), jnp.float32)
        for z in range(nz):
            state[z] = decay[z] * state[z]
            values = iterate_3[cell(moment, z), :] + state[z]
            iterate_3[cell(moment, z), :] = values
            layer = layer + (values - iterate_2[cell(moment, z), :])
        layer_sums[pl.ds(pl.multiple_of(moment * nx, nx), nx), :] = layer
        return tuple(state)

    lax.fori_loop(0, moments, finish, tuple(entry[z] for z in range(nz)), unroll=4)
    store = pltpu.make_async_copy(iterate_3, out_hbm, store_sem)
    store.start()
    by_row = [layer_sums[pl.ds(x, moments, stride=nx), :] for x in range(nx)]
    columns = sum(by_row[1:], by_row[0])
    moment_lane = lax.broadcasted_iota(jnp.int32, (moments, lanes), 1)
    balance = 4.0 * columns - by_row[0] - by_row[nx - 1]
    balance = balance + jnp.where(moment_lane > 0, pltpu.roll(columns, 1, 1), 0.0)
    balance = balance + jnp.where(
        moment_lane < lanes - 1, pltpu.roll(columns, lanes - 1, 1), 0.0
    )
    stacked = jnp.concatenate([balance, by_row[0], by_row[nx - 1], columns], axis=0)
    member = (lane_id // width == row_id).astype(jnp.float32)
    ends = jnp.where(
        row_id == 0, first_lane.astype(jnp.float32), last_lane.astype(jnp.float32)
    )
    ends = jnp.where(row_id < 2, ends, 0.0)

    def against(left_side, right_side):
        return lax.dot_general(
            left_side,
            right_side,
            (((1,), (1,)), ((), ())),
            precision=highest,
            preferred_element_type=jnp.float32,
        )

    coarse_tiles[me] = jnp.where(
        lane_id < 3 * moments, against(member, stacked), against(ends, stacked)
    )

    def coarse_copy(offset):
        return pltpu.make_async_remote_copy(
            src_ref=coarse_tiles.at[me],
            dst_ref=coarse_tiles.at[me],
            send_sem=coarse_send.at[offset],
            recv_sem=coarse_recv.at[offset],
            device_id=place((me + offset) % devices),
            device_id_type=pl.DeviceIdType.MESH,
        )

    def coarse_start(offset, carry):
        coarse_copy(offset).start()
        return carry

    def coarse_wait(offset, carry):
        coarse_copy(offset).wait()
        return carry

    lax.fori_loop(1, devices, coarse_start, 0)
    lax.fori_loop(1, devices, coarse_wait, 0)

    kinds = [[None] * spatial for _ in range(4)]
    quarter = lane_id // moments
    for slot in range(spatial):
        for kind in range(4):
            merged = None
            for team in range(teams):
                tile = coarse_tiles[team * spatial + slot]
                turn = (moments * (team - kind)) % lanes
                turned = pltpu.roll(tile, turn, 1) if turn else tile
                merged = turned if team == 0 else jnp.where(quarter == team, turned, merged)
            kinds[kind][slot] = merged
    tiles = []
    for gx in range(nsx):
        for gy in range(nsy):
            slot = gx * nsy + gy
            tile = kinds[0][slot]
            if gx + 1 < nsx:
                tile = tile + kinds[1][slot + nsy]
            if gx > 0:
                tile = tile + kinds[2][slot - nsy]
            if gy > 0:
                tile = tile + jnp.where(row_id == 0, kinds[3][slot - 1][1:2], 0.0)
            if gy + 1 < nsy:
                tile = tile + jnp.where(row_id == strips - 1, kinds[3][slot + 1][0:1], 0.0)
            tiles.append(tile)
    spectrum = jnp.dot(
        jnp.concatenate(tiles, axis=0),
        table_ref[0:total, :],
        precision=highest,
        preferred_element_type=jnp.float32,
    )
    right = []
    for gy in range(ncy):
        for gx in range(nsx):
            row = (gx * nsy + gy // strips) * nx + gy % strips
            right.append(spectrum[row : row + 1])
    for i in range(unknowns):
        for a in range(1, nsx + 1):
            if ratios[i][a] is not None:
                right[i + a] = right[i + a] - ratios[i][a] * right[i]
    for i in reversed(range(unknowns)):
        value = right[i] * inverses[i]
        for a in range(1, nsx + 1):
            if ratios[i][a] is not None:
                value = value - ratios[i][a] * right[i + a]
        right[i] = value
    for gx in range(nsx):
        for block in range(nsy):
            for d in range(strips):
                number = (block * strips + d) * nsx + gx
                solved_tiles[gx * nsy + block, d : d + 1, :] = right[number]
    own_rows = solved_tiles[here]
    spread = jnp.concatenate(
        [jnp.broadcast_to(own_rows[d : d + 1], (width, total)) for d in range(strips)], axis=0
    )
    own_moments = pl.ds(pl.multiple_of(total + tm * moments, moments), moments)
    added_ref[...] = against(table_ref[own_moments, :], spread)

    store.wait()


def local_fused(teams, nsx, nsy, driving_input, regime, reaction_rates):
    moments, nz, nx, lanes = driving_input.shape
    width = AGGREGATE_YCELLS
    total = teams * moments
    table = time_tables(total)
    sizes = (teams, nsx, nsy, moments, nz, nx, lanes, width)
    devices = teams * nsx * nsy
    blocks = 2 * moments * nz // lanes
    f32 = jnp.float32
    whole = pltpu.VMEM(driving_input.shape, f32)
    flat = pltpu.VMEM((moments * nz * nx, lanes), f32)
    in_hbm = pl.BlockSpec(memory_space=pltpu.HBM)
    dma = pltpu.SemaphoreType.DMA
    field, added = pl.pallas_call(
        functools.partial(fused_kernel, sizes),
        out_shape=(
            pltpu.VMEM((moments * nz * nx, lanes), f32),
            pltpu.VMEM((moments, lanes), f32),
        ),
        in_specs=[pl.BlockSpec(memory_space=pltpu.SMEM)] + [in_hbm] * 3,
        out_specs=(pl.BlockSpec(memory_space=pl.ANY), pl.BlockSpec(memory_space=pltpu.VMEM)),
        scratch_shapes=[
            whole,
            pltpu.VMEM(regime.shape, jnp.int32),
            pltpu.VMEM(table.shape, f32),
            pltpu.VMEM((nsx * nsy, nx, lanes), f32),
            pltpu.VMEM((devices, 8, total), f32),
            pltpu.VMEM((nsx * nsy, max(lanes // width, 8), total), f32),
            pltpu.VMEM((moments * nx, lanes), f32),
            flat,
            flat,
            flat,
            flat,
            pltpu.VMEM((4, teams, nz, nx, lanes), f32),
            pltpu.VMEM((3, 2, moments, nz, lanes), f32),
            pltpu.VMEM((3, 2, moments, nz, lanes), f32),
            pltpu.VMEM((3, blocks, nx, lanes), f32),
            pltpu.VMEM((3, 2, blocks, nx, lanes), f32),
            dma((3,)),
            dma,
            dma((8 * teams,)),
            dma((8 * teams,)),
            dma((nsx * nsy,)),
            dma((nsx * nsy,)),
            dma((devices,)),
            dma((devices,)),
            dma((12,)),
            dma((12,)),
        ],
        compiler_params=pltpu.CompilerParams(
            collective_id=0, has_side_effects=True, vmem_limit_bytes=62 * 1024 * 1024
        ),
    )(reaction_rates, driving_input, regime, jnp.asarray(table))
    return field.reshape(driving_input.shape) + added[:, None, None, :]


def local(driving_input, regime, reaction_rates):
    moments, nz, nx, lanes = driving_input.shape
    teams, nsx, nsy = (lax.axis_size(axis) for axis in ("tm", "sx", "sy"))
    strips = lanes // AGGREGATE_YCELLS
    whole_strips = nx == AGGREGATE_XCELLS and strips * AGGREGATE_YCELLS == lanes and strips <= 8
    tiled = nx == 8 and nz == 8 and lanes == 128 and moments % 8 == 0
    if whole_strips and tiled and teams * moments == 128 and 4 * moments == 128 and SWEEPS == 4:
        return local_fused(teams, nsx, nsy, driving_input, regime, reaction_rates)
    return local_general(driving_input, regime, reaction_rates)


def solution(mesh):
    placed = (P("tm", None, "sx", "sy"), P(None, "sx", "sy"), P())
    return jax.shard_map(
        local, mesh=mesh, in_specs=placed, out_specs=P("tm", None, "sx", "sy"), check_vma=False
    )
```

```python
import functools

import jax
import jax.numpy as jnp
import numpy as np
from jax import lax
from jax.experimental import pallas as pl
from jax.experimental.pallas import tpu as pltpu
from jax.sharding import PartitionSpec as P

AGGREGATE_XCELLS = 8
AGGREGATE_YCELLS = 32
SWEEPS = 4


TWO_PI = 2.0 * 3.141592653589793


def extended(block, sides, width):
    for axis, dim in sides:
        count = lax.axis_size(axis)
        forward = [(i, i + 1) for i in range(count - 1)]
        backward = [(target, source) for source, target in forward]
        low = lax.ppermute(
            lax.slice_in_dim(block, block.shape[dim] - width, None, axis=dim), axis, forward
        )
        high = lax.ppermute(lax.slice_in_dim(block, 0, width, axis=dim), axis, backward)
        block = jnp.concatenate([low, block, high], axis=dim)
    return block


def angle_table(row_index, col_index, cycle_duration):
    product = row_index[:, None] * col_index[None, :] % cycle_duration
    angles = product.astype(jnp.float32) * (TWO_PI / cycle_duration)
    return (jnp.cos(angles), jnp.sin(angles))


def matmul(left_side, right_side):
    return jnp.dot(
        left_side, right_side, precision=lax.Precision.HIGHEST, preferred_element_type=jnp.float32
    )


def complex_mul(left_real, left_imag, pair):
    return jnp.stack(
        [left_real * pair[0] - left_imag * pair[1], left_real * pair[1] + left_imag * pair[0]]
    )


def neighbors(present_guess):
    padded = extended(present_guess, (("sx", 3), ("sy", 4)), 1)
    running = padded[:, :, :, 2:, 1:-1] + padded[:, :, :, :-2, 1:-1]
    running = running + padded[:, :, :, 1:-1, 2:] + padded[:, :, :, 1:-1, :-2]
    running = running + jnp.roll(present_guess, 1, axis=2) + jnp.roll(present_guess, -1, axis=2)
    return running


def local_general(driving_input, regime, reaction_rates):
    moment_count, third_axis_count, first_axis_count, second_axis_count = driving_input.shape
    temporal_spacing = lax.axis_size("tm")
    sy_size = lax.axis_size("sy")
    cycle_duration = moment_count * temporal_spacing
    unknowns_in_tile = third_axis_count * first_axis_count * second_axis_count
    processor_lines = driving_input.reshape(moment_count, unknowns_in_tile)
    owned_slice_number = lax.axis_index("tm") * moment_count + jnp.arange(
        moment_count, dtype=jnp.int32
    )
    all_index = jnp.arange(cycle_duration, dtype=jnp.int32)
    cos_rows, sin_rows = angle_table(owned_slice_number, all_index, cycle_duration)

    def forward(running, segment, offset):
        return jnp.stack([matmul(cos_rows, segment), -matmul(sin_rows, segment)])

    eigen_spectra = forward(
        jnp.zeros((2, moment_count, unknowns_in_tile), jnp.float32),
        lax.all_gather(processor_lines, "tm", axis=0, tiled=True),
        jnp.int32(0),
    )
    source_term = eigen_spectra.reshape(
        2, moment_count, third_axis_count, first_axis_count, second_axis_count
    )
    phase_angle = owned_slice_number.astype(jnp.float32) * (TWO_PI / cycle_duration)
    shift_real = (1.0 - jnp.cos(phase_angle))[:, None, None, None]
    shift_imag = jnp.sin(phase_angle)[:, None, None, None]
    reaction = jnp.zeros(regime.shape, jnp.float32)
    for regime_no in range(reaction_rates.shape[0]):
        reaction = reaction + jnp.where(
            regime == regime_no, reaction_rates[regime_no], jnp.zeros((), jnp.float32)
        )
    diag_real = reaction[None] + 6.0 + shift_real
    diag_imag = jnp.zeros_like(diag_real) + shift_imag
    modulus = diag_real * diag_real + diag_imag * diag_imag
    inverse_real = diag_real / modulus
    inverse_imag = -diag_imag / modulus
    present_guess = complex_mul(inverse_real, inverse_imag, source_term)
    for sweep_no in range(SWEEPS - 1):
        present_guess = complex_mul(
            inverse_real, inverse_imag, source_term + neighbors(present_guess)
        )
    applied = complex_mul(diag_real, diag_imag, present_guess) - neighbors(present_guess)
    residual = source_term - applied
    first_axis_teams = first_axis_count // AGGREGATE_XCELLS
    second_axis_teams = second_axis_count // AGGREGATE_YCELLS
    per_device = first_axis_teams * second_axis_teams

    def aggregate(values):
        leading = values.shape[:-3]
        blocks = values.reshape(
            leading
            + (
                third_axis_count,
                first_axis_teams,
                AGGREGATE_XCELLS,
                second_axis_teams,
                AGGREGATE_YCELLS,
            )
        )
        return jnp.sum(blocks, axis=(-5, -3, -1)).reshape(leading + (per_device,))

    coarse_right = jnp.transpose(aggregate(residual), (1, 0, 2))
    rate_sums = aggregate(reaction)
    shift_column = 1.0 - jnp.cos(phase_angle)
    face_count = 2 * (AGGREGATE_YCELLS * third_axis_count + AGGREGATE_XCELLS * third_axis_count)
    volume = AGGREGATE_XCELLS * AGGREGATE_YCELLS * third_axis_count
    spatial = lax.axis_size("sx") * sy_size
    slot_count = -(-moment_count // spatial)
    padding_rows = slot_count * spatial - moment_count
    padded_right = jnp.pad(coarse_right, ((0, padding_rows), (0, 0), (0, 0)))
    sum_copies = jnp.broadcast_to(rate_sums[None, None, :], (spatial, 1, per_device))
    shared_right, shared_sums = (
        lax.all_to_all(padded_right, ("sx", "sy"), split_axis=0, concat_axis=2, tiled=True),
        lax.all_to_all(sum_copies, ("sx", "sy"), split_axis=0, concat_axis=2, tiled=True),
    )
    spatial_rank = lax.axis_index("sx") * sy_size + lax.axis_index("sy")
    padded_shift = jnp.pad(shift_column, (0, padding_rows))
    slot_shift = lax.dynamic_slice_in_dim(padded_shift, spatial_rank * slot_count, slot_count, 0)
    sum_values = shared_sums[0, 0]
    coarse_total = sum_values.shape[0]
    position = jnp.arange(coarse_total, dtype=jnp.int32)
    device = position // per_device
    within = position % per_device
    coarse_x = device // sy_size * first_axis_teams + within // second_axis_teams
    coarse_y = device % sy_size * second_axis_teams + within % second_axis_teams
    x_gap = jnp.abs(coarse_x[:, None] - coarse_x[None, :])
    y_gap = jnp.abs(coarse_y[:, None] - coarse_y[None, :])
    coupling = -(AGGREGATE_YCELLS * third_axis_count) * ((x_gap == 1) & (y_gap == 0)).astype(
        jnp.float32
    )
    coupling = coupling - AGGREGATE_XCELLS * third_axis_count * (
        (x_gap == 0) & (y_gap == 1)
    ).astype(jnp.float32)
    identity = (position[:, None] == position[None, :]).astype(jnp.float32)
    diagonal = sum_values + face_count
    system = (
        coupling[None]
        + identity[None] * (diagonal[None, :] + volume * slot_shift[:, None])[:, None, :]
    )
    factor = jnp.linalg.cholesky(system)
    right_side = jnp.transpose(shared_right, (0, 2, 1))
    forward_sub = lax.linalg.triangular_solve(factor, right_side, left_side=True, lower=True)
    coarse = lax.linalg.triangular_solve(
        factor, forward_sub, left_side=True, lower=True, transpose_a=True
    )
    solved = jnp.transpose(coarse, (0, 2, 1))
    returned = lax.all_to_all(solved, ("sx", "sy"), split_axis=2, concat_axis=0, tiled=True)
    own_coarse = returned[:moment_count]
    local_part = jnp.transpose(own_coarse, (1, 0, 2)).reshape(
        2, moment_count, 1, first_axis_teams, 1, second_axis_teams, 1
    )
    spread_values = jnp.broadcast_to(
        local_part,
        (
            2,
            moment_count,
            third_axis_count,
            first_axis_teams,
            AGGREGATE_XCELLS,
            second_axis_teams,
            AGGREGATE_YCELLS,
        ),
    )
    present_guess = present_guess + spread_values.reshape(
        2, moment_count, third_axis_count, first_axis_count, second_axis_count
    )
    unrolled_array = present_guess.reshape(2, moment_count, unknowns_in_tile)

    def backward(running, segment, offset):
        return matmul(cos_rows, segment[0]) - matmul(sin_rows, segment[1])

    result = (
        backward(
            jnp.zeros((moment_count, unknowns_in_tile), jnp.float32),
            lax.all_gather(unrolled_array, "tm", axis=1, tiled=True),
            jnp.int32(0),
        )
        / cycle_duration
    )
    return result.reshape(driving_input.shape)


def time_tables(count):
    half = count // 2
    lane = np.arange(count)
    frequency = np.where(lane <= half, lane, lane - half)
    imaginary = lane > half
    moment = np.arange(count)
    angle = 2.0 * np.pi * (moment[:, None] * frequency[None, :] % count) / count
    forward = np.where(imaginary[None, :], -np.sin(angle), np.cos(angle))
    weight = np.where((lane == 0) | (lane == half), 1.0, 2.0) / count
    theta = 2.0 * np.pi * frequency / count
    signed = np.where(lane % half == 0, 0.0, np.sin(theta)) * np.where(lane < half, 1.0, -1.0)
    shift = np.zeros((8, count))
    shift[0] = 1.0 - np.cos(theta)
    shift[1] = signed
    return np.concatenate([forward, forward * weight[None, :], shift]).astype(np.float32)


def fused_kernel(
    sizes,
    rates_ref,
    field_hbm,
    regime_hbm,
    table_hbm,
    out_hbm,
    added_ref,
    field_ref,
    regime_ref,
    table_ref,
    rate_tiles,
    coarse_tiles,
    all_kinds,
    solved_tiles,
    layer_sums,
    iterate_0,
    iterate_1,
    iterate_2,
    iterate_3,
    lasts,
    x_edges,
    x_halos,
    y_edges,
    y_halos,
    load_sem,
    store_sem,
    last_send,
    last_recv,
    rate_send,
    rate_recv,
    coarse_send,
    coarse_recv,
    kind_send,
    kind_recv,
    halo_send,
    halo_recv,
):
    teams, nsx, nsy, moments, nz, nx, lanes, width = sizes
    total = teams * moments
    strips = lanes // width
    plane = nz * nx
    spatial = nsx * nsy
    highest = lax.Precision.HIGHEST
    tm = lax.axis_index("tm")
    ix = lax.axis_index("sx")
    iy = lax.axis_index("sy")
    here = ix * nsy + iy

    loads = [
        pltpu.make_async_copy(regime_hbm, regime_ref, load_sem.at[0]),
        pltpu.make_async_copy(field_hbm, field_ref, load_sem.at[1]),
        pltpu.make_async_copy(table_hbm, table_ref, load_sem.at[2]),
    ]
    for load in loads:
        load.start()

    team_peers = [
        {"tm": (tm + offset) % teams, "sx": ix, "sy": iy} for offset in range(1, teams)
    ]
    space_peers = []
    for offset in range(1, spatial):
        peer = (here + offset) % spatial
        space_peers.append({"tm": tm, "sx": peer // nsy, "sy": peer % nsy})
    barrier = pltpu.get_barrier_semaphore()
    for peer in team_peers + space_peers:
        pl.semaphore_signal(
            barrier, inc=1, device_id=peer, device_id_type=pl.DeviceIdType.MESH
        )

    def gather(ref, targets, send_sem, recv_sem):
        return [
            pltpu.make_async_remote_copy(
                src_ref=ref,
                dst_ref=ref,
                send_sem=send_sem.at[number],
                recv_sem=recv_sem.at[number],
                device_id=peer,
                device_id_type=pl.DeviceIdType.MESH,
            )
            for number, peer in enumerate(targets)
        ]

    loads[0].wait()
    rates = jnp.zeros(regime_ref.shape, jnp.float32)
    regime = regime_ref[...]
    for number in range(rates_ref.shape[0]):
        rates = rates + jnp.where(regime == number, rates_ref[number], 0.0)
    rate_tiles[here] = jnp.sum(rates, axis=0)
    decay = 1.0 / (rates + 7.0)
    decay_block = jnp.ones_like(decay)
    power, left = decay, moments
    while left:
        if left & 1:
            decay_block = decay_block * power
        power = power * power
        left //= 2
    decay_round = jnp.ones_like(decay)
    for _ in range(teams):
        decay_round = decay_round * decay_block
    closing = 1.0 / (1.0 - decay_round)

    has = (ix > 0, ix < nsx - 1, iy > 0, iy < nsy - 1)
    neighbour = (
        {"tm": tm, "sx": (ix + nsx - 1) % nsx, "sy": iy},
        {"tm": tm, "sx": (ix + 1) % nsx, "sy": iy},
        {"tm": tm, "sx": ix, "sy": (iy + nsy - 1) % nsy},
        {"tm": tm, "sx": ix, "sy": (iy + 1) % nsy},
    )
    for number in range(3):
        for side in range(4):

            @pl.when(jnp.logical_not(has[side]))
            def _(halo=(x_halos if side < 2 else y_halos).at[number, side % 2]):
                halo[...] = jnp.zeros(halo.shape, jnp.float32)

    def halo_copies(number):
        copies = []
        for side in range(4):
            if side < 2:
                source = x_edges.at[number, side]
                target = x_halos.at[number, 1 - side]
            else:
                source = y_edges.at[number]
                target = y_halos.at[number, 3 - side]
            copies.append(
                pltpu.make_async_remote_copy(
                    src_ref=source,
                    dst_ref=target,
                    send_sem=halo_send.at[number * 4 + side],
                    recv_sem=halo_recv.at[number * 4 + (side ^ 1)],
                    device_id=neighbour[side],
                    device_id_type=pl.DeviceIdType.MESH,
                )
            )
        return copies

    def exchange_start(number):
        for side, copy in enumerate(halo_copies(number)):

            @pl.when(has[side])
            def _(copy=copy):
                copy.start()

    def exchange_wait(number):
        copies = halo_copies(number)
        for side in range(4):

            @pl.when(has[side])
            def _(side=side):
                copies[side].wait_send()
                copies[side ^ 1].wait_recv()

    def rate_copy(offset):
        peer = (here + offset) % spatial
        return pltpu.make_async_remote_copy(
            src_ref=rate_tiles.at[here],
            dst_ref=rate_tiles.at[here],
            send_sem=rate_send.at[offset],
            recv_sem=rate_recv.at[offset],
            device_id={"tm": tm, "sx": peer // nsy, "sy": peer % nsy},
            device_id_type=pl.DeviceIdType.MESH,
        )

    def last_copy(number, offset):
        return pltpu.make_async_remote_copy(
            src_ref=lasts.at[number, tm],
            dst_ref=lasts.at[number, tm],
            send_sem=last_send.at[number * teams + offset],
            recv_sem=last_recv.at[number * teams + offset],
            device_id={"tm": (tm + offset) % teams, "sx": ix, "sy": iy},
            device_id_type=pl.DeviceIdType.MESH,
        )

    def cell(moment, z):
        return pl.ds(pl.multiple_of((moment * nz + z) * nx, nx), nx)

    iterates = (iterate_0, iterate_1, iterate_2, iterate_3)
    chunk = lanes // 2 // nz
    row_id = lax.broadcasted_iota(jnp.int32, (nx, lanes), 0)
    lane_id = lax.broadcasted_iota(jnp.int32, (nx, lanes), 1)
    first_row, last_row = row_id == 0, row_id == nx - 1
    first_lane, last_lane = lane_id == 0, lane_id == lanes - 1
    odd_lane = lane_id % 2 == 1
    pair = (lane_id + 1) % lanes // 2

    def recurrence(number):
        def body(block, state):
            if number:
                high = y_halos[number - 1, 1, block]
                low = pltpu.roll(y_halos[number - 1, 0, block], 2, 1)
                ends = jnp.where(odd_lane, low, high)
                old = iterates[number - 1]
            state = list(state)
            for inner in range(chunk):
                moment = block * chunk + inner
                if number:
                    cells = [old[cell(moment, z), :] for z in range(nz)]
                for z in range(nz):
                    values = field_ref[moment, z]
                    if number:
                        here_cell = cells[z]
                        slot = inner * nz + z
                        turned = pltpu.roll(ends, (lanes - 2 * slot - 1) % lanes, 1)
                        low_row = x_halos[number - 1, 0, moment, z : z + 1, :]
                        high_row = x_halos[number - 1, 1, moment, z : z + 1, :]
                        values = values + cells[z - 1] + cells[(z + 1) % nz]
                        values = values + jnp.where(
                            first_row, low_row, pltpu.roll(here_cell, 1, 0)
                        )
                        values = values + jnp.where(
                            last_row, high_row, pltpu.roll(here_cell, nx - 1, 0)
                        )
                        values = values + jnp.where(
                            first_lane, turned, pltpu.roll(here_cell, 1, 1)
                        )
                        values = values + jnp.where(
                            last_lane, turned, pltpu.roll(here_cell, lanes - 1, 1)
                        )
                    state[z] = decay[z] * (values + state[z])
                    iterates[number][cell(moment, z), :] = state[z]
            return tuple(state)

        start = tuple(jnp.zeros((nx, lanes), jnp.float32) for _ in range(nz))
        state = lax.fori_loop(0, moments // chunk, body, start)
        for z in range(nz):
            lasts[number, tm, z] = state[z]

    def history(number):
        value = lasts[number, tm]
        for offset in range(1, teams):
            value = lasts[number, (tm + offset) % teams] + decay_block * value
        return value * closing

    def complete(number, entry):
        def body(block, state):
            state = list(state)
            packed = jnp.zeros((nx, lanes), jnp.float32)
            for inner in range(chunk):
                moment = block * chunk + inner
                for z in range(nz):
                    state[z] = decay[z] * state[z]
                    values = iterates[number][cell(moment, z), :] + state[z]
                    iterates[number][cell(moment, z), :] = values
                    slot = inner * nz + z
                    packed = jnp.where(pair == slot, pltpu.roll(values, 2 * slot, 1), packed)
                for side, edge_row in enumerate((0, nx - 1)):
                    rows = pl.ds(moment * plane + edge_row, nz, stride=nx)
                    x_edges[number, side, moment] = iterates[number][rows, :]
            y_edges[number, block] = packed
            return tuple(state)

        lax.fori_loop(0, moments // chunk, body, tuple(entry[z] for z in range(nz)))

    loads[1].wait()
    recurrence(0)
    pl.semaphore_wait(barrier, len(team_peers) + len(space_peers))
    for offset in range(1, teams):
        last_copy(0, offset).start()
    for offset in range(1, spatial):
        rate_copy(offset).start()
    for offset in range(1, teams):
        last_copy(0, offset).wait()
    complete(0, history(0))
    exchange_start(0)

    for offset in range(1, spatial):
        rate_copy(offset).wait()
    loads[2].wait()
    shift_real = table_ref[2 * total : 2 * total + 1, :]
    ncy = nsy * strips
    strip_block = lax.broadcasted_iota(jnp.int32, (nx, lanes), 1) // width
    faces = 2 * (width * nz + nx * nz)
    couple_x = -float(width * nz)
    couple_y = -float(nx * nz)
    unknowns = ncy * nsx
    band = [[None] * (nsx + 1) for _ in range(unknowns)]
    for gy in range(ncy):
        for gx in range(nsx):
            number = gy * nsx + gx
            tile = rate_tiles[gx * nsy + gy // strips]
            amount = jnp.sum(jnp.where(strip_block == gy % strips, tile, 0.0), axis=0, keepdims=True)
            amount = jnp.sum(amount, axis=1, keepdims=True)
            band[number][0] = amount + faces + float(nx * width * nz) * shift_real
            if gx + 1 < nsx:
                band[number][1] = jnp.full((1, total), couple_x, jnp.float32)
            if gy + 1 < ncy:
                extra = jnp.full((1, total), couple_y, jnp.float32)
                before = band[number][nsx]
                band[number][nsx] = extra if before is None else before + extra
    inverses = []
    ratios = []

    def factor(count):
        for i in range(len(inverses), min(unknowns, len(inverses) + count)):
            inverse = 1.0 / band[i][0]
            inverses.append(inverse)
            ratios.append([None] * (nsx + 1))
            for a in range(1, nsx + 1):
                if band[i][a] is None or i + a >= unknowns:
                    continue
                ratio = band[i][a] * inverse
                ratios[i][a] = ratio
                for b in range(a, nsx + 1):
                    if band[i][b] is None or i + b >= unknowns:
                        continue
                    term = ratio * band[i][b]
                    before = band[i + a][b - a]
                    band[i + a][b - a] = -term if before is None else before - term


    exchange_wait(0)
    share = -(-unknowns // 2)
    for number in range(1, 4):
        recurrence(number)
        for offset in range(1, teams):
            last_copy(number, offset).start()
        for offset in range(1, teams):
            last_copy(number, offset).wait()
        if number < 3:
            complete(number, history(number))
            exchange_start(number)
            factor(share)
            exchange_wait(number)

    entry = history(3)

    def finish(moment, state):
        state = list(state)
        layer = jnp.zeros((nx, lanes), jnp.float32)
        for z in range(nz):
            state[z] = decay[z] * state[z]
            values = iterate_3[cell(moment, z), :] + state[z]
            iterate_3[cell(moment, z), :] = values
            layer = layer + (values - iterate_2[cell(moment, z), :])
        layer_sums[pl.ds(pl.multiple_of(moment * nx, nx), nx), :] = layer
        return tuple(state)

    lax.fori_loop(0, moments, finish, tuple(entry[z] for z in range(nz)), unroll=4)
    store = pltpu.make_async_copy(iterate_3, out_hbm, store_sem)
    store.start()
    by_row = [layer_sums[pl.ds(x, moments, stride=nx), :] for x in range(nx)]
    columns = sum(by_row[1:], by_row[0])
    moment_lane = lax.broadcasted_iota(jnp.int32, (moments, lanes), 1)
    balance = 4.0 * columns - by_row[0] - by_row[nx - 1]
    balance = balance + jnp.where(moment_lane > 0, pltpu.roll(columns, 1, 1), 0.0)
    balance = balance + jnp.where(
        moment_lane < lanes - 1, pltpu.roll(columns, lanes - 1, 1), 0.0
    )
    stacked = jnp.concatenate([balance, by_row[0], by_row[nx - 1], columns], axis=0)
    member = (lane_id // width == row_id).astype(jnp.float32)
    ends = jnp.where(
        row_id == 0, first_lane.astype(jnp.float32), last_lane.astype(jnp.float32)
    )
    ends = jnp.where(row_id < 2, ends, 0.0)

    def against(left_side, right_side):
        return lax.dot_general(
            left_side,
            right_side,
            (((1,), (1,)), ((), ())),
            precision=highest,
            preferred_element_type=jnp.float32,
        )

    coarse_tiles[tm] = jnp.where(
        lane_id < 3 * moments, against(member, stacked), against(ends, stacked)
    )
    copies = gather(coarse_tiles.at[tm], team_peers, coarse_send, coarse_recv)
    for copy in copies:
        copy.start()
    for copy in copies:
        copy.wait()
    quarter = lane_id // moments
    for kind in range(4):
        merged = None
        for team in range(teams):
            tile = coarse_tiles[team]
            turn = (moments * (team - kind)) % lanes
            turned = pltpu.roll(tile, turn, 1) if turn else tile
            merged = turned if team == 0 else jnp.where(quarter == team, turned, merged)
        all_kinds[here, kind] = merged
    copies = gather(all_kinds.at[here], space_peers, kind_send, kind_recv)
    for copy in copies:
        copy.start()
    for copy in copies:
        copy.wait()
    kinds = [[all_kinds[slot, kind] for slot in range(spatial)] for kind in range(4)]
    tiles = []
    for gx in range(nsx):
        for gy in range(nsy):
            slot = gx * nsy + gy
            tile = kinds[0][slot]
            if gx + 1 < nsx:
                tile = tile + kinds[1][slot + nsy]
            if gx > 0:
                tile = tile + kinds[2][slot - nsy]
            if gy > 0:
                tile = tile + jnp.where(row_id == 0, kinds[3][slot - 1][1:2], 0.0)
            if gy + 1 < nsy:
                tile = tile + jnp.where(row_id == strips - 1, kinds[3][slot + 1][0:1], 0.0)
            tiles.append(tile)
    spectrum = jnp.dot(
        jnp.concatenate(tiles, axis=0),
        table_ref[0:total, :],
        precision=highest,
        preferred_element_type=jnp.float32,
    )
    right = []
    for gy in range(ncy):
        for gx in range(nsx):
            row = (gx * nsy + gy // strips) * nx + gy % strips
            right.append(spectrum[row : row + 1])
    for i in range(unknowns):
        for a in range(1, nsx + 1):
            if ratios[i][a] is not None:
                right[i + a] = right[i + a] - ratios[i][a] * right[i]
    for i in reversed(range(unknowns)):
        value = right[i] * inverses[i]
        for a in range(1, nsx + 1):
            if ratios[i][a] is not None:
                value = value - ratios[i][a] * right[i + a]
        right[i] = value
    for gx in range(nsx):
        for block in range(nsy):
            for d in range(strips):
                number = (block * strips + d) * nsx + gx
                solved_tiles[gx * nsy + block, d : d + 1, :] = right[number]
    own_rows = solved_tiles[here]
    spread = jnp.concatenate(
        [jnp.broadcast_to(own_rows[d : d + 1], (width, total)) for d in range(strips)], axis=0
    )
    own_moments = pl.ds(pl.multiple_of(total + tm * moments, moments), moments)
    added_ref[...] = against(table_ref[own_moments, :], spread)

    store.wait()


def local_fused(teams, nsx, nsy, driving_input, regime, reaction_rates):
    moments, nz, nx, lanes = driving_input.shape
    width = AGGREGATE_YCELLS
    total = teams * moments
    table = time_tables(total)
    sizes = (teams, nsx, nsy, moments, nz, nx, lanes, width)
    blocks = 2 * moments * nz // lanes
    f32 = jnp.float32
    whole = pltpu.VMEM(driving_input.shape, f32)
    flat = pltpu.VMEM((moments * nz * nx, lanes), f32)
    in_hbm = pl.BlockSpec(memory_space=pltpu.HBM)
    dma = pltpu.SemaphoreType.DMA
    field, added = pl.pallas_call(
        functools.partial(fused_kernel, sizes),
        out_shape=(
            pltpu.VMEM((moments * nz * nx, lanes), f32),
            pltpu.VMEM((moments, lanes), f32),
        ),
        in_specs=[pl.BlockSpec(memory_space=pltpu.SMEM)] + [in_hbm] * 3,
        out_specs=(pl.BlockSpec(memory_space=pl.ANY), pl.BlockSpec(memory_space=pltpu.VMEM)),
        scratch_shapes=[
            whole,
            pltpu.VMEM(regime.shape, jnp.int32),
            pltpu.VMEM(table.shape, f32),
            pltpu.VMEM((nsx * nsy, nx, lanes), f32),
            pltpu.VMEM((teams, 8, total), f32),
            pltpu.VMEM((nsx * nsy, 4, 8, total), f32),
            pltpu.VMEM((nsx * nsy, max(lanes // width, 8), total), f32),
            pltpu.VMEM((moments * nx, lanes), f32),
            flat,
            flat,
            flat,
            flat,
            pltpu.VMEM((4, teams, nz, nx, lanes), f32),
            pltpu.VMEM((3, 2, moments, nz, lanes), f32),
            pltpu.VMEM((3, 2, moments, nz, lanes), f32),
            pltpu.VMEM((3, blocks, nx, lanes), f32),
            pltpu.VMEM((3, 2, blocks, nx, lanes), f32),
            dma((3,)),
            dma,
            dma((4 * teams,)),
            dma((4 * teams,)),
            dma((nsx * nsy,)),
            dma((nsx * nsy,)),
            dma((teams,)),
            dma((teams,)),
            dma((nsx * nsy,)),
            dma((nsx * nsy,)),
            dma((12,)),
            dma((12,)),
        ],
        compiler_params=pltpu.CompilerParams(
            collective_id=0, has_side_effects=True, vmem_limit_bytes=62 * 1024 * 1024
        ),
    )(reaction_rates, driving_input, regime, jnp.asarray(table))
    return field.reshape(driving_input.shape) + added[:, None, None, :]


def local(driving_input, regime, reaction_rates):
    moments, nz, nx, lanes = driving_input.shape
    teams, nsx, nsy = (lax.axis_size(axis) for axis in ("tm", "sx", "sy"))
    strips = lanes // AGGREGATE_YCELLS
    whole_strips = nx == AGGREGATE_XCELLS and strips * AGGREGATE_YCELLS == lanes and strips <= 8
    tiled = nx == 8 and nz == 8 and lanes == 128 and moments % 8 == 0
    if whole_strips and tiled and teams * moments == 128 and 4 * moments == 128 and SWEEPS == 4:
        return local_fused(teams, nsx, nsy, driving_input, regime, reaction_rates)
    return local_general(driving_input, regime, reaction_rates)


def solution(mesh):
    placed = (P("tm", None, "sx", "sy"), P(None, "sx", "sy"), P())
    return jax.shard_map(
        local, mesh=mesh, in_specs=placed, out_specs=P("tm", None, "sx", "sy"), check_vma=False
    )
```

```python
import functools

import jax
import jax.numpy as jnp
import numpy as np
from jax import lax
from jax.experimental import pallas as pl
from jax.experimental.pallas import tpu as pltpu
from jax.sharding import PartitionSpec as P

AGGREGATE_XCELLS = 8
AGGREGATE_YCELLS = 32
SWEEPS = 4


TWO_PI = 2.0 * 3.141592653589793


def extended(block, sides, width):
    for axis, dim in sides:
        count = lax.axis_size(axis)
        forward = [(i, i + 1) for i in range(count - 1)]
        backward = [(target, source) for source, target in forward]
        low = lax.ppermute(
            lax.slice_in_dim(block, block.shape[dim] - width, None, axis=dim), axis, forward
        )
        high = lax.ppermute(lax.slice_in_dim(block, 0, width, axis=dim), axis, backward)
        block = jnp.concatenate([low, block, high], axis=dim)
    return block


def angle_table(row_index, col_index, cycle_duration):
    product = row_index[:, None] * col_index[None, :] % cycle_duration
    angles = product.astype(jnp.float32) * (TWO_PI / cycle_duration)
    return (jnp.cos(angles), jnp.sin(angles))


def matmul(left_side, right_side):
    return jnp.dot(
        left_side, right_side, precision=lax.Precision.HIGHEST, preferred_element_type=jnp.float32
    )


def complex_mul(left_real, left_imag, pair):
    return jnp.stack(
        [left_real * pair[0] - left_imag * pair[1], left_real * pair[1] + left_imag * pair[0]]
    )


def neighbors(present_guess):
    padded = extended(present_guess, (("sx", 3), ("sy", 4)), 1)
    running = padded[:, :, :, 2:, 1:-1] + padded[:, :, :, :-2, 1:-1]
    running = running + padded[:, :, :, 1:-1, 2:] + padded[:, :, :, 1:-1, :-2]
    running = running + jnp.roll(present_guess, 1, axis=2) + jnp.roll(present_guess, -1, axis=2)
    return running


def local_general(driving_input, regime, reaction_rates):
    moment_count, third_axis_count, first_axis_count, second_axis_count = driving_input.shape
    temporal_spacing = lax.axis_size("tm")
    sy_size = lax.axis_size("sy")
    cycle_duration = moment_count * temporal_spacing
    unknowns_in_tile = third_axis_count * first_axis_count * second_axis_count
    processor_lines = driving_input.reshape(moment_count, unknowns_in_tile)
    owned_slice_number = lax.axis_index("tm") * moment_count + jnp.arange(
        moment_count, dtype=jnp.int32
    )
    all_index = jnp.arange(cycle_duration, dtype=jnp.int32)
    cos_rows, sin_rows = angle_table(owned_slice_number, all_index, cycle_duration)

    def forward(running, segment, offset):
        return jnp.stack([matmul(cos_rows, segment), -matmul(sin_rows, segment)])

    eigen_spectra = forward(
        jnp.zeros((2, moment_count, unknowns_in_tile), jnp.float32),
        lax.all_gather(processor_lines, "tm", axis=0, tiled=True),
        jnp.int32(0),
    )
    source_term = eigen_spectra.reshape(
        2, moment_count, third_axis_count, first_axis_count, second_axis_count
    )
    phase_angle = owned_slice_number.astype(jnp.float32) * (TWO_PI / cycle_duration)
    shift_real = (1.0 - jnp.cos(phase_angle))[:, None, None, None]
    shift_imag = jnp.sin(phase_angle)[:, None, None, None]
    reaction = jnp.zeros(regime.shape, jnp.float32)
    for regime_no in range(reaction_rates.shape[0]):
        reaction = reaction + jnp.where(
            regime == regime_no, reaction_rates[regime_no], jnp.zeros((), jnp.float32)
        )
    diag_real = reaction[None] + 6.0 + shift_real
    diag_imag = jnp.zeros_like(diag_real) + shift_imag
    modulus = diag_real * diag_real + diag_imag * diag_imag
    inverse_real = diag_real / modulus
    inverse_imag = -diag_imag / modulus
    present_guess = complex_mul(inverse_real, inverse_imag, source_term)
    for sweep_no in range(SWEEPS - 1):
        present_guess = complex_mul(
            inverse_real, inverse_imag, source_term + neighbors(present_guess)
        )
    applied = complex_mul(diag_real, diag_imag, present_guess) - neighbors(present_guess)
    residual = source_term - applied
    first_axis_teams = first_axis_count // AGGREGATE_XCELLS
    second_axis_teams = second_axis_count // AGGREGATE_YCELLS
    per_device = first_axis_teams * second_axis_teams

    def aggregate(values):
        leading = values.shape[:-3]
        blocks = values.reshape(
            leading
            + (
                third_axis_count,
                first_axis_teams,
                AGGREGATE_XCELLS,
                second_axis_teams,
                AGGREGATE_YCELLS,
            )
        )
        return jnp.sum(blocks, axis=(-5, -3, -1)).reshape(leading + (per_device,))

    coarse_right = jnp.transpose(aggregate(residual), (1, 0, 2))
    rate_sums = aggregate(reaction)
    shift_column = 1.0 - jnp.cos(phase_angle)
    face_count = 2 * (AGGREGATE_YCELLS * third_axis_count + AGGREGATE_XCELLS * third_axis_count)
    volume = AGGREGATE_XCELLS * AGGREGATE_YCELLS * third_axis_count
    spatial = lax.axis_size("sx") * sy_size
    slot_count = -(-moment_count // spatial)
    padding_rows = slot_count * spatial - moment_count
    padded_right = jnp.pad(coarse_right, ((0, padding_rows), (0, 0), (0, 0)))
    sum_copies = jnp.broadcast_to(rate_sums[None, None, :], (spatial, 1, per_device))
    shared_right, shared_sums = (
        lax.all_to_all(padded_right, ("sx", "sy"), split_axis=0, concat_axis=2, tiled=True),
        lax.all_to_all(sum_copies, ("sx", "sy"), split_axis=0, concat_axis=2, tiled=True),
    )
    spatial_rank = lax.axis_index("sx") * sy_size + lax.axis_index("sy")
    padded_shift = jnp.pad(shift_column, (0, padding_rows))
    slot_shift = lax.dynamic_slice_in_dim(padded_shift, spatial_rank * slot_count, slot_count, 0)
    sum_values = shared_sums[0, 0]
    coarse_total = sum_values.shape[0]
    position = jnp.arange(coarse_total, dtype=jnp.int32)
    device = position // per_device
    within = position % per_device
    coarse_x = device // sy_size * first_axis_teams + within // second_axis_teams
    coarse_y = device % sy_size * second_axis_teams + within % second_axis_teams
    x_gap = jnp.abs(coarse_x[:, None] - coarse_x[None, :])
    y_gap = jnp.abs(coarse_y[:, None] - coarse_y[None, :])
    coupling = -(AGGREGATE_YCELLS * third_axis_count) * ((x_gap == 1) & (y_gap == 0)).astype(
        jnp.float32
    )
    coupling = coupling - AGGREGATE_XCELLS * third_axis_count * (
        (x_gap == 0) & (y_gap == 1)
    ).astype(jnp.float32)
    identity = (position[:, None] == position[None, :]).astype(jnp.float32)
    diagonal = sum_values + face_count
    system = (
        coupling[None]
        + identity[None] * (diagonal[None, :] + volume * slot_shift[:, None])[:, None, :]
    )
    factor = jnp.linalg.cholesky(system)
    right_side = jnp.transpose(shared_right, (0, 2, 1))
    forward_sub = lax.linalg.triangular_solve(factor, right_side, left_side=True, lower=True)
    coarse = lax.linalg.triangular_solve(
        factor, forward_sub, left_side=True, lower=True, transpose_a=True
    )
    solved = jnp.transpose(coarse, (0, 2, 1))
    returned = lax.all_to_all(solved, ("sx", "sy"), split_axis=2, concat_axis=0, tiled=True)
    own_coarse = returned[:moment_count]
    local_part = jnp.transpose(own_coarse, (1, 0, 2)).reshape(
        2, moment_count, 1, first_axis_teams, 1, second_axis_teams, 1
    )
    spread_values = jnp.broadcast_to(
        local_part,
        (
            2,
            moment_count,
            third_axis_count,
            first_axis_teams,
            AGGREGATE_XCELLS,
            second_axis_teams,
            AGGREGATE_YCELLS,
        ),
    )
    present_guess = present_guess + spread_values.reshape(
        2, moment_count, third_axis_count, first_axis_count, second_axis_count
    )
    unrolled_array = present_guess.reshape(2, moment_count, unknowns_in_tile)

    def backward(running, segment, offset):
        return matmul(cos_rows, segment[0]) - matmul(sin_rows, segment[1])

    result = (
        backward(
            jnp.zeros((moment_count, unknowns_in_tile), jnp.float32),
            lax.all_gather(unrolled_array, "tm", axis=1, tiled=True),
            jnp.int32(0),
        )
        / cycle_duration
    )
    return result.reshape(driving_input.shape)


def time_tables(count):
    half = count // 2
    lane = np.arange(count)
    frequency = np.where(lane <= half, lane, lane - half)
    imaginary = lane > half
    moment = np.arange(count)
    angle = 2.0 * np.pi * (moment[:, None] * frequency[None, :] % count) / count
    forward = np.where(imaginary[None, :], -np.sin(angle), np.cos(angle))
    weight = np.where((lane == 0) | (lane == half), 1.0, 2.0) / count
    theta = 2.0 * np.pi * frequency / count
    signed = np.where(lane % half == 0, 0.0, np.sin(theta)) * np.where(lane < half, 1.0, -1.0)
    shift = np.zeros((8, count))
    shift[0] = 1.0 - np.cos(theta)
    shift[1] = signed
    return np.concatenate([forward, forward * weight[None, :], shift]).astype(np.float32)


def fused_kernel(
    sizes,
    rates_ref,
    field_hbm,
    regime_hbm,
    table_hbm,
    out_hbm,
    added_ref,
    field_ref,
    regime_ref,
    table_ref,
    rate_tiles,
    coarse_tiles,
    solved_tiles,
    layer_sums,
    iterate_0,
    iterate_1,
    iterate_2,
    iterate_3,
    lasts,
    x_edges,
    x_halos,
    y_edges,
    y_halos,
    load_sem,
    store_sem,
    last_send,
    last_recv,
    rate_send,
    rate_recv,
    coarse_send,
    coarse_recv,
    halo_send,
    halo_recv,
):
    teams, nsx, nsy, moments, nz, nx, lanes, width = sizes
    total = teams * moments
    strips = lanes // width
    plane = nz * nx
    spatial = nsx * nsy
    devices = teams * spatial
    highest = lax.Precision.HIGHEST
    tm = lax.axis_index("tm")
    ix = lax.axis_index("sx")
    iy = lax.axis_index("sy")
    here = ix * nsy + iy
    me = tm * spatial + here

    loads = [
        pltpu.make_async_copy(regime_hbm, regime_ref, load_sem.at[0]),
        pltpu.make_async_copy(field_hbm, field_ref, load_sem.at[1]),
        pltpu.make_async_copy(table_hbm, table_ref, load_sem.at[2]),
    ]
    for load in loads:
        load.start()

    def place(rank):
        return {
            "tm": rank // spatial,
            "sx": (rank % spatial) // nsy,
            "sy": rank % nsy,
        }

    barrier = pltpu.get_barrier_semaphore()

    def greet(offset, carry):
        pl.semaphore_signal(
            barrier,
            inc=1,
            device_id=place((me + offset) % devices),
            device_id_type=pl.DeviceIdType.MESH,
        )
        return carry

    lax.fori_loop(1, devices, greet, 0)

    loads[0].wait()
    rates = jnp.zeros(regime_ref.shape, jnp.float32)
    regime = regime_ref[...]
    for number in range(rates_ref.shape[0]):
        rates = rates + jnp.where(regime == number, rates_ref[number], 0.0)
    rate_tiles[here] = jnp.sum(rates, axis=0)
    decay = 1.0 / (rates + 7.0)
    decay_block = jnp.ones_like(decay)
    power, left = decay, moments
    while left:
        if left & 1:
            decay_block = decay_block * power
        power = power * power
        left //= 2
    decay_round = jnp.ones_like(decay)
    for _ in range(teams):
        decay_round = decay_round * decay_block
    closing = 1.0 / (1.0 - decay_round)

    has = (ix > 0, ix < nsx - 1, iy > 0, iy < nsy - 1)
    neighbour = (
        {"tm": tm, "sx": (ix + nsx - 1) % nsx, "sy": iy},
        {"tm": tm, "sx": (ix + 1) % nsx, "sy": iy},
        {"tm": tm, "sx": ix, "sy": (iy + nsy - 1) % nsy},
        {"tm": tm, "sx": ix, "sy": (iy + 1) % nsy},
    )
    for number in range(3):
        for side in range(4):

            @pl.when(jnp.logical_not(has[side]))
            def _(halo=(x_halos if side < 2 else y_halos).at[number, side % 2]):
                halo[...] = jnp.zeros(halo.shape, jnp.float32)

    def halo_copies(number):
        copies = []
        for side in range(4):
            if side < 2:
                source = x_edges.at[number, side]
                target = x_halos.at[number, 1 - side]
            else:
                source = y_edges.at[number]
                target = y_halos.at[number, 3 - side]
            copies.append(
                pltpu.make_async_remote_copy(
                    src_ref=source,
                    dst_ref=target,
                    send_sem=halo_send.at[number * 4 + side],
                    recv_sem=halo_recv.at[number * 4 + (side ^ 1)],
                    device_id=neighbour[side],
                    device_id_type=pl.DeviceIdType.MESH,
                )
            )
        return copies

    def exchange_start(number):
        for side, copy in enumerate(halo_copies(number)):

            @pl.when(has[side])
            def _(copy=copy):
                copy.start()

    def exchange_wait(number):
        copies = halo_copies(number)
        for side in range(4):

            @pl.when(has[side])
            def _(side=side):
                copies[side].wait_send()
                copies[side ^ 1].wait_recv()

    def rate_copy(offset):
        peer = (here + offset) % spatial
        return pltpu.make_async_remote_copy(
            src_ref=rate_tiles.at[here],
            dst_ref=rate_tiles.at[here],
            send_sem=rate_send.at[offset],
            recv_sem=rate_recv.at[offset],
            device_id={"tm": tm, "sx": peer // nsy, "sy": peer % nsy},
            device_id_type=pl.DeviceIdType.MESH,
        )

    def last_copy(number, offset):
        return pltpu.make_async_remote_copy(
            src_ref=lasts.at[number, tm],
            dst_ref=lasts.at[number, tm],
            send_sem=last_send.at[number * teams + offset],
            recv_sem=last_recv.at[number * teams + offset],
            device_id={"tm": (tm + offset) % teams, "sx": ix, "sy": iy},
            device_id_type=pl.DeviceIdType.MESH,
        )

    def cell(moment, z):
        return pl.ds(pl.multiple_of((moment * nz + z) * nx, nx), nx)

    iterates = (iterate_0, iterate_1, iterate_2, iterate_3)
    chunk = lanes // 2 // nz
    row_id = lax.broadcasted_iota(jnp.int32, (nx, lanes), 0)
    lane_id = lax.broadcasted_iota(jnp.int32, (nx, lanes), 1)
    first_row, last_row = row_id == 0, row_id == nx - 1
    first_lane, last_lane = lane_id == 0, lane_id == lanes - 1
    odd_lane = lane_id % 2 == 1
    pair = (lane_id + 1) % lanes // 2

    def recurrence(number):
        def body(block, state):
            if number:
                high = y_halos[number - 1, 1, block]
                low = pltpu.roll(y_halos[number - 1, 0, block], 2, 1)
                ends = jnp.where(odd_lane, low, high)
                old = iterates[number - 1]
            state = list(state)
            for inner in range(chunk):
                moment = block * chunk + inner
                if number:
                    cells = [old[cell(moment, z), :] for z in range(nz)]
                for z in range(nz):
                    values = field_ref[moment, z]
                    if number:
                        here_cell = cells[z]
                        slot = inner * nz + z
                        turned = pltpu.roll(ends, (lanes - 2 * slot - 1) % lanes, 1)
                        low_row = x_halos[number - 1, 0, moment, z : z + 1, :]
                        high_row = x_halos[number - 1, 1, moment, z : z + 1, :]
                        values = values + cells[z - 1] + cells[(z + 1) % nz]
                        values = values + jnp.where(
                            first_row, low_row, pltpu.roll(here_cell, 1, 0)
                        )
                        values = values + jnp.where(
                            last_row, high_row, pltpu.roll(here_cell, nx - 1, 0)
                        )
                        values = values + jnp.where(
                            first_lane, turned, pltpu.roll(here_cell, 1, 1)
                        )
                        values = values + jnp.where(
                            last_lane, turned, pltpu.roll(here_cell, lanes - 1, 1)
                        )
                    state[z] = decay[z] * (values + state[z])
                    iterates[number][cell(moment, z), :] = state[z]
            return tuple(state)

        start = tuple(jnp.zeros((nx, lanes), jnp.float32) for _ in range(nz))
        state = lax.fori_loop(0, moments // chunk, body, start)
        for z in range(nz):
            lasts[number, tm, z] = state[z]

    def history(number):
        value = lasts[number, tm]
        for offset in range(1, teams):
            value = lasts[number, (tm + offset) % teams] + decay_block * value
        return value * closing

    def complete(number, entry):
        def body(block, state):
            state = list(state)
            packed = jnp.zeros((nx, lanes), jnp.float32)
            for inner in range(chunk):
                moment = block * chunk + inner
                for z in range(nz):
                    state[z] = decay[z] * state[z]
                    values = iterates[number][cell(moment, z), :] + state[z]
                    iterates[number][cell(moment, z), :] = values
                    slot = inner * nz + z
                    packed = jnp.where(pair == slot, pltpu.roll(values, 2 * slot, 1), packed)
                for side, edge_row in enumerate((0, nx - 1)):
                    rows = pl.ds(moment * plane + edge_row, nz, stride=nx)
                    x_edges[number, side, moment] = iterates[number][rows, :]
            y_edges[number, block] = packed
            return tuple(state)

        lax.fori_loop(0, moments // chunk, body, tuple(entry[z] for z in range(nz)))

    loads[1].wait()
    recurrence(0)
    pl.semaphore_wait(barrier, devices - 1)
    for offset in range(1, teams):
        last_copy(0, offset).start()
    for offset in range(1, spatial):
        rate_copy(offset).start()
    for offset in range(1, teams):
        last_copy(0, offset).wait()
    complete(0, history(0))
    exchange_start(0)

    for offset in range(1, spatial):
        rate_copy(offset).wait()
    loads[2].wait()
    shift_real = table_ref[2 * total : 2 * total + 1, :]
    ncy = nsy * strips
    strip_block = lax.broadcasted_iota(jnp.int32, (nx, lanes), 1) // width
    faces = 2 * (width * nz + nx * nz)
    couple_x = -float(width * nz)
    couple_y = -float(nx * nz)
    unknowns = ncy * nsx
    band = [[None] * (nsx + 1) for _ in range(unknowns)]
    for gy in range(ncy):
        for gx in range(nsx):
            number = gy * nsx + gx
            tile = rate_tiles[gx * nsy + gy // strips]
            amount = jnp.sum(jnp.where(strip_block == gy % strips, tile, 0.0), axis=0, keepdims=True)
            amount = jnp.sum(amount, axis=1, keepdims=True)
            band[number][0] = amount + faces + float(nx * width * nz) * shift_real
            if gx + 1 < nsx:
                band[number][1] = jnp.full((1, total), couple_x, jnp.float32)
            if gy + 1 < ncy:
                extra = jnp.full((1, total), couple_y, jnp.float32)
                before = band[number][nsx]
                band[number][nsx] = extra if before is None else before + extra
    inverses = []
    ratios = []
    for i in range(unknowns):
        inverse = 1.0 / band[i][0]
        inverses.append(inverse)
        ratios.append([None] * (nsx + 1))
        for a in range(1, nsx + 1):
            if band[i][a] is None or i + a >= unknowns:
                continue
            ratio = band[i][a] * inverse
            ratios[i][a] = ratio
            for b in range(a, nsx + 1):
                if band[i][b] is None or i + b >= unknowns:
                    continue
                term = ratio * band[i][b]
                before = band[i + a][b - a]
                band[i + a][b - a] = -term if before is None else before - term


    exchange_wait(0)
    for number in range(1, 4):
        recurrence(number)
        for offset in range(1, teams):
            last_copy(number, offset).start()
        for offset in range(1, teams):
            last_copy(number, offset).wait()
        if number < 3:
            complete(number, history(number))
            exchange_start(number)
            exchange_wait(number)

    entry = history(3)

    def finish(moment, state):
        state = list(state)
        layer = jnp.zeros((nx, lanes), jnp.float32)
        for z in range(nz):
            state[z] = decay[z] * state[z]
            values = iterate_3[cell(moment, z), :] + state[z]
            iterate_3[cell(moment, z), :] = values
            layer = layer + (values - iterate_2[cell(moment, z), :])
        layer_sums[pl.ds(pl.multiple_of(moment * nx, nx), nx), :] = layer
        return tuple(state)

    lax.fori_loop(0, moments, finish, tuple(entry[z] for z in range(nz)), unroll=8)
    store = pltpu.make_async_copy(iterate_3, out_hbm, store_sem)
    store.start()
    by_row = [layer_sums[pl.ds(x, moments, stride=nx), :] for x in range(nx)]
    columns = sum(by_row[1:], by_row[0])
    moment_lane = lax.broadcasted_iota(jnp.int32, (moments, lanes), 1)
    balance = 4.0 * columns - by_row[0] - by_row[nx - 1]
    balance = balance + jnp.where(moment_lane > 0, pltpu.roll(columns, 1, 1), 0.0)
    balance = balance + jnp.where(
        moment_lane < lanes - 1, pltpu.roll(columns, lanes - 1, 1), 0.0
    )
    stacked = jnp.concatenate([balance, by_row[0], by_row[nx - 1], columns], axis=0)
    member = (lane_id // width == row_id).astype(jnp.float32)
    ends = jnp.where(
        row_id == 0, first_lane.astype(jnp.float32), last_lane.astype(jnp.float32)
    )
    ends = jnp.where(row_id < 2, ends, 0.0)

    def against(left_side, right_side):
        return lax.dot_general(
            left_side,
            right_side,
            (((1,), (1,)), ((), ())),
            precision=highest,
            preferred_element_type=jnp.float32,
        )

    coarse_tiles[me] = jnp.where(
        lane_id < 3 * moments, against(member, stacked), against(ends, stacked)
    )

    def coarse_copy(offset):
        return pltpu.make_async_remote_copy(
            src_ref=coarse_tiles.at[me],
            dst_ref=coarse_tiles.at[me],
            send_sem=coarse_send.at[offset],
            recv_sem=coarse_recv.at[offset],
            device_id=place((me + offset) % devices),
            device_id_type=pl.DeviceIdType.MESH,
        )

    def coarse_start(offset, carry):
        coarse_copy(offset).start()
        return carry

    def coarse_wait(offset, carry):
        coarse_copy(offset).wait()
        return carry

    lax.fori_loop(1, devices, coarse_start, 0)
    lax.fori_loop(1, devices, coarse_wait, 0)

    kinds = [[None] * spatial for _ in range(4)]
    quarter = lane_id // moments
    for slot in range(spatial):
        for kind in range(4):
            merged = None
            for team in range(teams):
                tile = coarse_tiles[team * spatial + slot]
                turn = (moments * (team - kind)) % lanes
                turned = pltpu.roll(tile, turn, 1) if turn else tile
                merged = turned if team == 0 else jnp.where(quarter == team, turned, merged)
            kinds[kind][slot] = merged
    tiles = []
    for gx in range(nsx):
        for gy in range(nsy):
            slot = gx * nsy + gy
            tile = kinds[0][slot]
            if gx + 1 < nsx:
                tile = tile + kinds[1][slot + nsy]
            if gx > 0:
                tile = tile + kinds[2][slot - nsy]
            if gy > 0:
                tile = tile + jnp.where(row_id == 0, kinds[3][slot - 1][1:2], 0.0)
            if gy + 1 < nsy:
                tile = tile + jnp.where(row_id == strips - 1, kinds[3][slot + 1][0:1], 0.0)
            tiles.append(tile)
    spectrum = jnp.dot(
        jnp.concatenate(tiles, axis=0),
        table_ref[0:total, :],
        precision=highest,
        preferred_element_type=jnp.float32,
    )
    right = []
    for gy in range(ncy):
        for gx in range(nsx):
            row = (gx * nsy + gy // strips) * nx + gy % strips
            right.append(spectrum[row : row + 1])
    for i in range(unknowns):
        for a in range(1, nsx + 1):
            if ratios[i][a] is not None:
                right[i + a] = right[i + a] - ratios[i][a] * right[i]
    for i in reversed(range(unknowns)):
        value = right[i] * inverses[i]
        for a in range(1, nsx + 1):
            if ratios[i][a] is not None:
                value = value - ratios[i][a] * right[i + a]
        right[i] = value
    for gx in range(nsx):
        for block in range(nsy):
            for d in range(strips):
                number = (block * strips + d) * nsx + gx
                solved_tiles[gx * nsy + block, d : d + 1, :] = right[number]
    own_rows = solved_tiles[here]
    spread = jnp.concatenate(
        [jnp.broadcast_to(own_rows[d : d + 1], (width, total)) for d in range(strips)], axis=0
    )
    own_moments = pl.ds(pl.multiple_of(total + tm * moments, moments), moments)
    added_ref[...] = against(table_ref[own_moments, :], spread)

    store.wait()


def local_fused(teams, nsx, nsy, driving_input, regime, reaction_rates):
    moments, nz, nx, lanes = driving_input.shape
    width = AGGREGATE_YCELLS
    total = teams * moments
    table = time_tables(total)
    sizes = (teams, nsx, nsy, moments, nz, nx, lanes, width)
    devices = teams * nsx * nsy
    blocks = 2 * moments * nz // lanes
    f32 = jnp.float32
    whole = pltpu.VMEM(driving_input.shape, f32)
    flat = pltpu.VMEM((moments * nz * nx, lanes), f32)
    in_hbm = pl.BlockSpec(memory_space=pltpu.HBM)
    dma = pltpu.SemaphoreType.DMA
    field, added = pl.pallas_call(
        functools.partial(fused_kernel, sizes),
        out_shape=(
            pltpu.VMEM((moments * nz * nx, lanes), f32),
            pltpu.VMEM((moments, lanes), f32),
        ),
        in_specs=[pl.BlockSpec(memory_space=pltpu.SMEM)] + [in_hbm] * 3,
        out_specs=(pl.BlockSpec(memory_space=pl.ANY), pl.BlockSpec(memory_space=pltpu.VMEM)),
        scratch_shapes=[
            whole,
            pltpu.VMEM(regime.shape, jnp.int32),
            pltpu.VMEM(table.shape, f32),
            pltpu.VMEM((nsx * nsy, nx, lanes), f32),
            pltpu.VMEM((devices, 8, total), f32),
            pltpu.VMEM((nsx * nsy, max(lanes // width, 8), total), f32),
            pltpu.VMEM((moments * nx, lanes), f32),
            flat,
            flat,
            flat,
            flat,
            pltpu.VMEM((4, teams, nz, nx, lanes), f32),
            pltpu.VMEM((3, 2, moments, nz, lanes), f32),
            pltpu.VMEM((3, 2, moments, nz, lanes), f32),
            pltpu.VMEM((3, blocks, nx, lanes), f32),
            pltpu.VMEM((3, 2, blocks, nx, lanes), f32),
            dma((3,)),
            dma,
            dma((4 * teams,)),
            dma((4 * teams,)),
            dma((nsx * nsy,)),
            dma((nsx * nsy,)),
            dma((devices,)),
            dma((devices,)),
            dma((12,)),
            dma((12,)),
        ],
        compiler_params=pltpu.CompilerParams(
            collective_id=0, has_side_effects=True, vmem_limit_bytes=62 * 1024 * 1024
        ),
    )(reaction_rates, driving_input, regime, jnp.asarray(table))
    return field.reshape(driving_input.shape) + added[:, None, None, :]


def local(driving_input, regime, reaction_rates):
    moments, nz, nx, lanes = driving_input.shape
    teams, nsx, nsy = (lax.axis_size(axis) for axis in ("tm", "sx", "sy"))
    strips = lanes // AGGREGATE_YCELLS
    whole_strips = nx == AGGREGATE_XCELLS and strips * AGGREGATE_YCELLS == lanes and strips <= 8
    tiled = nx == 8 and nz == 8 and lanes == 128 and moments % 8 == 0
    if whole_strips and tiled and teams * moments == 128 and 4 * moments == 128 and SWEEPS == 4:
        return local_fused(teams, nsx, nsy, driving_input, regime, reaction_rates)
    return local_general(driving_input, regime, reaction_rates)


def solution(mesh):
    placed = (P("tm", None, "sx", "sy"), P(None, "sx", "sy"), P())
    return jax.shard_map(
        local, mesh=mesh, in_specs=placed, out_specs=P("tm", None, "sx", "sy"), check_vma=False
    )
```
